32 devices in a mesh: dp: 4 (over y, x), fsdp: 8 (over z, core).
Axes of the slice: x: 2, y: 2, z: 4, core: 2. Of those that a mesh axis runs over, the one named last changes fastest.
Arguments:
- inputs: bfloat16 [2, 64, 512, 512], P(None, ('dp', 'fsdp')), may hold values from -6 to 6
- lengths: int32 [2, 64], P(None, ('dp', 'fsdp')), may hold values from 64 to 512, as said below
- grad_out: bfloat16 [2, 64, 512, 512], P(None, ('dp', 'fsdp')), may hold values from -6 to 6
- query_weight: bfloat16 [512, 512], P(('dp', 'fsdp')), may hold values from -0.25 to 0.25
- key_weight: bfloat16 [512, 512], P(('dp', 'fsdp')), may hold values from -0.25 to 0.25
- value_weight: bfloat16 [512, 512], P(('dp', 'fsdp')), may hold values from -0.25 to 0.25
- mix_weight: bfloat16 [512, 512], P(('dp', 'fsdp')), may hold values from -1 to 1
- expand_weight: bfloat16 [512, 2048], P(('dp', 'fsdp')), may hold values from -0.25 to 0.25
- shrink_weight: bfloat16 [2048, 512], P(('dp', 'fsdp')), may hold values from -0.125 to 0.125
- position_table: bfloat16 [512, 512], P(None, ('dp', 'fsdp')), may hold values from -4 to 4
- query_bias: bfloat16 [512], P(('dp', 'fsdp')), may hold values from -3 to 3
- value_bias: bfloat16 [512], P(('dp', 'fsdp')), may hold values from -3 to 3
- mix_bias: bfloat16 [512], P(('dp', 'fsdp')), may hold values from -3 to 3
- expand_bias: bfloat16 [2048], P(('dp', 'fsdp')), may hold values from -3 to 3
- shrink_bias: bfloat16 [512], P(('dp', 'fsdp')), may hold values from -3 to 3
- gain_one: bfloat16 [512], P(('dp', 'fsdp')), may hold values from 0.25 to 1.75
- shift_one: bfloat16 [512], P(('dp', 'fsdp')), may hold values from -3 to 3
- gain_two: bfloat16 [512], P(('dp', 'fsdp')), may hold values from 0.25 to 1.75
- shift_two: bfloat16 [512], P(('dp', 'fsdp')), may hold values from -3 to 3
Outputs:
- output: bfloat16 [2, 64, 512, 512], P(None, ('dp', 'fsdp'))
- grad_inputs: bfloat16 [2, 64, 512, 512], P(None, ('dp', 'fsdp'))
- grad_query_weight: float32 [512, 512], P(('dp', 'fsdp'))
- grad_key_weight: float32 [512, 512], P(('dp', 'fsdp'))
- grad_value_weight: float32 [512, 512], P(('dp', 'fsdp'))
- grad_mix_weight: float32 [512, 512], P(('dp', 'fsdp'))
- grad_expand_weight: float32 [512, 2048], P(('dp', 'fsdp'))
- grad_shrink_weight: float32 [2048, 512], P(('dp', 'fsdp'))
- grad_position_table: float32 [512, 512], P(None, ('dp', 'fsdp'))
- grad_query_bias: float32 [512], P(('dp', 'fsdp'))
- grad_value_bias: float32 [512], P(('dp', 'fsdp'))
- grad_mix_bias: float32 [512], P(('dp', 'fsdp'))
- grad_expand_bias: float32 [2048], P(('dp', 'fsdp'))
- grad_shrink_bias: float32 [512], P(('dp', 'fsdp'))
- grad_gain_one: float32 [512], P(('dp', 'fsdp'))
- grad_shift_one: float32 [512], P(('dp', 'fsdp'))
- grad_gain_two: float32 [512], P(('dp', 'fsdp'))
- grad_shift_two: float32 [512], P(('dp', 'fsdp'))
The draws below stay inside these ranges and needn't reach their ends.
Inputs may be any that keep to these rules, and one draw needn't show every extreme that they name: `lengths`: number of real characters of each window; the rest of the window is padding. In every draw some window has exactly 512.
All inputs are finite; a program needn't handle non-finite values.
Results may differ from the reference program's by a relative error of at most 0.013.
The reference program's roundings to bfloat16 on the way count: a program that leaves them out, or rounds other values in their place, can miss the bound.
Values may be sent and summed in bfloat16 or wider, within the bound.
A program may use at most 192 MiB of HBM per device.

```python
import jax
import jax.numpy as jnp
from jax import lax

D = 512
HEADS = 8
FF = 2048
SEQ = 512
MIN_LEN = 64
MICRO = 2
WINDOWS_MB = 64


def draw_lengths(key, part):
    key = jax.random.fold_in(key, 7)
    first_key, second_key = jax.random.split(key)
    drawn = jax.random.randint(first_key, (MICRO, WINDOWS_MB), MIN_LEN, SEQ + 1)
    chosen = jax.random.randint(second_key, (), 0, MICRO * WINDOWS_MB)
    flat_ids = lax.broadcasted_iota(jnp.int32, (MICRO, WINDOWS_MB), 0) * WINDOWS_MB + lax.broadcasted_iota(jnp.int32, (MICRO, WINDOWS_MB), 1)
    return jnp.where(flat_ids == chosen, SEQ, drawn).astype(jnp.int32)


def block_levels(rng, dims, cuts, least, high):
    factor_of, own = 1.0, jax.random.fold_in(rng, 6)
    for axis_at, shards_of in cuts:
        steps = jnp.exp(jax.random.uniform(jax.random.fold_in(own, axis_at), (shards_of,), jnp.float32, least / len(cuts), high / len(cuts)))
        factor_of = factor_of * jnp.repeat(steps, dims[axis_at] // shards_of).reshape([-1 if axis == axis_at else 1 for axis in range(len(dims))])
    return factor_of


def gaussian(own_key, dims, width, limit, cuts=(), kind=jnp.bfloat16):
    entries = jax.random.normal(own_key, dims, jnp.float32) * width
    if len(cuts) > 0:
        entries = block_levels(own_key, dims, cuts, -0.22, 0.18) * entries
    return jnp.clip(entries, min=-limit, max=limit).astype(kind)


def setup_inputs(seed: int = 0) -> dict:
    streams_of = jax.random.split(jax.random.key(seed), 20)
    inputs = gaussian(streams_of[0], (MICRO, WINDOWS_MB, SEQ, D), 1.0, 6.0, ((1, 32),))
    lengths = draw_lengths(jax.random.fold_in(streams_of[19], 71), 0)
    grad_out = gaussian(streams_of[2], (MICRO, WINDOWS_MB, SEQ, D), 1.0, 6.0, ((1, 32),))
    query_weight = gaussian(streams_of[3], (D, D), D ** -0.5, 0.25, ((0, 32),))
    key_weight = gaussian(streams_of[4], (D, D), D ** -0.5, 0.25, ((0, 32),))
    value_weight = gaussian(streams_of[5], (D, D), D ** -0.5, 0.25, ((0, 32),))
    mix_weight = gaussian(streams_of[6], (D, D), (D // 16) ** -0.5, 1.0, ((0, 32),))
    expand_weight = gaussian(streams_of[7], (D, FF), D ** -0.5, 0.25, ((0, 32),))
    shrink_weight = gaussian(streams_of[8], (FF, D), FF ** -0.5, 0.125, ((0, 32),))
    position_table = gaussian(streams_of[9], (SEQ, D), 0.5, 4.0, ((1, 32),))
    query_bias = gaussian(streams_of[10], (D,), 0.5, 3.0, ((0, 32),))
    value_bias = gaussian(streams_of[11], (D,), 0.5, 3.0, ((0, 32),))
    mix_bias = gaussian(streams_of[12], (D,), 0.5, 3.0, ((0, 32),))
    expand_bias = gaussian(streams_of[13], (FF,), 0.5, 3.0, ((0, 32),))
    shrink_bias = gaussian(streams_of[14], (D,), 0.5, 3.0, ((0, 32),))
    gain_one = jnp.clip(1.0 + 0.15 * jax.random.normal(streams_of[15], (D,), jnp.float32), 0.25, 1.75).astype(jnp.bfloat16)
    shift_one = gaussian(streams_of[16], (D,), 0.5, 3.0, ((0, 32),))
    gain_two = jnp.clip(1.0 + 0.15 * jax.random.normal(streams_of[17], (D,), jnp.float32), 0.25, 1.75).astype(jnp.bfloat16)
    shift_two = gaussian(streams_of[18], (D,), 0.5, 3.0, ((0, 32),))
    return {"inputs": inputs, "lengths": lengths, "grad_out": grad_out, "query_weight": query_weight, "key_weight": key_weight, "value_weight": value_weight, "mix_weight": mix_weight, "expand_weight": expand_weight, "shrink_weight": shrink_weight, "position_table": position_table, "query_bias": query_bias, "value_bias": value_bias, "mix_bias": mix_bias, "expand_bias": expand_bias, "shrink_bias": shrink_bias, "gain_one": gain_one, "shift_one": shift_one, "gain_two": gain_two, "shift_two": shift_two}


@jax.custom_vjp
def low(v):
    return lax.optimization_barrier(v.astype(jnp.bfloat16)).astype(jnp.float32)

@jax.custom_vjp
def low_back(v):
    return v

def low_keep(v):
    return (low(v), None)

def low_pass(kept, grad):
    return (grad,)

def back_keep(v):
    return (v, None)

def back_low(kept, grad):
    return (low(grad),)
low.defvjp(low_keep, low_pass)
low_back.defvjp(back_keep, back_low)
epsilon = 1e-05

def matmul(operand, weight):
    return jnp.einsum('wsd,de->wse', operand, weight, precision=lax.Precision.HIGHEST)

def norm_apply(summed, gain_vec, shift_vec):
    center = summed - lax.optimization_barrier(jnp.mean(summed, -1, keepdims=True))
    spread = lax.optimization_barrier(jnp.mean(center * center, -1, keepdims=True))
    return center * lax.rsqrt(spread + epsilon) * gain_vec + shift_vec

def forward(params, windows_in, window_lengths):
    query_weight, key_weight, value_weight, mix_weight, expand_weight, shrink_weight, position_table, query_bias, value_bias, mix_bias, expand_bias, shrink_bias, gain_one, shift_one, gain_two, shift_two = params
    window_count, seqlen, model_width = windows_in.shape
    head_size = model_width // HEADS
    score_scale = head_size ** (-0.5)
    hidden = windows_in + position_table[None]
    hidden_low = low(hidden)
    queries = low_back(low(matmul(hidden_low, query_weight) + query_bias))
    keys_low = low_back(low(matmul(hidden_low, key_weight)))
    values_low = low_back(low(matmul(hidden_low, value_weight) + value_bias))
    query_heads = queries.reshape(window_count, seqlen, HEADS, head_size)
    key_heads = keys_low.reshape(window_count, seqlen, HEADS, head_size)
    value_heads = values_low.reshape(window_count, seqlen, HEADS, head_size)
    raw_scores = jnp.einsum('wqhe,wkhe->whqk', query_heads, key_heads, precision=lax.Precision.HIGHEST)
    scores = low_back(raw_scores * score_scale)
    row_ids = lax.broadcasted_iota(jnp.int32, (seqlen, seqlen), 0)
    col_ids = lax.broadcasted_iota(jnp.int32, (seqlen, seqlen), 1)
    allowed = (col_ids <= row_ids)[None, None] & (col_ids[None, None] < window_lengths[:, None, None, None])
    masked = jnp.where(allowed, scores, -1e+30)
    row_top = lax.optimization_barrier(jnp.max(masked, -1, keepdims=True))
    exponent = jnp.exp(masked - row_top)
    denom_sum = lax.optimization_barrier(jnp.sum(exponent, -1, keepdims=True))
    attn_probs = exponent / denom_sum
    mixed_heads = jnp.einsum('whqk,wkhe->wqhe', low(attn_probs), value_heads, precision=lax.Precision.HIGHEST)
    mixed_low = low_back(low(mixed_heads)).reshape(window_count, seqlen, model_width)
    attn_out = low_back(matmul(mixed_low, mix_weight) + mix_bias)
    first_sum = hidden + attn_out
    normed = norm_apply(first_sum, gain_one, shift_one)
    pre_act = low_back(matmul(low(normed), expand_weight) + expand_bias)
    act_low = low(jax.nn.gelu(pre_act))
    ff_out = low_back(matmul(act_low, shrink_weight) + shrink_bias)
    return norm_apply(normed + ff_out, gain_two, shift_two)

def reference(inputs, lengths, grad_out, query_weight, key_weight, value_weight, mix_weight, expand_weight, shrink_weight, position_table, query_bias, value_bias, mix_bias, expand_bias, shrink_bias, gain_one, shift_one, gain_two, shift_two):
    params = tuple((member.astype(jnp.float32) for member in (query_weight, key_weight, value_weight, mix_weight, expand_weight, shrink_weight, position_table, query_bias, value_bias, mix_bias, expand_bias, shrink_bias, gain_one, shift_one, gain_two, shift_two)))
    per_group = 8
    group_count = MICRO * WINDOWS_MB // per_group
    windows_in = inputs.astype(jnp.float32).reshape(group_count, per_group, SEQ, D)
    block_lengths = lengths.astype(jnp.int32).reshape(group_count, per_group)
    row_ids = jnp.arange(SEQ, dtype=jnp.int32)
    row_keep = (row_ids[None, None, :] < block_lengths[:, :, None]).astype(jnp.float32)
    cotangent = grad_out.astype(jnp.float32).reshape(group_count, per_group, SEQ, D) * row_keep[..., None]

    def one_group(running, pieces):
        block_in, block_len, block_cot = pieces
        result, pullback = jax.vjp(lambda weights, activity: forward(weights, activity, block_len), params, block_in)
        grad_params, grad_acts = pullback(block_cot)
        running = tuple((first + second for first, second in zip(running, grad_params)))
        return (running, (result.astype(jnp.bfloat16), grad_acts.astype(jnp.bfloat16)))
    zero_grads = tuple((jnp.zeros_like(member) for member in params))
    totals, (outputs, grads_in) = lax.scan(one_group, zero_grads, (windows_in, block_lengths, cotangent))
    return (outputs.reshape(MICRO, WINDOWS_MB, SEQ, D), grads_in.reshape(MICRO, WINDOWS_MB, SEQ, D), totals[0], totals[1], totals[2], totals[3], totals[4], totals[5], totals[6], totals[7], totals[8], totals[9], totals[10], totals[11], totals[12], totals[13], totals[14], totals[15])
```

```python
import functools
import jax, jax.numpy as jnp
from jax import lax
from jax.experimental import pallas as pl
from jax.experimental.pallas import tpu as pltpu
from jax.sharding import PartitionSpec as P

HEADS = 8
EPS = 1e-05
BF = jnp.bfloat16
F32 = jnp.float32
GELU_C = 0.7978845608028654
GELU_A = 0.044715


def nn(a, b):
    return lax.dot_general(a, b, (((1,), (0,)), ((), ())), preferred_element_type=F32)


def nt(a, b):
    return lax.dot_general(a, b, (((1,), (1,)), ((), ())), preferred_element_type=F32)


def tn(a, b):
    return lax.dot_general(a, b, (((0,), (0,)), ((), ())), preferred_element_type=F32)


def rows_of(vec, index):
    return vec[index : index + 1, :]


(BQ, BV, BM, BS, G1, S1, G2, S2) = range(8)


def attention_forward(w, r):
    seq, width = r.x.shape[1:]
    half = seq // 2
    head = width // HEADS
    hid = r.x[w].astype(F32) + r.pos[...].astype(F32)
    low = hid.astype(BF)
    r.low[w] = low
    r.q[w] = (((nn(low, r.wq[...]) + r.vec[BQ : BQ + 1, :]).astype(BF)).astype(F32) * (head**-0.5)).astype(BF)
    r.k[w] = nn(low, r.wk[...]).astype(BF)
    values = (nn(low, r.wv[...]) + r.vec[BV : BV + 1, :]).astype(BF)
    r.v[w] = values
    r.vt[...] = values.T
    make_mask(w, r)
    lane = lax.broadcasted_iota(jnp.int32, (seq, 2 * head), 1)
    for h in range(HEADS):
        pair = slice((h // 2) * 2 * head, (h // 2 + 1) * 2 * head)
        mine = (lane < head) if h % 2 == 0 else (lane >= head)
        qh = jnp.where(mine, r.q[w, :, pair], jnp.zeros((), BF))
        kp = r.k[w, :, pair]
        s0 = nt(kp[:half], qh) + r.mask[:half, :]
        s1 = nt(kp[half:], qh[half:]) + r.mask[half:, half:]
        m_left = jnp.max(s0[:, :half], axis=0, keepdims=True)
        m_right = jnp.maximum(
            jnp.max(s0[:, half:], axis=0, keepdims=True), jnp.max(s1, axis=0, keepdims=True)
        )
        top = jnp.concatenate([m_left, m_right], axis=1)
        e0 = jnp.exp(s0 - top)
        e1 = jnp.exp(s1 - m_right)
        n_all = jnp.sum(e0, axis=0, keepdims=True)
        n_right = n_all[:, half:] + jnp.sum(e1, axis=0, keepdims=True)
        total = jnp.concatenate([n_all[:, :half], n_right], axis=1)
        r.logt[w, h : h + 1, :] = top + jnp.log(total)
        inv = 1.0 / total
        p0 = (e0 * inv).astype(BF)
        p1 = (e1 * inv[:, half:]).astype(BF)
        vt = r.vt[h * head : (h + 1) * head, :]
        o_left = nn(vt[:, :half], p0[:, :half])
        o_right = nn(vt, jnp.concatenate([p0[:, half:], p1], axis=0))
        r.ot[h * head : (h + 1) * head, :half] = o_left.astype(BF)
        r.ot[h * head : (h + 1) * head, half:] = o_right.astype(BF)
    r.mixed[w] = r.ot[...].T


def make_mask(w, r):
    seq = r.x.shape[1]
    key_at = lax.broadcasted_iota(jnp.int32, (seq, seq), 0)
    query_at = lax.broadcasted_iota(jnp.int32, (seq, seq), 1)
    ok = (key_at <= query_at) & (key_at < r.lens[w])
    r.mask[...] = jnp.where(ok, 0.0, -1e30)


def norm_parts(total):
    center = total - jnp.mean(total, -1, keepdims=True)
    spread = jnp.mean(center * center, -1, keepdims=True)
    inv = lax.rsqrt(spread + EPS)
    return center * inv, inv


def norm_back(e, xhat, inv):
    return inv * (
        e - jnp.mean(e, -1, keepdims=True) - xhat * jnp.mean(e * xhat, -1, keepdims=True)
    )


def add_row(ref, index, value):
    ref[index : index + 1, :] += jnp.sum(value, axis=0, keepdims=True)


def feed_forward(w, r):
    seq, width = r.x.shape[1:]
    ff = r.we.shape[1]
    chunk = 512
    hid = r.x[w].astype(F32) + r.pos[...].astype(F32)
    mixed = r.mixed[w]
    first = hid + (nn(mixed, r.wm[...]) + r.vec[BM : BM + 1, :])
    xhat1, inv1 = norm_parts(first)
    r.xh1[...] = xhat1
    normed = xhat1 * r.vec[G1 : G1 + 1, :] + r.vec[S1 : S1 + 1, :]
    r.nl[...] = normed.astype(BF)
    ff_out = None
    for c in range(ff // chunk):
        cols = slice(c * chunk, (c + 1) * chunk)
        t = nn(r.nl[...], r.we[:, cols]) + r.eb[:, cols]
        t2 = t * t
        th = jnp.tanh(t * (t2 * (GELU_A * GELU_C) + GELU_C))
        ht = 0.5 * t
        act = (ht * th + ht).astype(BF)
        r.act[:, cols] = act
        slope = (0.5 * th + 0.5) + ht * (1.0 - th * th) * (t2 * (3 * GELU_A * GELU_C) + GELU_C)
        r.slope[:, cols] = slope
        part = nn(act, r.ws[cols, :])
        ff_out = part if ff_out is None else ff_out + part
    second = normed + (ff_out + r.vec[BS : BS + 1, :])
    xhat2, inv2 = norm_parts(second)
    r.out[w] = (xhat2 * r.vec[G2 : G2 + 1, :] + r.vec[S2 : S2 + 1, :]).astype(BF)
    row_at = lax.broadcasted_iota(jnp.int32, (seq, width), 0)
    cot = jnp.where(row_at < r.lens[w], r.go[w].astype(F32), 0.0)
    add_row(r.gvec, G2, cot * xhat2)
    add_row(r.gvec, S2, cot)
    d_second = norm_back(cot * r.vec[G2 : G2 + 1, :], xhat2, inv2)
    gff = d_second.astype(BF)
    r.gff[...] = gff
    add_row(r.gvec, BS, gff.astype(F32))
    d_normed = d_second
    for c in range(ff // chunk):
        cols = slice(c * chunk, (c + 1) * chunk)
        gpre = (nt(r.gff[...], r.ws[cols, :]) * r.slope[:, cols]).astype(BF)
        add_row_cols(r.geb, cols, gpre.astype(F32))
        r.gws[cols, :] += tn(r.act[:, cols], r.gff[...])
        r.gwe[:, cols] += tn(r.nl[...], gpre)
        d_normed = d_normed + nt(gpre, r.we[:, cols])
    xhat1 = r.xh1[...]
    add_row(r.gvec, G1, d_normed * xhat1)
    add_row(r.gvec, S1, d_normed)
    d_first = norm_back(d_normed * r.vec[G1 : G1 + 1, :], xhat1, inv1)
    r.dfirst[w] = d_first
    gattn = d_first.astype(BF)
    add_row(r.gvec, BM, gattn.astype(F32))
    r.gwm[...] += tn(mixed, gattn)
    gmix = nt(gattn, r.wm[...]).astype(BF)
    head = width // HEADS
    prod = gmix.astype(F32) * mixed.astype(F32)
    hi = prod.astype(BF)
    lo = (prod - hi.astype(F32)).astype(BF)
    sel_row = lax.broadcasted_iota(jnp.int32, (16, width), 0)
    sel_col = lax.broadcasted_iota(jnp.int32, (16, width), 1)
    sel = jnp.where(sel_col // head == sel_row, 1.0, 0.0).astype(BF)
    r.delta[w] = nt(sel, hi) + nt(sel, lo)
    r.mixed[w] = gmix


def add_row_cols(ref, cols, value):
    ref[:, cols] += jnp.sum(value, axis=0, keepdims=True)


def attention_backward(w, r):
    seq, width = r.x.shape[1:]
    half = seq // 2
    head = width // HEADS
    scale = head**-0.5
    make_mask(w, r)
    r.kt[...] = r.k[w].T
    lane = lax.broadcasted_iota(jnp.int32, (seq, 2 * head), 1)
    for p in range(HEADS // 2):
        pair = slice(p * 2 * head, (p + 1) * 2 * head)
        kp = r.k[w, :, pair]
        vp = r.v[w, :, pair]
        dk_top = dk_low = dv_top = dv_low = None
        for odd in range(2):
            h = 2 * p + odd
            mine = (lane >= head) if odd else (lane < head)
            qh = jnp.where(mine, r.q[w, :, pair], jnp.zeros((), BF))
            gh = jnp.where(mine, r.mixed[w, :, pair], jnp.zeros((), BF))
            logt = r.logt[w, h : h + 1, :]
            delta = r.delta[w, h : h + 1, :]
            p0 = jnp.exp(nt(kp[:half], qh) + r.mask[:half, :] - logt)
            p1 = jnp.exp(nt(kp[half:], qh[half:]) + r.mask[half:, half:] - logt[:, half:])
            d0 = (p0 * (nt(vp[:half], gh) - delta)).astype(BF)
            d1 = (p1 * (nt(vp[half:], gh[half:]) - delta[:, half:])).astype(BF)
            p0 = p0.astype(BF)
            p1 = p1.astype(BF)
            parts = (nn(d0, qh), nn(d1, qh[half:]), nn(p0, gh), nn(p1, gh[half:]))
            if odd:
                dk_top, dk_low, dv_top, dv_low = (
                    first + second for first, second in zip((dk_top, dk_low, dv_top, dv_low), parts)
                )
            else:
                dk_top, dk_low, dv_top, dv_low = parts
            kt = r.kt[h * head : (h + 1) * head, :]
            q_left = nn(kt[:, :half], d0[:, :half])
            q_right = nn(kt, jnp.concatenate([d0[:, half:], d1], axis=0))
            r.ot[h * head : (h + 1) * head, :half] = (q_left * scale).astype(BF)
            r.ot[h * head : (h + 1) * head, half:] = (q_right * scale).astype(BF)
        r.gk[:half, pair] = dk_top.astype(BF)
        r.gk[half:, pair] = dk_low.astype(BF)
        r.gv[:half, pair] = dv_top.astype(BF)
        r.gv[half:, pair] = dv_low.astype(BF)
    gq = r.ot[...].T
    gk = r.gk[...]
    gv = r.gv[...]
    low = r.low[w]
    r.gwq[...] += tn(low, gq)
    r.gwk[...] += tn(low, gk)
    r.gwv[...] += tn(low, gv)
    add_row(r.gvec, BQ, gq.astype(F32))
    add_row(r.gvec, BV, gv.astype(F32))
    d_hidden = r.dfirst[w] + nt(gq, r.wq[...]) + nt(gk, r.wk[...]) + nt(gv, r.wv[...])
    r.gpos[...] += d_hidden
    r.gin[w] = d_hidden.astype(BF)


class Refs:
    def __init__(self, **kw):
        self.__dict__.update(kw)


IN_NAMES = ("lens", "x", "go", "wq", "wk", "wv", "wm", "we", "ws", "pos", "vec", "eb")
OUT_NAMES = ("out", "gin", "gwq", "gwk", "gwv", "gwm", "gwe", "gws", "gpos", "gvec", "geb")


def scratch_list(count, seq, width, ff):
    return dict(
        low=pltpu.VMEM((count, seq, width), BF),
        q=pltpu.VMEM((count, seq, width), BF),
        k=pltpu.VMEM((count, seq, width), BF),
        v=pltpu.VMEM((count, seq, width), BF),
        mixed=pltpu.VMEM((count, seq, width), BF),
        logt=pltpu.VMEM((count, HEADS, seq), F32),
        delta=pltpu.VMEM((count, 16, seq), F32),
        dfirst=pltpu.VMEM((count, seq, width), F32),
        vt=pltpu.VMEM((width, seq), BF),
        kt=pltpu.VMEM((width, seq), BF),
        ot=pltpu.VMEM((width, seq), BF),
        gk=pltpu.VMEM((seq, width), BF),
        gv=pltpu.VMEM((seq, width), BF),
        mask=pltpu.VMEM((seq, seq), F32),
        xh1=pltpu.VMEM((seq, width), F32),
        nl=pltpu.VMEM((seq, width), BF),
        gff=pltpu.VMEM((seq, width), BF),
        act=pltpu.VMEM((seq, ff), BF),
        slope=pltpu.VMEM((seq, ff), F32),
    )


def compute_kernel(names, phases, *refs):
    r = Refs(**dict(zip(names, refs)))
    for name in OUT_NAMES[2:]:
        ref = getattr(r, name)
        ref[...] = jnp.zeros(ref.shape, ref.dtype)
    count = r.x.shape[0]
    def loop(fn):
        def body(w, c):
            fn(w, r)
            return c
        lax.fori_loop(0, count, body, 0)
    if 1 in phases: loop(attention_forward)
    if 2 in phases: loop(feed_forward)
    if 3 in phases: loop(attention_backward)


def compute(lens, x, go, wq, wk, wv, wm, we, ws, pos, vec, eb, phases=(1, 2, 3)):
    count, seq, width = x.shape
    ff = we.shape[1]
    scr = scratch_list(count, seq, width, ff)
    S = jax.ShapeDtypeStruct
    outs = (
        S((count, seq, width), BF), S((count, seq, width), BF),
        S((width, width), F32), S((width, width), F32), S((width, width), F32), S((width, width), F32),
        S((width, ff), F32), S((ff, width), F32), S((seq, width), F32), S((8, width), F32), S((1, ff), F32),
    )
    names = IN_NAMES + OUT_NAMES + tuple(scr)
    vm = pl.BlockSpec(memory_space=pltpu.VMEM)
    return pl.pallas_call(
        functools.partial(compute_kernel, names, phases),
        out_shape=outs,
        in_specs=[pl.BlockSpec(memory_space=pltpu.SMEM)] + [vm] * (len(IN_NAMES) - 1),
        out_specs=[vm] * len(outs),
        scratch_shapes=list(scr.values()),
        compiler_params=pltpu.CompilerParams(vmem_limit_bytes=63 * 2**20),
        name="layer",
    )(lens, x, go, wq, wk, wv, wm, we, ws, pos, vec, eb)


MESH = pl.DeviceIdType.MESH


class Place:
    def __init__(self, dp_count, z_count):
        self.dp_count, self.z_count = dp_count, z_count
        self.dp = lax.axis_index("dp")
        fsdp = lax.axis_index("fsdp")
        self.z, self.c = fsdp // 2, lax.rem(fsdp, 2)

    def z_at(self, shift):
        return lax.rem(self.z + shift + self.z_count, self.z_count)

    def dp_at(self, shift):
        return lax.rem(self.dp + shift + self.dp_count, self.dp_count)

    def peers(self):
        near = [(self.dp, self.z * 2 + (1 - self.c))]
        along_z = [(self.dp, self.z_at(s) * 2 + self.c) for s in range(1, self.z_count)]
        along_dp = [(self.dp_at(s), self.z * 2 + self.c) for s in range(1, self.dp_count)]
        return near, along_z, along_dp

    def barrier(self):
        sem = pltpu.get_barrier_semaphore()
        near, along_z, along_dp = self.peers()
        everyone = near + along_z + along_dp
        for peer in everyone:
            pl.semaphore_signal(sem, inc=1, device_id=peer, device_id_type=MESH)
        pl.semaphore_wait(sem, len(everyone))


def remote(src, dst, sems, index, peer):
    send, recv = sems
    return pltpu.make_async_remote_copy(
        src_ref=src, dst_ref=dst, send_sem=send.at[index], recv_sem=recv.at[index],
        device_id=peer, device_id_type=MESH,
    )


class Gather:
    def __init__(self, place, shard, whole, sems):
        self.p, self.shard, self.whole, self.sems = place, shard, whole, sems
        self.near, self.along_z, self.along_dp = place.peers()

    def z_copy(self, shift, z):
        p = self.p
        return remote(self.shard, self.whole.at[p.dp, z, p.c], self.sems, shift - 1, self.along_z[shift - 1])

    def dp_copy(self, shift, dp):
        p = self.p
        at = self.p.z_count - 1 + shift - 1
        return remote(self.whole.at[p.dp, :, p.c], self.whole.at[dp, :, p.c], self.sems, at, self.along_dp[shift - 1])

    def core_copy(self, core):
        at = self.p.z_count + self.p.dp_count - 2
        return remote(self.whole.at[:, :, self.p.c], self.whole.at[:, :, core], self.sems, at, self.near[0])

    def start_z(self):
        p = self.p
        for shift in range(1, p.z_count):
            self.z_copy(shift, p.z).start()
        self.whole[p.dp, p.z, p.c] = self.shard[...]

    def start_dp(self):
        p = self.p
        for shift in range(1, p.z_count):
            self.z_copy(shift, p.z_at(-shift)).wait_recv()
        for shift in range(1, p.dp_count):
            self.dp_copy(shift, p.dp).start()

    def start_core(self):
        p = self.p
        for shift in range(1, p.dp_count):
            self.dp_copy(shift, p.dp_at(-shift)).wait_recv()
        self.core_copy(p.c).start()

    def finish(self):
        self.core_copy(1 - self.p.c).wait_recv()

    def drain(self):
        p = self.p
        for shift in range(1, p.z_count):
            self.z_copy(shift, p.z).wait_send()
        for shift in range(1, p.dp_count):
            self.dp_copy(shift, p.dp).wait_send()
        self.core_copy(p.c).wait_send()


class Scatter:
    def __init__(self, place, total, result, bufs, sems):
        self.p, self.total, self.result, self.sems = place, total, result, sems
        self.to_core, self.from_core, self.to_dp, self.from_dp, self.from_z, self.own = bufs
        self.near, self.along_z, self.along_dp = place.peers()

    def core_copy(self):
        at = self.p.z_count + self.p.dp_count - 2
        return remote(self.to_core, self.from_core, self.sems, at, self.near[0])

    def dp_copy(self, shift):
        at = self.p.z_count - 1 + shift - 1
        return remote(self.to_dp.at[self.p.dp_at(shift)], self.from_dp.at[shift - 1], self.sems, at, self.along_dp[shift - 1])

    def z_copy(self, shift):
        return remote(self.to_dp.at[self.p.dp, self.p.z_at(shift)], self.from_z.at[shift - 1], self.sems, shift - 1, self.along_z[shift - 1])

    def start_core(self):
        self.to_core[...] = self.total[:, :, 1 - self.p.c].astype(BF)
        self.core_copy().start()

    def start_dp(self):
        p = self.p
        self.core_copy().wait_recv()
        both = self.total[:, :, p.c] + self.from_core[...].astype(F32)
        self.to_dp[...] = both.astype(BF)
        for shift in range(1, p.dp_count):
            self.dp_copy(shift).start()
        self.own[...] = self.total[p.dp, :, p.c] + self.from_core[p.dp].astype(F32)

    def start_z(self):
        p = self.p
        for shift in range(1, p.dp_count):
            self.dp_copy(shift).wait_recv()
        added = self.own[...]
        for shift in range(1, p.dp_count):
            added = added + self.from_dp[shift - 1].astype(F32)
        self.own[...] = added
        self.to_dp[p.dp] = added.astype(BF)
        for shift in range(1, p.z_count):
            self.z_copy(shift).start()

    def finish(self):
        p = self.p
        for shift in range(1, p.z_count):
            self.z_copy(shift).wait_recv()
        added = self.own[p.z]
        for shift in range(1, p.z_count):
            added = added + self.from_z[shift - 1].astype(F32)
        self.result[...] = added

    def drain(self):
        p = self.p
        self.core_copy().wait_send()
        for shift in range(1, p.dp_count):
            self.dp_copy(shift).wait_send()
        for shift in range(1, p.z_count):
            self.z_copy(shift).wait_send()


class SumAll:
    def __init__(self, place, total, bufs, sems):
        self.p, self.total, self.sems = place, total, sems
        self.send_dp, self.send_z, self.landing = bufs
        self.near, self.along_z, self.along_dp = place.peers()

    def copies(self, hop):
        p = self.p
        z, dp = p.z_count - 1, p.dp_count - 1
        if hop == 0:
            return [remote(self.total, self.landing.at[z + dp], self.sems, z + dp, self.near[0])]
        if hop == 1:
            return [remote(self.send_dp, self.landing.at[z + s], self.sems, z + s, self.along_dp[s]) for s in range(dp)]
        return [remote(self.send_z, self.landing.at[s], self.sems, s, self.along_z[s]) for s in range(z)]

    def arrived(self, hop, first):
        for copy in self.copies(hop):
            copy.wait_recv()
        z, dp = self.p.z_count - 1, self.p.dp_count - 1
        slots = ([z + dp], range(z, z + dp), range(z))[hop]
        added = first[...]
        for slot in slots:
            added = added + self.landing[slot]
        return added

    def start_core(self):
        self.copies(0)[0].start()

    def start_dp(self):
        self.send_dp[...] = self.arrived(0, self.total)
        for copy in self.copies(1):
            copy.start()

    def start_z(self):
        self.send_z[...] = self.arrived(1, self.send_dp)
        for copy in self.copies(2):
            copy.start()

    def finish(self, result):
        result[...] = self.arrived(2, self.send_z)

    def drain(self):
        for hop in range(3):
            for copy in self.copies(hop):
                copy.wait_send()


def sem_pair(place_counts):
    dp_count, z_count = place_counts
    hops = dp_count + z_count - 1
    return [pltpu.SemaphoreType.DMA((hops,)), pltpu.SemaphoreType.DMA((hops,))]


AXES = ("dp", "fsdp")
LANES = 128


def gather_kernel(counts, tensors, *refs):
    shards, wholes, sems = refs[:tensors], refs[tensors : 2 * tensors], refs[2 * tensors :]
    place = Place(*counts)
    place.barrier()
    gathers = [
        Gather(place, shard, whole, (sems[2 * i], sems[2 * i + 1]))
        for i, (shard, whole) in enumerate(zip(shards, wholes))
    ]
    for step in ("start_z", "start_dp", "start_core", "finish", "drain"):
        for gather in gathers:
            getattr(gather, step)()


def gather_all(counts, shards):
    dp_count, z_count = counts
    vm = pl.BlockSpec(memory_space=pltpu.VMEM)
    outs = pl.pallas_call(
        functools.partial(gather_kernel, counts, len(shards)),
        out_shape=tuple(
            jax.ShapeDtypeStruct((dp_count, z_count, 2) + shard.shape, shard.dtype) for shard in shards
        ),
        in_specs=[vm] * len(shards),
        out_specs=[vm] * len(shards),
        scratch_shapes=sum([sem_pair(counts) for _ in shards], []),
        compiler_params=pltpu.CompilerParams(
            collective_id=0, has_side_effects=True, vmem_limit_bytes=60 * 2**20
        ),
        name="gather",
    )(*shards)
    return [out.reshape((-1,) + out.shape[4:]) for out in outs]


def scatter_kernel(counts, tensors, *refs):
    totals, small = refs[:tensors], refs[tensors]
    results, small_result = refs[tensors + 1 : 2 * tensors + 1], refs[2 * tensors + 1]
    rest = list(refs[2 * tensors + 2 :])
    place = Place(*counts)
    place.barrier()
    jobs = []
    for total, result in zip(totals, results):
        bufs, sems, rest = rest[:6], rest[6:8], rest[8:]
        jobs.append(Scatter(place, total, result, bufs, sems))
    sums = SumAll(place, small, rest[:3], rest[3:5])
    for step in ("start_core", "start_dp", "start_z"):
        for job in jobs:
            getattr(job, step)()
        getattr(sums, step)()
    for job in jobs:
        job.finish()
    sums.finish(small_result)
    for job in jobs + [sums]:
        job.drain()


def scatter_bufs(counts, shape):
    dp_count, z_count = counts
    return [
        pltpu.VMEM((dp_count, z_count) + shape, BF),
        pltpu.VMEM((dp_count, z_count) + shape, BF),
        pltpu.VMEM((dp_count, z_count) + shape, BF),
        pltpu.VMEM((dp_count - 1, z_count) + shape, BF),
        pltpu.VMEM((z_count - 1,) + shape, BF),
        pltpu.VMEM((z_count,) + shape, F32),
    ]


def scatter_all(counts, totals, small):
    dp_count, z_count = counts
    devices = dp_count * z_count * 2
    vm = pl.BlockSpec(memory_space=pltpu.VMEM)
    totals = [total.reshape((dp_count, z_count, 2, -1) + total.shape[1:]) for total in totals]
    shapes = [total.shape[3:] for total in totals]
    scratch = []
    for shape in shapes:
        scratch += scatter_bufs(counts, shape) + sem_pair(counts)
    hops = dp_count + z_count - 1
    scratch += [pltpu.VMEM(small.shape, F32), pltpu.VMEM(small.shape, F32), pltpu.VMEM((hops,) + small.shape, F32)]
    scratch += sem_pair(counts)
    return pl.pallas_call(
        functools.partial(scatter_kernel, counts, len(totals)),
        out_shape=tuple(jax.ShapeDtypeStruct(shape, F32) for shape in shapes)
        + (jax.ShapeDtypeStruct(small.shape, F32),),
        in_specs=[vm] * (len(totals) + 1),
        out_specs=[vm] * (len(totals) + 1),
        scratch_shapes=scratch,
        compiler_params=pltpu.CompilerParams(
            collective_id=1, has_side_effects=True, vmem_limit_bytes=60 * 2**20
        ),
        name="scatter",
    )(*totals, small)


def local(dp_count, fsdp_count, inputs, lengths, grad_out, *params):
    micro, windows, seq, width = inputs.shape
    count = micro * windows
    wq, wk, wv, wm, we, ws, pos = params[:7]
    bq, bv, bm, eb, bs, g1, s1, g2, s2 = params[7:]
    devices = dp_count * fsdp_count
    counts = (dp_count, fsdp_count // 2)
    rows = wq.shape[0]
    remote_path = fsdp_count % 2 == 0 and rows % 16 == 0 and ws.shape[0] <= LANES and LANES % ws.shape[0] == 0
    me = lax.axis_index("dp") * fsdp_count + lax.axis_index("fsdp")
    vectors = (bq, bv, bm, bs, g1, s1, g2, s2)
    if remote_path:
        lane = lax.broadcasted_iota(jnp.int32, (1, LANES), 1)
        per_row, per_row_ff = LANES // rows, LANES // eb.shape[0]
        eight = jnp.where(
            lane // rows == me % per_row, jnp.tile(jnp.stack(vectors), (1, per_row)), jnp.zeros((), BF)
        )
        one = jnp.where(
            lane // eb.shape[0] == me % per_row_ff, jnp.tile(eb[None], (1, per_row_ff)), jnp.zeros((), BF)
        )
        small = jnp.concatenate([eight, one, jnp.zeros((7, LANES), BF)], axis=0)
        gathered = gather_all(counts, (pos.T, wq, wk, wv, small, wm, we, ws))
        post, wq, wk, wv, small, wm, we, ws = gathered
        pos = post.T
        blocks = small.reshape(devices, 16, LANES).astype(F32)
        vec = blocks[:, :8].reshape(devices // per_row, per_row, 8, LANES).sum(1)
        vec = vec.transpose(1, 0, 2).reshape(8, width)
        eb_all = blocks[:, 8].reshape(devices // per_row_ff, per_row_ff, LANES).sum(1).reshape(1, -1)
    else:
        whole = lambda a, axis=0: lax.all_gather(a, AXES, axis=axis, tiled=True)
        wq, wk, wv, wm, we, ws = (whole(a) for a in (wq, wk, wv, wm, we, ws))
        pos = whole(pos, 1)
        vec = jnp.stack([whole(a).astype(F32) for a in vectors])
        eb_all = whole(eb).astype(F32)[None]
    flat = lambda a: a.reshape((count,) + a.shape[2:])
    out, gin, gwq, gwk, gwv, gwm, gwe, gws, gpos, gvec, geb = compute(
        lengths.reshape(count), flat(inputs), flat(grad_out), wq, wk, wv, wm, we, ws, pos, vec, eb_all
    )
    if remote_path:
        small = jnp.concatenate([gvec, geb.reshape(-1, width), jnp.zeros((4, width), F32)], axis=0)
        gwe, gws, gwm, gwq, gwk, gwv, gpost, small = scatter_all(
            counts, (gwe, gws, gwm, gwq, gwk, gwv, gpos.T), small
        )
        gpos = gpost.T
        mine = lax.dynamic_slice(small[:8], (0, me * rows), (8, rows))
        geb = lax.dynamic_slice(small[8:12].reshape(-1), (me * eb.shape[0],), eb.shape)
        gvec = tuple(mine[i] for i in range(8))
    else:
        share = lambda a, axis=0: lax.psum_scatter(a, AXES, scatter_dimension=axis, tiled=True)
        gwq, gwk, gwv, gwm, gwe, gws = (share(a) for a in (gwq, gwk, gwv, gwm, gwe, gws))
        gpos = share(gpos, 1)
        gvec = tuple(share(gvec[i]) for i in range(8))
        geb = share(geb[0])
    gbq, gbv, gbm, gbs, gg1, gs1, gg2, gs2 = gvec
    return (
        out.reshape(inputs.shape), gin.reshape(inputs.shape), gwq, gwk, gwv, gwm, gwe, gws, gpos,
        gbq, gbv, gbm, geb, gbs, gg1, gs1, gg2, gs2,
    )


def solution(mesh):
    batch = P(None, AXES, None, None)
    matrix, vector, table = P(AXES, None), P(AXES), P(None, AXES)
    weights = (matrix,) * 6 + (table,) + (vector,) * 9
    return jax.shard_map(
        functools.partial(local, mesh.shape["dp"], mesh.shape["fsdp"]),
        mesh=mesh,
        in_specs=(batch, P(None, AXES), batch) + weights,
        out_specs=(batch, batch) + weights,
        check_vma=False,
    )
```

```python
import functools

import jax
import jax.numpy as jnp
from jax import lax
from jax.experimental import pallas as pl
from jax.experimental.pallas import tpu as pltpu
from jax.sharding import PartitionSpec as P

HEADS = 8
EPS = 1e-05
BF = jnp.bfloat16
F32 = jnp.float32
GELU_C = 0.7978845608028654
GELU_A = 0.044715
AXES = ("dp", "fsdp")
LANES = 128
MESH = pl.DeviceIdType.MESH
FF_PARTS = 2

(BQ, BV, BM, BS, G1, S1, G2, S2) = range(8)


class Refs:
    def __init__(self, **kw):
        self.__dict__.update(kw)


def nn(a, b):
    return lax.dot_general(a, b, (((1,), (0,)), ((), ())), preferred_element_type=F32)


def nt(a, b):
    return lax.dot_general(a, b, (((1,), (1,)), ((), ())), preferred_element_type=F32)


def tn(a, b):
    return lax.dot_general(a, b, (((0,), (0,)), ((), ())), preferred_element_type=F32)


def flat(value):
    return value.reshape(-1, value.shape[-1])


def add_into(ref, value):
    ref[...] += value.reshape(ref.shape)


def add_row(ref, index, value):
    ref[index : index + 1, :] += jnp.sum(value, axis=0, keepdims=True)


def make_mask(w, r):
    seq = r.x.shape[1]
    key_at = lax.broadcasted_iota(jnp.int32, (seq, seq), 0)
    query_at = lax.broadcasted_iota(jnp.int32, (seq, seq), 1)
    ok = (key_at <= query_at) & (key_at < r.lens[w])
    r.mask[...] = jnp.where(ok, 0.0, -1e30)


def hidden_and_keys(w, r):
    low = (r.x[w].astype(F32) + r.pos[...].astype(F32)).astype(BF)
    r.low[w] = low
    r.k[w] = nn(low, flat(r.wk[...])).astype(BF)


def attention_forward(w, r, hook):
    seq, width = r.x.shape[1:]
    half = seq // 2
    head = width // HEADS
    low = r.low[w]
    queries = (nn(low, flat(r.wq[...])) + r.vec[BQ : BQ + 1, :]).astype(BF)
    r.q[w] = (queries.astype(F32) * (head**-0.5)).astype(BF)
    values = (nn(low, flat(r.wv[...])) + r.vec[BV : BV + 1, :]).astype(BF)
    r.v[w] = values
    r.vt[...] = values.T
    make_mask(w, r)
    lane = lax.broadcasted_iota(jnp.int32, (seq, 2 * head), 1)
    for h in range(HEADS):
        if h == HEADS // 2:
            hook(w)
        pair = slice((h // 2) * 2 * head, (h // 2 + 1) * 2 * head)
        mine = (lane < head) if h % 2 == 0 else (lane >= head)
        qh = jnp.where(mine, r.q[w, :, pair], jnp.zeros((), BF))
        kp = r.k[w, :, pair]
        s0 = nt(kp[:half], qh) + r.mask[:half, :]
        s1 = nt(kp[half:], qh[half:]) + r.mask[half:, half:]
        m_left = jnp.max(s0[:, :half], axis=0, keepdims=True)
        m_right = jnp.maximum(
            jnp.max(s0[:, half:], axis=0, keepdims=True), jnp.max(s1, axis=0, keepdims=True)
        )
        top = jnp.concatenate([m_left, m_right], axis=1)
        e0 = jnp.exp(s0 - top)
        e1 = jnp.exp(s1 - m_right)
        n_all = jnp.sum(e0, axis=0, keepdims=True)
        n_right = n_all[:, half:] + jnp.sum(e1, axis=0, keepdims=True)
        total = jnp.concatenate([n_all[:, :half], n_right], axis=1)
        r.logt[w, h : h + 1, :] = top + jnp.log(total)
        inv = 1.0 / total
        p0 = (e0 * inv).astype(BF)
        p1 = (e1 * inv[:, half:]).astype(BF)
        vt = r.vt[h * head : (h + 1) * head, :]
        o_left = nn(vt[:, :half], p0[:, :half])
        o_right = nn(vt, jnp.concatenate([p0[:, half:], p1], axis=0))
        r.ot[h * head : (h + 1) * head, :half] = o_left.astype(BF)
        r.ot[h * head : (h + 1) * head, half:] = o_right.astype(BF)
    r.mixed[w] = r.ot[...].T


def norm_parts(total):
    center = total - jnp.mean(total, -1, keepdims=True)
    spread = jnp.mean(center * center, -1, keepdims=True)
    inv = lax.rsqrt(spread + EPS)
    return center * inv, inv


def norm_back(e, xhat, inv):
    return inv * (
        e - jnp.mean(e, -1, keepdims=True) - xhat * jnp.mean(e * xhat, -1, keepdims=True)
    )


def feed_forward(w, part, r):
    rows, width = r.nl.shape[0] // FF_PARTS, r.x.shape[-1]
    here = pl.ds(pl.multiple_of(part * rows, rows), rows)
    chunks = r.ws.shape[0]
    chunk = r.we.shape[-1] // chunks
    hid = r.x[w, here, :].astype(F32) + r.pos[here, :].astype(F32)
    first = hid + (nn(r.mixed[w, here, :], flat(r.wm[...])) + r.vec[BM : BM + 1, :])
    xhat1, inv1 = norm_parts(first)
    r.xh1[:rows] = xhat1
    normed = xhat1 * r.vec[G1 : G1 + 1, :] + r.vec[S1 : S1 + 1, :]
    r.nl[:rows] = normed.astype(BF)
    ff_out = None
    for c in range(chunks):
        cols = slice(c * chunk, (c + 1) * chunk)
        t = nn(r.nl[:rows], flat(r.we[..., cols])) + r.eb[:, cols]
        t2 = t * t
        th = jnp.tanh(t * (t2 * (GELU_A * GELU_C) + GELU_C))
        ht = 0.5 * t
        act = (ht * th + ht).astype(BF)
        r.act[:, cols] = act
        slope = (0.5 * th + 0.5) + ht * (1.0 - th * th) * (t2 * (3 * GELU_A * GELU_C) + GELU_C)
        r.slope[:, cols] = slope
        part_out = nn(act, flat(r.ws[c]))
        ff_out = part_out if ff_out is None else ff_out + part_out
    second = normed + (ff_out + r.vec[BS : BS + 1, :])
    xhat2, inv2 = norm_parts(second)
    row_at = part * rows + lax.broadcasted_iota(jnp.int32, (rows, width), 0)
    cot = jnp.where(row_at < r.lens[w], r.go[w, here, :].astype(F32), 0.0)
    r.go[w, here, :] = (xhat2 * r.vec[G2 : G2 + 1, :] + r.vec[S2 : S2 + 1, :]).astype(BF)
    add_row(r.gvec, G2, cot * xhat2)
    add_row(r.gvec, S2, cot)
    d_second = norm_back(cot * r.vec[G2 : G2 + 1, :], xhat2, inv2)
    gff = d_second.astype(BF)
    r.gff[:rows] = gff
    add_row(r.gvec, BS, gff.astype(F32))
    d_normed = d_second
    for c in range(chunks):
        cols = slice(c * chunk, (c + 1) * chunk)
        gpre = (nt(r.gff[:rows], flat(r.ws[c])) * r.slope[:, cols]).astype(BF)
        r.geb[:, cols] += jnp.sum(gpre.astype(F32), axis=0, keepdims=True)
        r.gws[c] += tn(r.act[:, cols], r.gff[:rows]).reshape(r.gws.shape[1:])
        r.gwe[..., cols] += tn(r.nl[:rows], gpre).reshape(r.gwe.shape[:-1] + (chunk,))
        d_normed = d_normed + nt(gpre, flat(r.we[..., cols]))
    xhat1 = r.xh1[:rows]
    add_row(r.gvec, G1, d_normed * xhat1)
    add_row(r.gvec, S1, d_normed)
    d_first = norm_back(d_normed * r.vec[G1 : G1 + 1, :], xhat1, inv1)
    r.dfirst[w, here, :] = d_first
    gattn = d_first.astype(BF)
    add_row(r.gvec, BM, gattn.astype(F32))
    mixed = r.mixed[w, here, :]
    add_into(r.gwm, tn(mixed, gattn))
    gmix = nt(gattn, flat(r.wm[...])).astype(BF)
    head = width // HEADS
    prod = gmix.astype(F32) * mixed.astype(F32)
    hi = prod.astype(BF)
    lo = (prod - hi.astype(F32)).astype(BF)
    sel_row = lax.broadcasted_iota(jnp.int32, (16, width), 0)
    sel_col = lax.broadcasted_iota(jnp.int32, (16, width), 1)
    sel = jnp.where(sel_col // head == sel_row, 1.0, 0.0).astype(BF)
    r.delta[w, :, here] = nt(sel, hi) + nt(sel, lo)
    r.mixed[w, here, :] = gmix


def attention_backward(w, r, hook):
    seq, width = r.x.shape[1:]
    half = seq // 2
    head = width // HEADS
    scale = head**-0.5
    make_mask(w, r)
    r.vt[...] = r.k[w].T
    lane = lax.broadcasted_iota(jnp.int32, (seq, 2 * head), 1)
    for p in range(HEADS // 2):
        if p == HEADS // 4:
            hook(w)
        pair = slice(p * 2 * head, (p + 1) * 2 * head)
        kp = r.k[w, :, pair]
        vp = r.v[w, :, pair]
        sums = None
        for odd in range(2):
            h = 2 * p + odd
            mine = (lane >= head) if odd else (lane < head)
            qh = jnp.where(mine, r.q[w, :, pair], jnp.zeros((), BF))
            gh = jnp.where(mine, r.mixed[w, :, pair], jnp.zeros((), BF))
            logt = r.logt[w, h : h + 1, :]
            delta = r.delta[w, h : h + 1, :]
            p0 = jnp.exp(nt(kp[:half], qh) + r.mask[:half, :] - logt)
            p1 = jnp.exp(nt(kp[half:], qh[half:]) + r.mask[half:, half:] - logt[:, half:])
            d0 = (p0 * (nt(vp[:half], gh) - delta)).astype(BF)
            d1 = (p1 * (nt(vp[half:], gh[half:]) - delta[:, half:])).astype(BF)
            p0 = p0.astype(BF)
            p1 = p1.astype(BF)
            parts = (nn(d0, qh), nn(d1, qh[half:]), nn(p0, gh), nn(p1, gh[half:]))
            sums = parts if sums is None else tuple(a + b for a, b in zip(sums, parts))
            kt = r.vt[h * head : (h + 1) * head, :]
            q_left = nn(kt[:, :half], d0[:, :half])
            q_right = nn(kt, jnp.concatenate([d0[:, half:], d1], axis=0))
            r.ot[h * head : (h + 1) * head, :half] = (q_left * scale).astype(BF)
            r.ot[h * head : (h + 1) * head, half:] = (q_right * scale).astype(BF)
        r.nl[:half, pair] = sums[0].astype(BF)
        r.nl[half:, pair] = sums[1].astype(BF)
        r.gff[:half, pair] = sums[2].astype(BF)
        r.gff[half:, pair] = sums[3].astype(BF)
    gq = r.ot[...].T
    gk = r.nl[...]
    gv = r.gff[...]
    low = r.low[w]
    add_into(r.gwq, tn(low, gq))
    add_into(r.gwk, tn(low, gk))
    add_into(r.gwv, tn(low, gv))
    add_row(r.gvec, BQ, gq.astype(F32))
    add_row(r.gvec, BV, gv.astype(F32))
    d_hidden = (
        r.dfirst[w]
        + nt(gq, flat(r.wq[...]))
        + nt(gk, flat(r.wk[...]))
        + nt(gv, flat(r.wv[...]))
    )
    r.gpos[...] += d_hidden
    r.x[w] = d_hidden.astype(BF)


def windows(count, body):
    def step(w, carry):
        body(w)
        return carry

    lax.fori_loop(0, count, step, 0)


def at_window(w, plan):
    for index, steps in plan:

        @pl.when(w == index)
        def _():
            for step in steps:
                step()


class Place:
    def __init__(self, dp_count, z_count):
        self.dp_count, self.z_count = dp_count, z_count
        self.dp = lax.axis_index("dp")
        fsdp = lax.axis_index("fsdp")
        self.z, self.c = fsdp // 2, lax.rem(fsdp, 2)
        self.near = (self.dp, self.z * 2 + (1 - self.c))

    def z_at(self, shift):
        return lax.rem(self.z + shift + self.z_count, self.z_count)

    def dp_flip(self, bit):
        low, high = lax.rem(self.dp, 2), self.dp // 2
        if bit in (0, 2):
            low = 1 - low
        if bit in (1, 2):
            high = 1 - high
        return high * 2 + low

    def along_z(self, shift):
        return (self.dp, self.z_at(shift) * 2 + self.c)

    def along_dp(self, bit):
        return (self.dp_flip(bit), self.z * 2 + self.c)

    def barrier(self):
        sem = pltpu.get_barrier_semaphore()
        everyone = [self.near] + [self.along_z(s) for s in range(1, self.z_count)]
        everyone += [self.along_dp(bit) for bit in range(3)]
        for peer in everyone:
            pl.semaphore_signal(sem, inc=1, device_id=peer, device_id_type=MESH)
        pl.semaphore_wait(sem, len(everyone))


def remote(src, dst, sems, index, peer):
    send, recv = sems
    return pltpu.make_async_remote_copy(
        src_ref=src, dst_ref=dst, send_sem=send.at[index], recv_sem=recv.at[index],
        device_id=peer, device_id_type=MESH,
    )


def hop_count(dp_count, z_count):
    return (z_count - 1) + 3 + 1


class Gather:
    def __init__(self, place, shard, whole, sems, first):
        self.p, self.shard, self.whole, self.sems = place, shard, whole, sems
        self.first, self.second = first, 1 - first
        self.base = place.z_count - 1

    def z_copy(self, shift, z):
        p = self.p
        return remote(self.shard, self.whole.at[p.dp, z, p.c], self.sems, shift - 1, p.along_z(shift))

    def dp_copy(self, slot, owner, bit):
        p = self.p
        block = self.whole.at[owner, :, p.c]
        return remote(block, block, self.sems, self.base + slot, p.along_dp(bit))

    def sent(self):
        p = self.p
        return [
            self.dp_copy(0, p.dp, self.first),
            self.dp_copy(1, p.dp, self.second),
            self.dp_copy(2, p.dp_flip(self.first), self.second),
        ]

    def taken(self):
        p = self.p
        return [
            self.dp_copy(0, p.dp_flip(self.first), self.first),
            self.dp_copy(1, p.dp_flip(self.second), self.second),
            self.dp_copy(2, p.dp_flip(2), self.second),
        ]

    def core_copy(self, core):
        half = self.whole.at[:, :, core]
        return remote(half, half, self.sems, self.base + 3, self.p.near)

    def start_z(self):
        p = self.p
        for shift in range(1, p.z_count):
            self.z_copy(shift, p.z).start()
        self.whole[p.dp, p.z, p.c] = self.shard[...]

    def start_dp(self):
        p = self.p
        for shift in range(1, p.z_count):
            self.z_copy(shift, p.z_at(-shift)).wait_recv()
        sent = self.sent()
        sent[0].start()
        sent[1].start()

    def pass_on(self):
        self.taken()[0].wait_recv()
        self.sent()[2].start()

    def start_core(self):
        taken = self.taken()
        taken[1].wait_recv()
        taken[2].wait_recv()
        self.core_copy(self.p.c).start()

    def finish(self):
        self.core_copy(1 - self.p.c).wait_recv()

    def drain(self):
        p = self.p
        for shift in range(1, p.z_count):
            self.z_copy(shift, p.z).wait_send()
        for copy in self.sent():
            copy.wait_send()
        self.core_copy(p.c).wait_send()


class Scatter:
    def __init__(self, place, total, result, bufs, sems, first):
        self.p, self.total, self.result, self.sems = place, total, result, sems
        self.out, self.from_core, self.from_dp, self.from_z = bufs
        self.first, self.second = first, 1 - first
        self.base = place.z_count - 1

    def core_copy(self):
        return remote(self.out, self.from_core, self.sems, self.base + 3, self.p.near)

    def dp_copies(self):
        p = self.p
        mine, other, far = (p.dp_flip(bit) for bit in (self.first, self.second, 2))
        return [
            remote(self.out.at[far], self.from_dp.at[0], self.sems, self.base, p.along_dp(self.first)),
            remote(self.out.at[mine], self.from_dp.at[1], self.sems, self.base + 1, p.along_dp(self.first)),
            remote(self.out.at[other], self.from_dp.at[2], self.sems, self.base + 2, p.along_dp(self.second)),
        ]

    def z_copy(self, shift):
        p = self.p
        block = self.out.at[p.dp, p.z_at(shift)]
        return remote(block, self.from_z.at[shift - 1], self.sems, shift - 1, p.along_z(shift))

    def blocks(self, body):
        p = self.p

        def step(at, carry):
            body(at // p.z_count, lax.rem(at, p.z_count))
            return carry

        lax.fori_loop(0, p.dp_count * p.z_count, step, 0)

    def start_core(self):
        far = 1 - self.p.c

        def body(d, z):
            self.out[d, z] = self.total[d, z, far].astype(BF)

        self.blocks(body)
        self.core_copy().start()

    def start_dp(self):
        c = self.p.c
        copy = self.core_copy()
        copy.wait_recv()
        copy.wait_send()

        def body(d, z):
            both = self.total[d, z, c] + self.from_core[d, z].astype(F32)
            self.total[d, z, c] = both
            self.out[d, z] = both.astype(BF)

        self.blocks(body)
        copies = self.dp_copies()
        copies[0].start()
        copies[1].start()

    def pass_on(self):
        p = self.p
        copies = self.dp_copies()
        copies[0].wait_recv()
        other = p.dp_flip(self.second)
        for z in range(p.z_count):
            added = self.total[other, z, p.c] + self.from_dp[0, z].astype(F32)
            self.out[other, z] = added.astype(BF)
        copies[2].start()

    def start_z(self):
        p = self.p
        copies = self.dp_copies()
        copies[1].wait_recv()
        copies[2].wait_recv()
        for z in range(p.z_count):
            added = self.total[p.dp, z, p.c] + self.from_dp[1, z].astype(F32) + self.from_dp[2, z].astype(F32)
            self.total[p.dp, z, p.c] = added
            self.out[p.dp, z] = added.astype(BF)
        for shift in range(1, p.z_count):
            self.z_copy(shift).start()

    def finish(self):
        p = self.p
        added = self.total[p.dp, p.z, p.c]
        for shift in range(1, p.z_count):
            self.z_copy(shift).wait_recv()
            added = added + self.from_z[shift - 1].astype(F32)
        self.result[...] = added

    def drain(self):
        for copy in self.dp_copies():
            copy.wait_send()
        for shift in range(1, self.p.z_count):
            self.z_copy(shift).wait_send()


class SumAll:
    def __init__(self, place, total, result, bufs, sems):
        self.p, self.total, self.result, self.sems = place, total, result, sems
        self.send_dp, self.send_z, self.landing = bufs

    def copies(self, hop):
        p = self.p
        base = p.z_count - 1
        if hop == 0:
            return [(base + 3, remote(self.total, self.landing.at[base + 3], self.sems, base + 3, p.near))]
        if hop == 1:
            return [
                (base + b, remote(self.send_dp, self.landing.at[base + b], self.sems, base + b, p.along_dp(b)))
                for b in range(3)
            ]
        return [
            (s - 1, remote(self.send_z, self.landing.at[s - 1], self.sems, s - 1, p.along_z(s)))
            for s in range(1, p.z_count)
        ]

    def arrived(self, hop, own):
        added = own[...]
        for slot, copy in self.copies(hop):
            copy.wait_recv()
            added = added + self.landing[slot]
        return added

    def start(self, hop):
        for _, copy in self.copies(hop):
            copy.start()

    def start_core(self):
        self.start(0)

    def start_dp(self):
        self.send_dp[...] = self.arrived(0, self.total)
        self.start(1)

    def pass_on(self):
        pass

    def start_z(self):
        self.send_z[...] = self.arrived(1, self.send_dp)
        self.start(2)

    def finish(self):
        self.result[...] = self.arrived(2, self.send_z)

    def drain(self):
        for hop in range(3):
            for _, copy in self.copies(hop):
                copy.wait_send()


WEIGHTS = ("wk", "wq", "wv", "wm", "we", "ws")
GRADS = ("gws", "gwe", "gwm", "gwq", "gwk", "gwv")
EARLY = ("post", "small", "wk", "wq", "wv")
LATE = ("wm", "we", "ws")
FIRST = dict(post=0, small=0, wk=1, wq=0, wv=1, wm=0, we=0, ws=1, gws=1, gwe=0, gwm=0, gwq=0, gwk=1, gwv=1, gpost=0)


def work_scratch(count, seq, width, ff):
    vm = pltpu.VMEM
    return dict(
        low=vm((count, seq, width), BF),
        q=vm((count, seq, width), BF),
        k=vm((count, seq, width), BF),
        v=vm((count, seq, width), BF),
        mixed=vm((count, seq, width), BF),
        dfirst=vm((count, seq, width), F32),
        logt=vm((count, HEADS, seq), F32),
        delta=vm((count, 16, seq), F32),
        vt=vm((width, seq), BF),
        ot=vm((width, seq), BF),
        mask=vm((seq, seq), F32),
        xh1=vm((seq // FF_PARTS, width), F32),
        nl=vm((seq, width), BF),
        gff=vm((seq, width), BF),
        act=vm((seq // FF_PARTS, ff), BF),
        slope=vm((seq // FF_PARTS, ff), F32),
        gpos=vm((seq, width), F32),
        x=vm((count, seq, width), BF),
        go=vm((count, seq, width), BF),
        io_sem=pltpu.SemaphoreType.DMA((4, count)),
    )


def zero_sums(r):
    for name in GRADS:
        ref = getattr(r, name)

        def step(at, carry):
            ref[at // ref.shape[1], lax.rem(at, ref.shape[1])] = jnp.zeros(ref.shape[2:], ref.dtype)
            return carry

        lax.fori_loop(0, ref.shape[0] * ref.shape[1], step, 0)
    for name in ("gpos", "gvec", "geb"):
        ref = getattr(r, name)
        ref[...] = jnp.zeros(ref.shape, ref.dtype)


def io_copies(r, count):
    def load(w):
        return (
            pltpu.make_async_copy(r.x_in.at[w], r.x.at[w], r.io_sem.at[0, w]),
            pltpu.make_async_copy(r.go_in.at[w], r.go.at[w], r.io_sem.at[1, w]),
        )

    def store_out(w):
        return pltpu.make_async_copy(r.go.at[w], r.out.at[w], r.io_sem.at[2, w])

    def store_gin(w):
        return pltpu.make_async_copy(r.x.at[w], r.gin.at[w], r.io_sem.at[3, w])

    return load, store_out, store_gin


def alone_kernel(names, *refs):
    r = Refs(**dict(zip(names, refs)))
    count = r.x.shape[0]
    load, store_out, store_gin = io_copies(r, count)
    for w in range(count):
        for copy in load(w):
            copy.start()
    zero_sums(r)
    for w in range(count):
        for copy in load(w):
            copy.wait()

    def second(w):
        windows(FF_PARTS, lambda part: feed_forward(w, part, r))
        store_out(w).start()

    def third(w):
        attention_backward(w, r, lambda w: None)
        store_gin(w).start()

    windows(count, lambda w: hidden_and_keys(w, r))
    windows(count, lambda w: attention_forward(w, r, lambda w: None))
    windows(count, second)
    windows(count, third)
    r.gpos_out[...] = r.gpos[...]
    for w in range(count):
        store_out(w).wait()
        store_gin(w).wait()


def vectors_from(r, dp_count, z_count, rows):
    devices = dp_count * z_count * 2
    per_row = LANES // rows
    ff_rows = r.eb.shape[1] // devices
    per_row_ff = LANES // ff_rows

    def block(d):
        return r.small[d // (2 * z_count), (d // 2) % z_count, d % 2].astype(F32)

    for g in range(devices // per_row):
        added = block(g * per_row)[:8]
        for d in range(g * per_row + 1, (g + 1) * per_row):
            added = added + block(d)[:8]
        r.vec[:, g * LANES : (g + 1) * LANES] = added
    for g in range(devices // per_row_ff):
        added = block(g * per_row_ff)[8:9]
        for d in range(g * per_row_ff + 1, (g + 1) * per_row_ff):
            added = added + block(d)[8:9]
        r.eb[:, g * LANES : (g + 1) * LANES] = added


def place_small(r, place):
    rows, ff_rows = r.eight.shape[1], r.one.shape[1]
    me = (place.dp * place.z_count + place.z) * 2 + place.c

    def spread(n):
        at = lax.rem(me, LANES // n) * n
        source = lax.broadcasted_iota(jnp.int32, (n, LANES), 0)
        target = lax.broadcasted_iota(jnp.int32, (n, LANES), 1)
        return jnp.where(target == source + at, 1.0, 0.0).astype(BF)

    r.small_shard[0:8, :] = nn(r.eight[...], spread(rows))
    r.small_shard[8:16, :] = jnp.broadcast_to(nn(r.one[...], spread(ff_rows))[:1], (8, LANES))


def whole_kernel(counts, names, *refs):
    r = Refs(**dict(zip(names, refs)))
    count = r.x.shape[0]
    rows = r.wq_shard.shape[0]
    place = Place(*counts)
    load, store_out, store_gin = io_copies(r, count)
    for w in range(count):
        for copy in load(w):
            copy.start()
    place_small(r, place)
    r.small_low[...] = r.small_shard[...].astype(BF)
    gathers = {}
    for name in EARLY + LATE:
        shard = r.small_low if name == "small" else getattr(r, name + "_shard")
        sems = (getattr(r, name + "_send"), getattr(r, name + "_recv"))
        gathers[name] = Gather(place, shard, getattr(r, name), sems, FIRST[name])
    early = [gathers[name] for name in EARLY]
    late = [gathers[name] for name in LATE]
    place.barrier()
    for job in early + late:
        job.start_z()
    zero_sums(r)
    for job in early:
        job.start_dp()
    for job in early:
        job.pass_on()
    for job in early:
        job.start_core()
    for job in late:
        job.start_dp()
    for job in early[:3]:
        job.finish()
    r.pos[...] = flat(r.post[...]).T
    vectors_from(r, counts[0], counts[1], rows)
    for w in range(count):
        for copy in load(w):
            copy.wait()
    windows(count, lambda w: hidden_and_keys(w, r))
    for job in early[3:]:
        job.finish()

    wm, we, ws = late
    first_plan = ((1, (wm.pass_on, we.pass_on)), (3, (ws.pass_on, wm.start_core)))
    first_mid = ()

    def first_body(w):
        at_window(w, first_plan)
        attention_forward(w, r, lambda at: at_window(at, first_mid))

    windows(count, first_body)
    we.start_core()
    ws.start_core()
    for job in late:
        job.finish()

    def second_body(w):
        windows(FF_PARTS, lambda part: feed_forward(w, part, r))
        store_out(w).start()

    windows(count, second_body)

    scatters = {}
    for name in GRADS + ("gpost",):
        total = r.gpost_sum if name == "gpost" else getattr(r, name)
        bufs = [getattr(r, name + tail) for tail in ("_out", "_core", "_dp", "_z")]
        sems = (getattr(r, name + "_send"), getattr(r, name + "_recv"))
        scatters[name] = Scatter(place, total, getattr(r, name + "_result"), bufs, sems, FIRST[name])
    sums = SumAll(
        place, r.gsmall, r.gsmall_result, (r.gsmall_dp, r.gsmall_z, r.gsmall_in), (r.gsmall_send, r.gsmall_recv)
    )
    gws, gwe, gwm = (scatters[name] for name in ("gws", "gwe", "gwm"))
    last = [scatters[name] for name in ("gwq", "gwk", "gwv", "gpost")]
    gws.start_core()
    gwe.start_core()
    gwm.start_core()
    third_plan = ((1, (gwe.start_dp, gwm.start_dp)), (3, (gwe.pass_on, gwm.pass_on)))
    third_mid = ((0, (gws.start_dp,)), (2, (gws.pass_on,)), (3, (gws.start_z,)))

    def third_body(w):
        at_window(w, third_plan)
        attention_backward(w, r, lambda at: at_window(at, third_mid))
        store_gin(w).start()

    windows(count, third_body)
    for job in last[:3]:
        job.start_core()
    add_blocks = r.gpos[...].T
    r.gpost_sum[...] = add_blocks.reshape(r.gpost_sum.shape)
    last[3].start_core()
    ff_rows = r.geb.shape[1] // r.gvec.shape[1]
    width = r.gvec.shape[1]
    r.gsmall[0:8, :] = r.gvec[...]
    r.gsmall[8:16, :] = jnp.zeros((8, width), F32)
    for i in range(ff_rows):
        r.gsmall[8 + i : 9 + i, :] = r.geb[:, i * width : (i + 1) * width]
    sums.start_core()
    last = last + [sums]
    for job in last:
        job.start_dp()
    gwe.start_z()
    gwm.start_z()
    for job in last:
        job.pass_on()
    for job in last:
        job.start_z()
    everyone = [gws, gwe, gwm] + last
    for job in everyone:
        job.finish()
    for job in early + late + everyone:
        job.drain()
    for w in range(count):
        store_out(w).wait()
        store_gin(w).wait()


def unpack_kernel(counts, names, *refs):
    r = Refs(**dict(zip(names, refs)))
    copies = [
        pltpu.make_async_copy(getattr(r, name + "_in"), getattr(r, name), r.sem.at[i])
        for i, name in enumerate(("out", "gin"))
    ]
    for copy in copies:
        copy.start()
    for name in GRADS:
        getattr(r, name)[...] = getattr(r, name + "_in")[...]
    r.gpos[...] = r.gpost_in[...].T
    place = Place(*counts)
    me = (place.dp * place.z_count + place.z) * 2 + place.c
    rows, ff_rows = r.gvec.shape[1], r.geb.shape[1]
    width = r.gsmall_in.shape[1]
    turned = pltpu.roll(r.gsmall_in[0:8, :], width - me * rows, axis=1)
    r.gvec[...] = turned[:, :rows]
    start = me * ff_rows
    lines = r.gsmall_in[8:16, :]
    line_at = lax.broadcasted_iota(jnp.int32, (8, width), 0)
    line = jnp.sum(jnp.where(line_at == start // width, lines, 0.0), axis=0, keepdims=True)
    line = jnp.broadcast_to(line, (8, width))
    r.geb[...] = pltpu.roll(line, width - lax.rem(start, width), axis=1)[0:1, :ff_rows]
    for copy in copies:
        copy.wait()


def call(kernel, name, ins, outs, scratch, **params):
    names = tuple(ins) + tuple(outs) + tuple(scratch)
    spec = lambda space: pl.BlockSpec(memory_space=space)
    results = pl.pallas_call(
        functools.partial(kernel, names),
        out_shape=tuple(shape for shape, _ in outs.values()),
        in_specs=[spec(space) for _, space in ins.values()],
        out_specs=tuple(spec(space) for _, space in outs.values()),
        scratch_shapes=list(scratch.values()),
        compiler_params=pltpu.CompilerParams(vmem_limit_bytes=63 * 2**20, **params),
        name=name,
    )(*[value for value, _ in ins.values()])
    return dict(zip(outs, results))


def local(dp_count, fsdp_count, inputs, lengths, grad_out, *params):
    micro, per_micro, seq, width = inputs.shape
    count = micro * per_micro
    wq, wk, wv, wm, we, ws, pos = params[:7]
    bq, bv, bm, eb, bs, g1, s1, g2, s2 = params[7:]
    ff = we.shape[1]
    rows, ff_rows = wq.shape[0], ws.shape[0]
    vectors = (bq, bv, bm, bs, g1, s1, g2, s2)
    vm, hbm = pltpu.VMEM, pl.ANY
    shape_of = jax.ShapeDtypeStruct
    merged = lambda a: a.reshape((count,) + a.shape[2:])
    act = shape_of((count, seq, width), BF)
    data = dict(
        lens=(lengths.reshape(count), pltpu.SMEM), x_in=(merged(inputs), hbm), go_in=(merged(grad_out), hbm)
    )
    scratch = work_scratch(count, seq, width, ff)
    if dp_count == 4 and fsdp_count % 2 == 0 and rows % 16 == 0 and LANES % rows == 0 and LANES % ff_rows == 0:
        counts = (dp_count, fsdp_count // 2)
        lead = (dp_count, fsdp_count // 2, 2)
        shards = dict(wq=wq, wk=wk, wv=wv, wm=wm, we=we, ws=ws, post=pos.T)
        ins = dict(data)
        for name, shard in shards.items():
            ins[name + "_shard"] = (shard, vm)
        ins["eight"] = (jnp.stack(vectors), vm)
        ins["one"] = (jnp.broadcast_to(eb[None], (8, ff_rows)), vm)
        outs = dict(out=(act, hbm), gin=(act, hbm))
        results = dict(gwq=wq, gwk=wk, gwv=wv, gwm=wm, gwe=we, gws=ws, gpost=pos.T)
        for name, like in results.items():
            outs[name + "_result"] = (shape_of(like.shape, F32), vm)
        outs["gsmall_result"] = (shape_of((16, width), F32), vm)
        hops = hop_count(*counts)
        pair = lambda name: {name + tail: pltpu.SemaphoreType.DMA((hops,)) for tail in ("_send", "_recv")}
        for name, shard in shards.items():
            scratch[name] = vm(lead + shard.shape, BF)
            scratch.update(pair(name))
        scratch["small"] = vm(lead + (16, LANES), BF)
        scratch["small_shard"] = vm((16, LANES), F32)
        scratch["small_low"] = vm((16, LANES), BF)
        scratch["pos"] = vm((seq, width), BF)
        scratch["vec"] = vm((8, width), F32)
        scratch["eb"] = vm((1, ff), F32)
        scratch["gvec"] = vm((8, width), F32)
        scratch["geb"] = vm((1, ff), F32)
        scratch.update(pair("small"))
        scratch.update(pair("gsmall"))
        for name, like in results.items():
            scratch["gpost_sum" if name == "gpost" else name] = vm(lead + like.shape, F32)
            scratch[name + "_out"] = vm(lead[:2] + like.shape, BF)
            scratch[name + "_core"] = vm(lead[:2] + like.shape, BF)
            scratch[name + "_dp"] = vm((3,) + lead[1:2] + like.shape, BF)
            scratch[name + "_z"] = vm((lead[1] - 1,) + like.shape, BF)
            scratch.update(pair(name))
        for tail in ("", "_dp", "_z"):
            scratch["gsmall" + tail] = vm((16, width), F32)
        scratch["gsmall_in"] = vm((hops, 16, width), F32)
        got = call(
            functools.partial(whole_kernel, counts), "layer", ins, outs, scratch,
            collective_id=0, has_side_effects=True,
        )
        ins = {}
        for name in ("out", "gin"):
            ins[name + "_in"] = (got[name], hbm)
        for name in GRADS + ("gpost", "gsmall"):
            ins[name + "_in"] = (got[name + "_result"], vm)
        outs = dict(out=(act, hbm), gin=(act, hbm))
        for name in GRADS:
            outs[name] = (shape_of(results[name].shape, F32), vm)
        outs["gpos"] = (shape_of(pos.shape, F32), vm)
        outs["gvec"] = (shape_of((8, rows), F32), vm)
        outs["geb"] = (shape_of((1, ff_rows), F32), vm)
        got = call(
            functools.partial(unpack_kernel, counts), "unpack", ins, outs, dict(sem=pltpu.SemaphoreType.DMA((2,)))
        )
        gvec, geb, gpos = got["gvec"], got["geb"][0], got["gpos"]
        grads = got
    else:
        lead = (4, 4, 2)
        cut = lambda a: a.reshape(lead + (-1, a.shape[-1]))
        gather = lambda a, axis=0: lax.all_gather(a, AXES, axis=axis, tiled=True)
        share = lambda a, axis=0: lax.psum_scatter(a, AXES, scatter_dimension=axis, tiled=True)
        ins = dict(data)
        for name, shard in dict(wq=wq, wk=wk, wv=wv, wm=wm, we=we, ws=ws).items():
            ins[name] = (cut(gather(shard)), vm)
        ins["pos"] = (gather(pos, 1), vm)
        ins["vec"] = (jnp.stack([gather(a).astype(F32) for a in vectors]), vm)
        ins["eb"] = (gather(eb).astype(F32)[None], vm)
        outs = dict(out=(act, hbm), gin=(act, hbm))
        for name in GRADS:
            outs[name] = (shape_of(ins["w" + name[2:]][0].shape, F32), vm)
        outs["gpos_out"] = (shape_of((seq, width), F32), vm)
        outs["gvec"] = (shape_of((8, width), F32), vm)
        outs["geb"] = (shape_of((1, ff), F32), vm)
        got = call(alone_kernel, "layer_alone", ins, outs, scratch)
        grads = {name: share(flat(got[name])) for name in GRADS}
        gpos = share(got["gpos_out"], 1)
        gvec = [share(got["gvec"][i]) for i in range(8)]
        geb = share(got["geb"][0])
    gbq, gbv, gbm, gbs, gg1, gs1, gg2, gs2 = (gvec[i] for i in range(8))
    return (
        got["out"].reshape(inputs.shape), got["gin"].reshape(inputs.shape),
        grads["gwq"], grads["gwk"], grads["gwv"], grads["gwm"], grads["gwe"], grads["gws"], gpos,
        gbq, gbv, gbm, geb, gbs, gg1, gs1, gg2, gs2,
    )


def solution(mesh):
    batch = P(None, AXES, None, None)
    matrix, vector, table = P(AXES, None), P(AXES), P(None, AXES)
    weights = (matrix,) * 6 + (table,) + (vector,) * 9
    return jax.shard_map(
        functools.partial(local, mesh.shape["dp"], mesh.shape["fsdp"]),
        mesh=mesh,
        in_specs=(batch, P(None, AXES), batch) + weights,
        out_specs=(batch, batch) + weights,
        check_vma=False,
    )
```

```python
import functools

import jax
import jax.numpy as jnp
from jax import lax
from jax.experimental import pallas as pl
from jax.experimental.pallas import tpu as pltpu
from jax.sharding import PartitionSpec as P

HEADS = 8
EPS = 1e-05
BF = jnp.bfloat16
F32 = jnp.float32
GELU_C = 0.7978845608028654
GELU_A = 0.044715
AXES = ("dp", "fsdp")
LANES = 128
MESH = pl.DeviceIdType.MESH
FF_PARTS = 2

(BQ, BV, BM, BS, G1, S1, G2, S2) = range(8)


class Refs:
    def __init__(self, **kw):
        self.__dict__.update(kw)


def nn(a, b):
    return lax.dot_general(a, b, (((1,), (0,)), ((), ())), preferred_element_type=F32)


def nt(a, b):
    return lax.dot_general(a, b, (((1,), (1,)), ((), ())), preferred_element_type=F32)


def tn(a, b):
    return lax.dot_general(a, b, (((0,), (0,)), ((), ())), preferred_element_type=F32)


def flat(value):
    return value.reshape(-1, value.shape[-1])


def add_into(ref, value):
    ref[...] += value.reshape(ref.shape)


def add_row(ref, index, value):
    ref[index : index + 1, :] += jnp.sum(value, axis=0, keepdims=True)


def length_of(w, r):
    per_micro = r.lens.shape[1]
    return r.lens[w // per_micro, lax.rem(w, per_micro)]


def make_mask(w, r):
    seq = r.x.shape[1]
    key_at = lax.broadcasted_iota(jnp.int32, (seq, seq), 0)
    query_at = lax.broadcasted_iota(jnp.int32, (seq, seq), 1)
    ok = (key_at <= query_at) & (key_at < length_of(w, r))
    r.mask[...] = jnp.where(ok, 0.0, -1e30)


def hidden_and_keys(w, r):
    low = (r.x[w].astype(F32) + r.pos[...].astype(F32)).astype(BF)
    r.low[w] = low
    r.k[w] = nn(low, flat(r.wk[...])).astype(BF)


def attention_forward(w, r, hook):
    seq, width = r.x.shape[1:]
    half = seq // 2
    head = width // HEADS
    low = r.low[w]
    queries = (nn(low, flat(r.wq[...])) + r.vec[BQ : BQ + 1, :]).astype(BF)
    r.q[w] = (queries.astype(F32) * (head**-0.5)).astype(BF)
    values = (nn(low, flat(r.wv[...])) + r.vec[BV : BV + 1, :]).astype(BF)
    r.v[w] = values
    r.vt[...] = values.T
    make_mask(w, r)
    lane = lax.broadcasted_iota(jnp.int32, (seq, 2 * head), 1)
    for h in range(HEADS):
        if h == HEADS // 2:
            hook(w)
        pair = slice((h // 2) * 2 * head, (h // 2 + 1) * 2 * head)
        mine = (lane < head) if h % 2 == 0 else (lane >= head)
        qh = jnp.where(mine, r.q[w, :, pair], jnp.zeros((), BF))
        kp = r.k[w, :, pair]
        s0 = nt(kp[:half], qh) + r.mask[:half, :]
        s1 = nt(kp[half:], qh[half:]) + r.mask[half:, half:]
        m_left = jnp.max(s0[:, :half], axis=0, keepdims=True)
        m_right = jnp.maximum(
            jnp.max(s0[:, half:], axis=0, keepdims=True), jnp.max(s1, axis=0, keepdims=True)
        )
        top = jnp.concatenate([m_left, m_right], axis=1)
        e0 = jnp.exp(s0 - top)
        e1 = jnp.exp(s1 - m_right)
        n_all = jnp.sum(e0, axis=0, keepdims=True)
        n_right = n_all[:, half:] + jnp.sum(e1, axis=0, keepdims=True)
        total = jnp.concatenate([n_all[:, :half], n_right], axis=1)
        r.logt[w, h : h + 1, :] = top + jnp.log(total)
        inv = 1.0 / total
        p0 = (e0 * inv).astype(BF)
        p1 = (e1 * inv[:, half:]).astype(BF)
        vt = r.vt[h * head : (h + 1) * head, :]
        o_left = nn(vt[:, :half], p0[:, :half])
        o_right = nn(vt, jnp.concatenate([p0[:, half:], p1], axis=0))
        r.ot[h * head : (h + 1) * head, :half] = o_left.astype(BF)
        r.ot[h * head : (h + 1) * head, half:] = o_right.astype(BF)
    r.mixed[w] = r.ot[...].T


def norm_parts(total):
    center = total - jnp.mean(total, -1, keepdims=True)
    spread = jnp.mean(center * center, -1, keepdims=True)
    inv = lax.rsqrt(spread + EPS)
    return center * inv, inv


def norm_back(e, xhat, inv):
    return inv * (
        e - jnp.mean(e, -1, keepdims=True) - xhat * jnp.mean(e * xhat, -1, keepdims=True)
    )


def feed_forward(w, part, r):
    rows, width = r.nl.shape[0] // FF_PARTS, r.x.shape[-1]
    here = pl.ds(pl.multiple_of(part * rows, rows), rows)
    chunks = r.ws.shape[0]
    chunk = r.we.shape[-1] // chunks
    hid = r.x[w, here, :].astype(F32) + r.pos[here, :].astype(F32)
    first = hid + (nn(r.mixed[w, here, :], flat(r.wm[...])) + r.vec[BM : BM + 1, :])
    xhat1, inv1 = norm_parts(first)
    r.xh1[:rows] = xhat1
    normed = xhat1 * r.vec[G1 : G1 + 1, :] + r.vec[S1 : S1 + 1, :]
    r.nl[:rows] = normed.astype(BF)
    ff_out = None
    for c in range(chunks):
        cols = slice(c * chunk, (c + 1) * chunk)
        t = nn(r.nl[:rows], flat(r.we[..., cols])) + r.eb[:, cols]
        t2 = t * t
        th = jnp.tanh(t * (t2 * (GELU_A * GELU_C) + GELU_C))
        ht = 0.5 * t
        act = (ht * th + ht).astype(BF)
        r.act[:, cols] = act
        slope = (0.5 * th + 0.5) + ht * (1.0 - th * th) * (t2 * (3 * GELU_A * GELU_C) + GELU_C)
        r.slope[:, cols] = slope
        part_out = nn(act, flat(r.ws[c]))
        ff_out = part_out if ff_out is None else ff_out + part_out
    second = normed + (ff_out + r.vec[BS : BS + 1, :])
    xhat2, inv2 = norm_parts(second)
    row_at = part * rows + lax.broadcasted_iota(jnp.int32, (rows, width), 0)
    cot = jnp.where(row_at < length_of(w, r), r.go[w, here, :].astype(F32), 0.0)
    r.go[w, here, :] = (xhat2 * r.vec[G2 : G2 + 1, :] + r.vec[S2 : S2 + 1, :]).astype(BF)
    add_row(r.gvec, G2, cot * xhat2)
    add_row(r.gvec, S2, cot)
    d_second = norm_back(cot * r.vec[G2 : G2 + 1, :], xhat2, inv2)
    gff = d_second.astype(BF)
    r.gff[:rows] = gff
    add_row(r.gvec, BS, gff.astype(F32))
    d_normed = d_second
    for c in range(chunks):
        cols = slice(c * chunk, (c + 1) * chunk)
        gpre = (nt(r.gff[:rows], flat(r.ws[c])) * r.slope[:, cols]).astype(BF)
        r.geb[:, cols] += jnp.sum(gpre.astype(F32), axis=0, keepdims=True)
        r.gws[c] += tn(r.act[:, cols], r.gff[:rows]).reshape(r.gws.shape[1:])
        r.gwe[..., cols] += tn(r.nl[:rows], gpre).reshape(r.gwe.shape[:-1] + (chunk,))
        d_normed = d_normed + nt(gpre, flat(r.we[..., cols]))
    xhat1 = r.xh1[:rows]
    add_row(r.gvec, G1, d_normed * xhat1)
    add_row(r.gvec, S1, d_normed)
    d_first = norm_back(d_normed * r.vec[G1 : G1 + 1, :], xhat1, inv1)
    r.dfirst[w, here, :] = d_first
    gattn = d_first.astype(BF)
    add_row(r.gvec, BM, gattn.astype(F32))
    mixed = r.mixed[w, here, :]
    add_into(r.gwm, tn(mixed, gattn))
    gmix = nt(gattn, flat(r.wm[...])).astype(BF)
    head = width // HEADS
    prod = gmix.astype(F32) * mixed.astype(F32)
    hi = prod.astype(BF)
    lo = (prod - hi.astype(F32)).astype(BF)
    sel_row = lax.broadcasted_iota(jnp.int32, (16, width), 0)
    sel_col = lax.broadcasted_iota(jnp.int32, (16, width), 1)
    sel = jnp.where(sel_col // head == sel_row, 1.0, 0.0).astype(BF)
    r.delta[w, :, here] = nt(sel, hi) + nt(sel, lo)
    r.mixed[w, here, :] = gmix


def attention_backward(w, r, hook):
    seq, width = r.x.shape[1:]
    half = seq // 2
    head = width // HEADS
    scale = head**-0.5
    make_mask(w, r)
    r.vt[...] = r.k[w].T
    lane = lax.broadcasted_iota(jnp.int32, (seq, 2 * head), 1)
    for p in range(HEADS // 2):
        if p == HEADS // 4:
            hook(w)
        pair = slice(p * 2 * head, (p + 1) * 2 * head)
        kp = r.k[w, :, pair]
        vp = r.v[w, :, pair]
        sums = None
        for odd in range(2):
            h = 2 * p + odd
            mine = (lane >= head) if odd else (lane < head)
            qh = jnp.where(mine, r.q[w, :, pair], jnp.zeros((), BF))
            gh = jnp.where(mine, r.mixed[w, :, pair], jnp.zeros((), BF))
            logt = r.logt[w, h : h + 1, :]
            delta = r.delta[w, h : h + 1, :]
            p0 = jnp.exp(nt(kp[:half], qh) + r.mask[:half, :] - logt)
            p1 = jnp.exp(nt(kp[half:], qh[half:]) + r.mask[half:, half:] - logt[:, half:])
            d0 = (p0 * (nt(vp[:half], gh) - delta)).astype(BF)
            d1 = (p1 * (nt(vp[half:], gh[half:]) - delta[:, half:])).astype(BF)
            p0 = p0.astype(BF)
            p1 = p1.astype(BF)
            parts = (nn(d0, qh), nn(d1, qh[half:]), nn(p0, gh), nn(p1, gh[half:]))
            sums = parts if sums is None else tuple(a + b for a, b in zip(sums, parts))
            kt = r.vt[h * head : (h + 1) * head, :]
            q_left = nn(kt[:, :half], d0[:, :half])
            q_right = nn(kt, jnp.concatenate([d0[:, half:], d1], axis=0))
            r.ot[h * head : (h + 1) * head, :half] = (q_left * scale).astype(BF)
            r.ot[h * head : (h + 1) * head, half:] = (q_right * scale).astype(BF)
        r.nl[:half, pair] = sums[0].astype(BF)
        r.nl[half:, pair] = sums[1].astype(BF)
        r.gff[:half, pair] = sums[2].astype(BF)
        r.gff[half:, pair] = sums[3].astype(BF)
    gq = r.ot[...].T
    gk = r.nl[...]
    gv = r.gff[...]
    low = r.low[w]
    add_into(r.gwq, tn(low, gq))
    add_into(r.gwk, tn(low, gk))
    add_into(r.gwv, tn(low, gv))
    add_row(r.gvec, BQ, gq.astype(F32))
    add_row(r.gvec, BV, gv.astype(F32))
    d_hidden = (
        r.dfirst[w]
        + nt(gq, flat(r.wq[...]))
        + nt(gk, flat(r.wk[...]))
        + nt(gv, flat(r.wv[...]))
    )
    r.gpos[...] += d_hidden
    r.x[w] = d_hidden.astype(BF)


def windows(count, body):
    def step(w, carry):
        body(w)
        return carry

    lax.fori_loop(0, count, step, 0)


def at_window(w, plan):
    for index, steps in plan:

        @pl.when(w == index)
        def _():
            for step in steps:
                step()


class Place:
    def __init__(self, dp_count, z_count):
        self.dp_count, self.z_count = dp_count, z_count
        self.dp = lax.axis_index("dp")
        fsdp = lax.axis_index("fsdp")
        self.z, self.c = fsdp // 2, lax.rem(fsdp, 2)
        self.near = (self.dp, self.z * 2 + (1 - self.c))

    def z_at(self, shift):
        return lax.rem(self.z + shift + self.z_count, self.z_count)

    def dp_flip(self, bit):
        low, high = lax.rem(self.dp, 2), self.dp // 2
        if bit in (0, 2):
            low = 1 - low
        if bit in (1, 2):
            high = 1 - high
        return high * 2 + low

    def along_z(self, shift):
        return (self.dp, self.z_at(shift) * 2 + self.c)

    def along_dp(self, bit):
        return (self.dp_flip(bit), self.z * 2 + self.c)

    def barrier(self):
        sem = pltpu.get_barrier_semaphore()
        everyone = [self.near] + [self.along_z(s) for s in range(1, self.z_count)]
        everyone += [self.along_dp(bit) for bit in range(3)]
        for peer in everyone:
            pl.semaphore_signal(sem, inc=1, device_id=peer, device_id_type=MESH)
        pl.semaphore_wait(sem, len(everyone))


def remote(src, dst, sems, index, peer):
    send, recv = sems
    return pltpu.make_async_remote_copy(
        src_ref=src, dst_ref=dst, send_sem=send.at[index], recv_sem=recv.at[index],
        device_id=peer, device_id_type=MESH,
    )


def hop_count(dp_count, z_count):
    return (z_count - 1) + 3 + 1


class Gather:
    def __init__(self, place, shard, whole, sems, first):
        self.p, self.shard, self.whole, self.sems = place, shard, whole, sems
        self.first, self.second = first, 1 - first
        self.base = place.z_count - 1

    def z_copy(self, shift, z):
        p = self.p
        return remote(self.shard, self.whole.at[p.dp, z, p.c], self.sems, shift - 1, p.along_z(shift))

    def dp_copy(self, slot, owner, bit):
        p = self.p
        block = self.whole.at[owner, :, p.c]
        return remote(block, block, self.sems, self.base + slot, p.along_dp(bit))

    def sent(self):
        p = self.p
        return [
            self.dp_copy(0, p.dp, self.first),
            self.dp_copy(1, p.dp, self.second),
            self.dp_copy(2, p.dp_flip(self.first), self.second),
        ]

    def taken(self):
        p = self.p
        return [
            self.dp_copy(0, p.dp_flip(self.first), self.first),
            self.dp_copy(1, p.dp_flip(self.second), self.second),
            self.dp_copy(2, p.dp_flip(2), self.second),
        ]

    def core_copy(self, core):
        half = self.whole.at[:, :, core]
        return remote(half, half, self.sems, self.base + 3, self.p.near)

    def start_z(self):
        p = self.p
        for shift in range(1, p.z_count):
            self.z_copy(shift, p.z).start()
        self.whole[p.dp, p.z, p.c] = self.shard[...]

    def start_dp(self):
        p = self.p
        for shift in range(1, p.z_count):
            self.z_copy(shift, p.z_at(-shift)).wait_recv()
        sent = self.sent()
        sent[0].start()
        sent[1].start()

    def pass_on(self):
        self.taken()[0].wait_recv()
        self.sent()[2].start()

    def start_core(self):
        taken = self.taken()
        taken[1].wait_recv()
        taken[2].wait_recv()
        self.core_copy(self.p.c).start()

    def finish(self):
        self.core_copy(1 - self.p.c).wait_recv()

    def drain(self):
        p = self.p
        for shift in range(1, p.z_count):
            self.z_copy(shift, p.z).wait_send()
        for copy in self.sent():
            copy.wait_send()
        self.core_copy(p.c).wait_send()


class Scatter:
    def __init__(self, place, total, result, bufs, sems, first):
        self.p, self.total, self.result, self.sems = place, total, result, sems
        self.out, self.from_core, self.from_dp, self.from_z = bufs
        self.first, self.second = first, 1 - first
        self.base = place.z_count - 1

    def core_copy(self):
        return remote(self.out, self.from_core, self.sems, self.base + 3, self.p.near)

    def dp_copies(self):
        p = self.p
        mine, other, far = (p.dp_flip(bit) for bit in (self.first, self.second, 2))
        return [
            remote(self.out.at[far], self.from_dp.at[0], self.sems, self.base, p.along_dp(self.first)),
            remote(self.out.at[mine], self.from_dp.at[1], self.sems, self.base + 1, p.along_dp(self.first)),
            remote(self.out.at[other], self.from_dp.at[2], self.sems, self.base + 2, p.along_dp(self.second)),
        ]

    def z_copy(self, shift):
        p = self.p
        block = self.out.at[p.dp, p.z_at(shift)]
        return remote(block, self.from_z.at[shift - 1], self.sems, shift - 1, p.along_z(shift))

    def blocks(self, body):
        p = self.p

        def step(at, carry):
            body(at // p.z_count, lax.rem(at, p.z_count))
            return carry

        lax.fori_loop(0, p.dp_count * p.z_count, step, 0)

    def start_core(self):
        far = 1 - self.p.c

        def body(d, z):
            self.out[d, z] = self.total[d, z, far].astype(BF)

        self.blocks(body)
        self.core_copy().start()

    def start_dp(self):
        c = self.p.c
        copy = self.core_copy()
        copy.wait_recv()
        copy.wait_send()

        def body(d, z):
            both = self.total[d, z, c] + self.from_core[d, z].astype(F32)
            self.total[d, z, c] = both
            self.out[d, z] = both.astype(BF)

        self.blocks(body)
        copies = self.dp_copies()
        copies[0].start()
        copies[1].start()

    def pass_on(self):
        p = self.p
        copies = self.dp_copies()
        copies[0].wait_recv()
        other = p.dp_flip(self.second)
        for z in range(p.z_count):
            added = self.total[other, z, p.c] + self.from_dp[0, z].astype(F32)
            self.out[other, z] = added.astype(BF)
        copies[2].start()

    def start_z(self):
        p = self.p
        copies = self.dp_copies()
        copies[1].wait_recv()
        copies[2].wait_recv()
        for z in range(p.z_count):
            added = self.total[p.dp, z, p.c] + self.from_dp[1, z].astype(F32) + self.from_dp[2, z].astype(F32)
            self.total[p.dp, z, p.c] = added
            self.out[p.dp, z] = added.astype(BF)
        for shift in range(1, p.z_count):
            self.z_copy(shift).start()

    def finish(self):
        p = self.p
        added = self.total[p.dp, p.z, p.c]
        for shift in range(1, p.z_count):
            self.z_copy(shift).wait_recv()
            added = added + self.from_z[shift - 1].astype(F32)
        self.result[...] = added

    def drain(self):
        for copy in self.dp_copies():
            copy.wait_send()
        for shift in range(1, self.p.z_count):
            self.z_copy(shift).wait_send()


class SumAll:
    def __init__(self, place, total, result, bufs, sems):
        self.p, self.total, self.result, self.sems = place, total, result, sems
        self.send_dp, self.send_z, self.landing = bufs

    def copies(self, hop):
        p = self.p
        base = p.z_count - 1
        if hop == 0:
            return [(base + 3, remote(self.total, self.landing.at[base + 3], self.sems, base + 3, p.near))]
        if hop == 1:
            return [
                (base + b, remote(self.send_dp, self.landing.at[base + b], self.sems, base + b, p.along_dp(b)))
                for b in range(3)
            ]
        return [
            (s - 1, remote(self.send_z, self.landing.at[s - 1], self.sems, s - 1, p.along_z(s)))
            for s in range(1, p.z_count)
        ]

    def arrived(self, hop, own):
        added = own[...]
        for slot, copy in self.copies(hop):
            copy.wait_recv()
            added = added + self.landing[slot]
        return added

    def start(self, hop):
        for _, copy in self.copies(hop):
            copy.start()

    def start_core(self):
        self.start(0)

    def start_dp(self):
        self.send_dp[...] = self.arrived(0, self.total)
        self.start(1)

    def pass_on(self):
        pass

    def start_z(self):
        self.send_z[...] = self.arrived(1, self.send_dp)
        self.start(2)

    def finish(self):
        self.result[...] = self.arrived(2, self.send_z)

    def drain(self):
        for hop in range(3):
            for _, copy in self.copies(hop):
                copy.wait_send()


WEIGHTS = ("wk", "wq", "wv", "wm", "we", "ws")
GRADS = ("gws", "gwe", "gwm", "gwq", "gwk", "gwv")
EARLY = ("post", "small", "wk", "wq", "wv")
LATE = ("wm", "we", "ws")
FIRST = dict(post=0, small=0, wk=1, wq=0, wv=1, wm=0, we=0, ws=1, gws=1, gwe=0, gwm=0, gwq=0, gwk=1, gwv=1, gpost=0)


def work_scratch(count, seq, width, ff):
    vm = pltpu.VMEM
    return dict(
        low=vm((count, seq, width), BF),
        q=vm((count, seq, width), BF),
        k=vm((count, seq, width), BF),
        v=vm((count, seq, width), BF),
        mixed=vm((count, seq, width), BF),
        dfirst=vm((count, seq, width), F32),
        logt=vm((count, HEADS, seq), F32),
        delta=vm((count, 16, seq), F32),
        vt=vm((width, seq), BF),
        ot=vm((width, seq), BF),
        mask=vm((seq, seq), F32),
        xh1=vm((seq // FF_PARTS, width), F32),
        nl=vm((seq, width), BF),
        gff=vm((seq, width), BF),
        act=vm((seq // FF_PARTS, ff), BF),
        slope=vm((seq // FF_PARTS, ff), F32),
        gpos=vm((seq, width), F32),
        x=vm((count, seq, width), BF),
        go=vm((count, seq, width), BF),
        io_sem=pltpu.SemaphoreType.DMA((4, count)),
    )


def zero_sums(r):
    for name in GRADS:
        ref = getattr(r, name)

        def step(at, carry):
            ref[at // ref.shape[1], lax.rem(at, ref.shape[1])] = jnp.zeros(ref.shape[2:], ref.dtype)
            return carry

        lax.fori_loop(0, ref.shape[0] * ref.shape[1], step, 0)
    for name in ("gpos", "gvec", "geb"):
        ref = getattr(r, name)
        ref[...] = jnp.zeros(ref.shape, ref.dtype)


def io_copies(r, count):
    def load(w):
        return (
            pltpu.make_async_copy(r.x_in.at[w], r.x.at[w], r.io_sem.at[0, w]),
            pltpu.make_async_copy(r.go_in.at[w], r.go.at[w], r.io_sem.at[1, w]),
        )

    def store_out(w):
        return pltpu.make_async_copy(r.go.at[w], r.out.at[w], r.io_sem.at[2, w])

    def store_gin(w):
        return pltpu.make_async_copy(r.x.at[w], r.gin.at[w], r.io_sem.at[3, w])

    return load, store_out, store_gin


def alone_kernel(names, *refs):
    r = Refs(**dict(zip(names, refs)))
    count = r.x.shape[0]
    load, store_out, store_gin = io_copies(r, count)
    for w in range(count):
        for copy in load(w):
            copy.start()
    zero_sums(r)
    for w in range(count):
        for copy in load(w):
            copy.wait()

    def second(w):
        windows(FF_PARTS, lambda part: feed_forward(w, part, r))
        store_out(w).start()

    def third(w):
        attention_backward(w, r, lambda w: None)
        store_gin(w).start()

    windows(count, lambda w: hidden_and_keys(w, r))
    windows(count, lambda w: attention_forward(w, r, lambda w: None))
    windows(count, second)
    windows(count, third)
    r.gpos_out[...] = r.gpos[...]
    for w in range(count):
        store_out(w).wait()
        store_gin(w).wait()


def vectors_from(r, dp_count, z_count, rows):
    devices = dp_count * z_count * 2
    per_row = LANES // rows
    ff_rows = r.eb.shape[1] // devices
    per_row_ff = LANES // ff_rows

    def block(d):
        return r.small[d // (2 * z_count), (d // 2) % z_count, d % 2].astype(F32)

    for g in range(devices // per_row):
        added = block(g * per_row)[:8]
        for d in range(g * per_row + 1, (g + 1) * per_row):
            added = added + block(d)[:8]
        r.vec[:, g * LANES : (g + 1) * LANES] = added
    for g in range(devices // per_row_ff):
        added = block(g * per_row_ff)[8:9]
        for d in range(g * per_row_ff + 1, (g + 1) * per_row_ff):
            added = added + block(d)[8:9]
        r.eb[:, g * LANES : (g + 1) * LANES] = added


def place_small(r, place):
    rows, ff_rows = r.vec0.shape[1], r.ebs.shape[1]
    me = (place.dp * place.z_count + place.z) * 2 + place.c

    def spread(n):
        at = lax.rem(me, LANES // n) * n
        source = lax.broadcasted_iota(jnp.int32, (n, LANES), 0)
        target = lax.broadcasted_iota(jnp.int32, (n, LANES), 1)
        return jnp.where(target == source + at, 1.0, 0.0).astype(BF)

    for i in range(8):
        r.eight[i : i + 1, :] = getattr(r, "vec" + str(i))[...].astype(F32)
    r.small_low[0:8, :] = nn(r.eight[...].astype(BF), spread(rows)).astype(BF)
    one = jnp.broadcast_to(r.ebs[...].astype(F32), (8, ff_rows)).astype(BF)
    r.small_low[8:16, :] = nn(one, spread(ff_rows)).astype(BF)


def whole_kernel(counts, names, *refs):
    r = Refs(**dict(zip(names, refs)))
    count = r.x.shape[0]
    rows = r.wq_shard.shape[0]
    place = Place(*counts)
    load, store_out, store_gin = io_copies(r, count)
    for w in range(count):
        for copy in load(w):
            copy.start()
    place_small(r, place)
    gathers = {}
    for name in EARLY + LATE:
        shard = r.small_low if name == "small" else getattr(r, name + "_shard")
        sems = (getattr(r, name + "_send"), getattr(r, name + "_recv"))
        gathers[name] = Gather(place, shard, getattr(r, name), sems, FIRST[name])
    early = [gathers[name] for name in EARLY]
    late = [gathers[name] for name in LATE]
    place.barrier()
    for job in early + late:
        job.start_z()
    zero_sums(r)
    for job in early:
        job.start_dp()
    for job in early:
        job.pass_on()
    for job in early:
        job.start_core()
    for job in late:
        job.start_dp()
    for job in early[:3]:
        job.finish()
    r.pos[...] = flat(r.post[...]).T
    vectors_from(r, counts[0], counts[1], rows)
    for w in range(count):
        for copy in load(w):
            copy.wait()
    windows(count, lambda w: hidden_and_keys(w, r))
    for job in early[3:]:
        job.finish()

    wm, we, ws = late
    first_plan = ((1, (wm.pass_on, we.pass_on)), (3, (ws.pass_on, wm.start_core)))
    first_mid = ()

    def first_body(w):
        at_window(w, first_plan)
        attention_forward(w, r, lambda at: at_window(at, first_mid))

    windows(count, first_body)
    we.start_core()
    ws.start_core()
    for job in late:
        job.finish()

    def second_body(w):
        windows(FF_PARTS, lambda part: feed_forward(w, part, r))
        store_out(w).start()

    windows(count, second_body)

    scatters = {}
    for name in GRADS + ("gpost",):
        total = r.gpost_sum if name == "gpost" else getattr(r, name)
        bufs = [getattr(r, name + tail) for tail in ("_out", "_core", "_dp", "_z")]
        sems = (getattr(r, name + "_send"), getattr(r, name + "_recv"))
        scatters[name] = Scatter(place, total, getattr(r, name + "_result"), bufs, sems, FIRST[name])
    sums = SumAll(
        place, r.gsmall, r.gsmall_result, (r.gsmall_dp, r.gsmall_z, r.gsmall_in), (r.gsmall_send, r.gsmall_recv)
    )
    gws, gwe, gwm = (scatters[name] for name in ("gws", "gwe", "gwm"))
    last = [scatters[name] for name in ("gwq", "gwk", "gwv", "gpost")]
    gws.start_core()
    gwe.start_core()
    gwm.start_core()
    third_plan = ((1, (gwe.start_dp, gwm.start_dp)), (3, (gwe.pass_on, gwm.pass_on)))
    third_mid = ((0, (gws.start_dp,)), (2, (gws.pass_on,)), (3, (gws.start_z,)))

    def third_body(w):
        at_window(w, third_plan)
        attention_backward(w, r, lambda at: at_window(at, third_mid))
        store_gin(w).start()

    windows(count, third_body)
    for job in last[:3]:
        job.start_core()
    add_blocks = r.gpos[...].T
    r.gpost_sum[...] = add_blocks.reshape(r.gpost_sum.shape)
    last[3].start_core()
    ff_rows = r.geb.shape[1] // r.gvec.shape[1]
    width = r.gvec.shape[1]
    r.gsmall[0:8, :] = r.gvec[...]
    r.gsmall[8:16, :] = jnp.zeros((8, width), F32)
    for i in range(ff_rows):
        r.gsmall[8 + i : 9 + i, :] = r.geb[:, i * width : (i + 1) * width]
    sums.start_core()
    last = last + [sums]
    for job in last:
        job.start_dp()
    gwe.start_z()
    gwm.start_z()
    for job in last:
        job.pass_on()
    for job in last:
        job.start_z()
    everyone = [gws, gwe, gwm] + last
    for job in everyone:
        job.finish()
    for job in early + late + everyone:
        job.drain()
    for w in range(count):
        store_out(w).wait()
        store_gin(w).wait()


def unpack_kernel(counts, names, *refs):
    r = Refs(**dict(zip(names, refs)))
    count = r.out.shape[0]
    loads, stores = [], []
    for w in range(count):
        for i, name in enumerate(("out", "gin")):
            source, target = getattr(r, name + "_in").at[w], getattr(r, name).at[w]
            loads.append(pltpu.make_async_copy(source, r.held.at[i, w], r.sem.at[0, i, w]))
            stores.append(pltpu.make_async_copy(r.held.at[i, w], target, r.sem.at[1, i, w]))
    for copy in loads:
        copy.start()
    for load, store in zip(loads, stores):
        load.wait()
        store.start()
    for name in GRADS:
        getattr(r, name)[...] = getattr(r, name + "_in")[...]
    r.gpos[...] = r.gpost_in[...].T
    place = Place(*counts)
    me = (place.dp * place.z_count + place.z) * 2 + place.c
    rows, ff_rows = r.gvec.shape[1], r.geb.shape[1]
    width = r.gsmall_in.shape[1]
    turned = pltpu.roll(r.gsmall_in[0:8, :], width - me * rows, axis=1)
    r.gvec[...] = turned[:, :rows]
    start = me * ff_rows
    lines = r.gsmall_in[8:16, :]
    line_at = lax.broadcasted_iota(jnp.int32, (8, width), 0)
    line = jnp.sum(jnp.where(line_at == start // width, lines, 0.0), axis=0, keepdims=True)
    line = jnp.broadcast_to(line, (8, width))
    r.geb[...] = pltpu.roll(line, width - lax.rem(start, width), axis=1)[0:1, :ff_rows]
    for copy in stores:
        copy.wait()


def call(kernel, name, ins, outs, scratch, **params):
    names = tuple(ins) + tuple(outs) + tuple(scratch)
    spec = lambda space: pl.BlockSpec(memory_space=space)
    results = pl.pallas_call(
        functools.partial(kernel, names),
        out_shape=tuple(shape for shape, _ in outs.values()),
        in_specs=[spec(space) for _, space in ins.values()],
        out_specs=tuple(spec(space) for _, space in outs.values()),
        scratch_shapes=list(scratch.values()),
        compiler_params=pltpu.CompilerParams(vmem_limit_bytes=63 * 2**20, **params),
        name=name,
    )(*[value for value, _ in ins.values()])
    return dict(zip(outs, results))


def local(dp_count, fsdp_count, inputs, lengths, grad_out, *params):
    micro, per_micro, seq, width = inputs.shape
    count = micro * per_micro
    wq, wk, wv, wm, we, ws, pos = params[:7]
    bq, bv, bm, eb, bs, g1, s1, g2, s2 = params[7:]
    ff = we.shape[1]
    rows, ff_rows = wq.shape[0], ws.shape[0]
    vectors = (bq, bv, bm, bs, g1, s1, g2, s2)
    vm, hbm = pltpu.VMEM, pl.ANY
    shape_of = jax.ShapeDtypeStruct
    merged = lambda a: a.reshape((count,) + a.shape[2:])
    act = shape_of((count, seq, width), BF)
    data = dict(
        lens=(lengths, pltpu.SMEM), x_in=(merged(inputs), hbm), go_in=(merged(grad_out), hbm)
    )
    scratch = work_scratch(count, seq, width, ff)
    if dp_count == 4 and fsdp_count % 2 == 0 and rows % 16 == 0 and LANES % rows == 0 and LANES % ff_rows == 0:
        counts = (dp_count, fsdp_count // 2)
        lead = (dp_count, fsdp_count // 2, 2)
        shards = dict(wq=wq, wk=wk, wv=wv, wm=wm, we=we, ws=ws, post=pos.T)
        ins = dict(data)
        for name, shard in shards.items():
            ins[name + "_shard"] = (shard, vm)
        for i, vector in enumerate(vectors):
            ins["vec" + str(i)] = (vector[None], vm)
        ins["ebs"] = (eb[None], vm)
        outs = dict(out=(act, hbm), gin=(act, hbm))
        results = dict(gwq=wq, gwk=wk, gwv=wv, gwm=wm, gwe=we, gws=ws, gpost=pos.T)
        for name, like in results.items():
            outs[name + "_result"] = (shape_of(like.shape, F32), vm)
        outs["gsmall_result"] = (shape_of((16, width), F32), vm)
        hops = hop_count(*counts)
        pair = lambda name: {name + tail: pltpu.SemaphoreType.DMA((hops,)) for tail in ("_send", "_recv")}
        for name, shard in shards.items():
            scratch[name] = vm(lead + shard.shape, BF)
            scratch.update(pair(name))
        scratch["small"] = vm(lead + (16, LANES), BF)
        scratch["eight"] = vm((8, rows), F32)
        scratch["small_low"] = vm((16, LANES), BF)
        scratch["pos"] = vm((seq, width), BF)
        scratch["vec"] = vm((8, width), F32)
        scratch["eb"] = vm((1, ff), F32)
        scratch["gvec"] = vm((8, width), F32)
        scratch["geb"] = vm((1, ff), F32)
        scratch.update(pair("small"))
        scratch.update(pair("gsmall"))
        for name, like in results.items():
            scratch["gpost_sum" if name == "gpost" else name] = vm(lead + like.shape, F32)
            scratch[name + "_out"] = vm(lead[:2] + like.shape, BF)
            scratch[name + "_core"] = vm(lead[:2] + like.shape, BF)
            scratch[name + "_dp"] = vm((3,) + lead[1:2] + like.shape, BF)
            scratch[name + "_z"] = vm((lead[1] - 1,) + like.shape, BF)
            scratch.update(pair(name))
        for tail in ("", "_dp", "_z"):
            scratch["gsmall" + tail] = vm((16, width), F32)
        scratch["gsmall_in"] = vm((hops, 16, width), F32)
        got = call(
            functools.partial(whole_kernel, counts), "layer", ins, outs, scratch,
            collective_id=0, has_side_effects=True,
        )
        ins = {}
        for name in ("out", "gin"):
            ins[name + "_in"] = (got[name], hbm)
        for name in GRADS + ("gpost", "gsmall"):
            ins[name + "_in"] = (got[name + "_result"], vm)
        outs = dict(out=(act, hbm), gin=(act, hbm))
        for name in GRADS:
            outs[name] = (shape_of(results[name].shape, F32), vm)
        outs["gpos"] = (shape_of(pos.shape, F32), vm)
        outs["gvec"] = (shape_of((8, rows), F32), vm)
        outs["geb"] = (shape_of((1, ff_rows), F32), vm)
        got = call(
            functools.partial(unpack_kernel, counts), "unpack", ins, outs,
            dict(held=vm((2,) + act.shape, BF), sem=pltpu.SemaphoreType.DMA((2, 2, count))),
        )
        gvec, geb, gpos = got["gvec"], got["geb"][0], got["gpos"]
        grads = got
    else:
        lead = (4, 4, 2)
        cut = lambda a: a.reshape(lead + (-1, a.shape[-1]))
        gather = lambda a, axis=0: lax.all_gather(a, AXES, axis=axis, tiled=True)
        share = lambda a, axis=0: lax.psum_scatter(a, AXES, scatter_dimension=axis, tiled=True)
        ins = dict(data)
        for name, shard in dict(wq=wq, wk=wk, wv=wv, wm=wm, we=we, ws=ws).items():
            ins[name] = (cut(gather(shard)), vm)
        ins["pos"] = (gather(pos, 1), vm)
        ins["vec"] = (jnp.stack([gather(a).astype(F32) for a in vectors]), vm)
        ins["eb"] = (gather(eb).astype(F32)[None], vm)
        outs = dict(out=(act, hbm), gin=(act, hbm))
        for name in GRADS:
            outs[name] = (shape_of(ins["w" + name[2:]][0].shape, F32), vm)
        outs["gpos_out"] = (shape_of((seq, width), F32), vm)
        outs["gvec"] = (shape_of((8, width), F32), vm)
        outs["geb"] = (shape_of((1, ff), F32), vm)
        got = call(alone_kernel, "layer_alone", ins, outs, scratch)
        grads = {name: share(flat(got[name])) for name in GRADS}
        gpos = share(got["gpos_out"], 1)
        gvec = [share(got["gvec"][i]) for i in range(8)]
        geb = share(got["geb"][0])
    gbq, gbv, gbm, gbs, gg1, gs1, gg2, gs2 = (gvec[i] for i in range(8))
    return (
        got["out"].reshape(inputs.shape), got["gin"].reshape(inputs.shape),
        grads["gwq"], grads["gwk"], grads["gwv"], grads["gwm"], grads["gwe"], grads["gws"], gpos,
        gbq, gbv, gbm, geb, gbs, gg1, gs1, gg2, gs2,
    )


def solution(mesh):
    batch = P(None, AXES, None, None)
    matrix, vector, table = P(AXES, None), P(AXES), P(None, AXES)
    weights = (matrix,) * 6 + (table,) + (vector,) * 9
    return jax.shard_map(
        functools.partial(local, mesh.shape["dp"], mesh.shape["fsdp"]),
        mesh=mesh,
        in_specs=(batch, P(None, AXES), batch) + weights,
        out_specs=(batch, batch) + weights,
        check_vma=False,
    )
```

```python
import functools

import jax
import jax.numpy as jnp
from jax import lax
from jax.experimental import pallas as pl
from jax.experimental.pallas import tpu as pltpu
from jax.sharding import PartitionSpec as P

HEADS = 8
EPS = 1e-05
BF = jnp.bfloat16
F32 = jnp.float32
GELU_C = 0.7978845608028654
GELU_A = 0.044715
AXES = ("dp", "fsdp")
LANES = 128
MESH = pl.DeviceIdType.MESH
FF_PARTS = 1
GROUPS = 2

(BQ, BV, BM, BS, G1, S1, G2, S2) = range(8)
(Q, K, V, LOW) = range(4)


class Refs:
    def __init__(self, **kw):
        self.__dict__.update(kw)


def nn(a, b):
    return lax.dot_general(a, b, (((1,), (0,)), ((), ())), preferred_element_type=F32)


def nt(a, b):
    return lax.dot_general(a, b, (((1,), (1,)), ((), ())), preferred_element_type=F32)


def tn(a, b):
    return lax.dot_general(a, b, (((0,), (0,)), ((), ())), preferred_element_type=F32)


def flat(value):
    return value.reshape(-1, value.shape[-1])


def add_into(ref, value):
    ref[...] += value.reshape(ref.shape)


def add_row(ref, index, value):
    ref[index : index + 1, :] += jnp.sum(value, axis=0, keepdims=True)


def length_of(w, r):
    per_micro = r.lens.shape[1]
    return r.lens[w // per_micro, lax.rem(w, per_micro)]


def make_mask(w, r):
    seq = r.x.shape[1]
    key_at = lax.broadcasted_iota(jnp.int32, (seq, seq), 0)
    query_at = lax.broadcasted_iota(jnp.int32, (seq, seq), 1)
    ok = (key_at <= query_at) & (key_at < length_of(w, r))
    r.mask[...] = jnp.where(ok, 0.0, -1e30)


def hidden_and_keys(w, r):
    low = (r.x[w].astype(F32) + r.pos[...].astype(F32)).astype(BF)
    r.ab[LOW, w] = low
    r.ab[K, w] = nn(low, flat(r.wk[...])).astype(BF)


def attention_forward(w, r):
    seq, width = r.x.shape[1:]
    half = seq // 2
    head = width // HEADS
    low = r.ab[LOW, w]
    queries = (nn(low, flat(r.wq[...])) + r.vec[BQ : BQ + 1, :]).astype(BF)
    r.ab[Q, w] = (queries.astype(F32) * (head**-0.5)).astype(BF)
    values = (nn(low, flat(r.wv[...])) + r.vec[BV : BV + 1, :]).astype(BF)
    r.ab[V, w] = values
    r.vt[...] = values.T
    make_mask(w, r)
    lane = lax.broadcasted_iota(jnp.int32, (seq, 2 * head), 1)
    for h in range(HEADS):
        pair = slice((h // 2) * 2 * head, (h // 2 + 1) * 2 * head)
        mine = (lane < head) if h % 2 == 0 else (lane >= head)
        qh = jnp.where(mine, r.ab[Q, w, :, pair], jnp.zeros((), BF))
        kp = r.ab[K, w, :, pair]
        s0 = nt(kp[:half], qh) + r.mask[:half, :]
        s1 = nt(kp[half:], qh[half:]) + r.mask[half:, half:]
        m_left = jnp.max(s0[:, :half], axis=0, keepdims=True)
        m_right = jnp.maximum(
            jnp.max(s0[:, half:], axis=0, keepdims=True), jnp.max(s1, axis=0, keepdims=True)
        )
        top = jnp.concatenate([m_left, m_right], axis=1)
        e0 = jnp.exp(s0 - top)
        e1 = jnp.exp(s1 - m_right)
        n_all = jnp.sum(e0, axis=0, keepdims=True)
        n_right = n_all[:, half:] + jnp.sum(e1, axis=0, keepdims=True)
        total = jnp.concatenate([n_all[:, :half], n_right], axis=1)
        r.logt[w, h : h + 1, :] = top + jnp.log(total)
        inv = 1.0 / total
        p0 = (e0 * inv).astype(BF)
        p1 = (e1 * inv[:, half:]).astype(BF)
        vt = r.vt[h * head : (h + 1) * head, :]
        o_left = nn(vt[:, :half], p0[:, :half])
        o_right = nn(vt, jnp.concatenate([p0[:, half:], p1], axis=0))
        r.ot[h * head : (h + 1) * head, :half] = o_left.astype(BF)
        r.ot[h * head : (h + 1) * head, half:] = o_right.astype(BF)
    r.mixed[w] = r.ot[...].T
    for i in range(4):
        park_copy(r, i, w).start()


def norm_parts(total):
    center = total - jnp.mean(total, -1, keepdims=True)
    spread = jnp.mean(center * center, -1, keepdims=True)
    inv = lax.rsqrt(spread + EPS)
    return center * inv, inv


def norm_back(e, xhat, inv):
    return inv * (
        e - jnp.mean(e, -1, keepdims=True) - xhat * jnp.mean(e * xhat, -1, keepdims=True)
    )


def slot_of(kind, w, c):
    return (kind + 2 * lax.rem(w, 2), c)


def part_copy(r, kind, w, part, c, rows):
    here = slice(part * rows, (part + 1) * rows)
    target = r.kept.at[1 + kind, c, w]
    return pltpu.make_async_copy(r.ab.at[slot_of(kind, w, c)], target, r.part_sem.at[kind, lax.rem(w, 2), c])


def park_copy(r, i, w):
    return pltpu.make_async_copy(r.ab.at[i, w], r.kept.at[0, i, w], r.park_sem.at[i, w])


def finish_parking(r):
    for i in range(4):
        for w in range(r.x.shape[0]):
            park_copy(r, i, w).wait()


def block_load(r, kind, c, buffer):
    return pltpu.make_async_copy(r.kept.at[kind, c], r.ab.at[buffer], r.load_sem.at[buffer])


BUFFERS = (2, 3, 0, 1, 2, 0, 1, 3)
FOLLOWS = {0: (2, 0), 1: (2, 3), 2: (2, 1), 3: (2, 2), 4: (0, 2), 5: (0, 0), 6: (0, 1), 7: (0, 3)}


def weight_sums(r, emit, after):
    count = r.x.shape[0]
    rows, chunks = r.slope.shape[0], r.ws.shape[0]
    for kind in range(2):
        for part in range(FF_PARTS):
            for c in range(chunks):
                part_copy(r, kind, count - 2, part, c, rows).wait()
                part_copy(r, kind, count - 1, part, c, rows).wait()
    for item in range(4):
        block_load(r, 1, item, BUFFERS[item]).start()
    for item in range(2 * chunks):
        buffer, c = BUFFERS[item], item % chunks
        block_load(r, 1 + item // chunks, c, buffer).wait()
        block = flat(r.ab[buffer])
        if item < chunks:
            emit(item, tn(block, flat(r.gff[...])))
        else:
            emit(item, tn(flat(r.nl[...]), block))
        block_load(r, *FOLLOWS[item], buffer).start()
        after(item)
    for buffer in range(4):
        block_load(r, 0, buffer, buffer).wait()


def feed_forward(w, part, r):
    rows, width = r.slope.shape[0], r.x.shape[-1]
    here = slice(part * rows, (part + 1) * rows)
    chunks = r.ws.shape[0]
    chunk = r.we.shape[-1] // chunks

    @pl.when(w > 1)
    def _():
        for kind in range(2):
            for c in range(chunks):
                part_copy(r, kind, w - 2, part, c, rows).wait()

    hid = r.x[w, here, :].astype(F32) + r.pos[here, :].astype(F32)
    first = hid + (nn(r.mixed[w, here, :], flat(r.wm[...])) + r.vec[BM : BM + 1, :])
    xhat1, inv1 = norm_parts(first)
    r.xh1[...] = xhat1
    normed = xhat1 * r.vec[G1 : G1 + 1, :] + r.vec[S1 : S1 + 1, :]
    r.nl[w, here, :] = normed.astype(BF)
    ff_out = None
    for c in range(chunks):
        cols = slice(c * chunk, (c + 1) * chunk)
        t = nn(r.nl[w, here, :], flat(r.we[..., cols])) + r.eb[:, cols]
        t2 = t * t
        th = jnp.tanh(t * (t2 * (GELU_A * GELU_C) + GELU_C))
        ht = 0.5 * t
        act = (ht * th + ht).astype(BF)
        slot = slot_of(0, w, c)
        r.ab[slot] = act
        slope = (0.5 * th + 0.5) + ht * (1.0 - th * th) * (t2 * (3 * GELU_A * GELU_C) + GELU_C)
        r.slope[:, cols] = slope
        part_out = nn(act, flat(r.ws[c]))
        ff_out = part_out if ff_out is None else ff_out + part_out
    second = normed + (ff_out + r.vec[BS : BS + 1, :])
    xhat2, inv2 = norm_parts(second)
    row_at = part * rows + lax.broadcasted_iota(jnp.int32, (rows, width), 0)
    cot = jnp.where(row_at < length_of(w, r), r.go[w, here, :].astype(F32), 0.0)
    r.go[w, here, :] = (xhat2 * r.vec[G2 : G2 + 1, :] + r.vec[S2 : S2 + 1, :]).astype(BF)
    add_row(r.gvec, G2, cot * xhat2)
    add_row(r.gvec, S2, cot)
    d_second = norm_back(cot * r.vec[G2 : G2 + 1, :], xhat2, inv2)
    gff = d_second.astype(BF)
    r.gff[w, here, :] = gff
    add_row(r.gvec, BS, gff.astype(F32))
    d_normed = d_second
    for c in range(chunks):
        cols = slice(c * chunk, (c + 1) * chunk)
        gpre = (nt(r.gff[w, here, :], flat(r.ws[c])) * r.slope[:, cols]).astype(BF)
        r.geb[:, cols] += jnp.sum(gpre.astype(F32), axis=0, keepdims=True)
        slot = slot_of(1, w, c)
        r.ab[slot] = gpre
        d_normed = d_normed + nt(gpre, flat(r.we[..., cols]))
    xhat1 = r.xh1[...]
    add_row(r.gvec, G1, d_normed * xhat1)
    add_row(r.gvec, S1, d_normed)
    d_first = norm_back(d_normed * r.vec[G1 : G1 + 1, :], xhat1, inv1)
    r.dfirst[w, here, :] = d_first
    gattn = d_first.astype(BF)
    add_row(r.gvec, BM, gattn.astype(F32))
    mixed = r.mixed[w, here, :]
    add_into(r.gwm, tn(mixed, gattn))
    gmix = nt(gattn, flat(r.wm[...])).astype(BF)
    head = width // HEADS
    prod = gmix.astype(F32) * mixed.astype(F32)
    hi = prod.astype(BF)
    lo = (prod - hi.astype(F32)).astype(BF)
    sel_row = lax.broadcasted_iota(jnp.int32, (16, width), 0)
    sel_col = lax.broadcasted_iota(jnp.int32, (16, width), 1)
    sel = jnp.where(sel_col // head == sel_row, 1.0, 0.0).astype(BF)
    r.delta[w, :, here] = nt(sel, hi) + nt(sel, lo)
    r.mixed[w, here, :] = gmix
    for kind in range(2):
        for c in range(chunks):
            part_copy(r, kind, w, part, c, rows).start()


def attention_backward(w, group, r):
    seq, width = r.x.shape[1:]
    half = seq // 2
    head = width // HEADS
    scale = head**-0.5
    cols = slice(group * (width // GROUPS), (group + 1) * (width // GROUPS))
    make_mask(w, r)
    r.vt[cols, :] = r.ab[K, w, :, cols].T
    lane = lax.broadcasted_iota(jnp.int32, (seq, 2 * head), 1)
    pairs = HEADS // 2 // GROUPS
    for p in range(group * pairs, (group + 1) * pairs):
        pair = slice(p * 2 * head, (p + 1) * 2 * head)
        kp = r.ab[K, w, :, pair]
        vp = r.ab[V, w, :, pair]
        sums = None
        for odd in range(2):
            h = 2 * p + odd
            mine = (lane >= head) if odd else (lane < head)
            qh = jnp.where(mine, r.ab[Q, w, :, pair], jnp.zeros((), BF))
            gh = jnp.where(mine, r.mixed[w, :, pair], jnp.zeros((), BF))
            logt = r.logt[w, h : h + 1, :]
            delta = r.delta[w, h : h + 1, :]
            p0 = jnp.exp(nt(kp[:half], qh) + r.mask[:half, :] - logt)
            p1 = jnp.exp(nt(kp[half:], qh[half:]) + r.mask[half:, half:] - logt[:, half:])
            d0 = (p0 * (nt(vp[:half], gh) - delta)).astype(BF)
            d1 = (p1 * (nt(vp[half:], gh[half:]) - delta[:, half:])).astype(BF)
            p0 = p0.astype(BF)
            p1 = p1.astype(BF)
            parts = (nn(d0, qh), nn(d1, qh[half:]), nn(p0, gh), nn(p1, gh[half:]))
            sums = parts if sums is None else tuple(a + b for a, b in zip(sums, parts))
            kt = r.vt[h * head : (h + 1) * head, :]
            q_left = nn(kt[:, :half], d0[:, :half])
            q_right = nn(kt, jnp.concatenate([d0[:, half:], d1], axis=0))
            r.ot[h * head : (h + 1) * head, :half] = (q_left * scale).astype(BF)
            r.ot[h * head : (h + 1) * head, half:] = (q_right * scale).astype(BF)
        grads = [part.astype(BF) for part in sums]
        r.ab[K, w, :half, pair] = grads[0]
        r.ab[K, w, half:, pair] = grads[1]
        r.ab[V, w, :half, pair] = grads[2]
        r.ab[V, w, half:, pair] = grads[3]
        gq = r.ot[pair, :].T
        r.ab[Q, w, :, pair] = gq
        r.gvec[BQ : BQ + 1, pair] += jnp.sum(gq.astype(F32), axis=0, keepdims=True)
        gv = grads[2].astype(F32) + grads[3].astype(F32)
        r.gvec[BV : BV + 1, pair] += jnp.sum(gv, axis=0, keepdims=True)


def projection_sums(group, r):
    width = r.x.shape[-1]
    size = width // GROUPS
    cols = slice(group * size, (group + 1) * size)
    total = getattr(r, "gqkv" + str(group))
    for at, kind in enumerate((Q, K, V)):
        total[:, at * size : (at + 1) * size] = tn(flat(r.ab[LOW]), flat(r.ab[kind, :, :, cols]))


def hidden_back(w, r):
    d_hidden = (
        r.dfirst[w]
        + nt(r.ab[Q, w], flat(r.wq[...]))
        + nt(r.ab[K, w], flat(r.wk[...]))
        + nt(r.ab[V, w], flat(r.wv[...]))
    )
    r.gpos[...] += d_hidden
    r.x[w] = d_hidden.astype(BF)


def windows(count, body):
    def step(w, carry):
        body(w)
        return carry

    lax.fori_loop(0, count, step, 0)


def at_window(w, plan):
    for index, steps in plan:

        @pl.when(w == index)
        def _():
            for step in steps:
                step()


class Place:
    def __init__(self, dp_count, z_count):
        self.dp_count, self.z_count = dp_count, z_count
        self.dp = lax.axis_index("dp")
        fsdp = lax.axis_index("fsdp")
        self.z, self.c = fsdp // 2, lax.rem(fsdp, 2)
        self.near = (self.dp, self.z * 2 + (1 - self.c))

    def z_at(self, shift):
        return lax.rem(self.z + shift + self.z_count, self.z_count)

    def dp_flip(self, bit):
        low, high = lax.rem(self.dp, 2), self.dp // 2
        if bit in (0, 2):
            low = 1 - low
        if bit in (1, 2):
            high = 1 - high
        return high * 2 + low

    def along_z(self, shift):
        return (self.dp, self.z_at(shift) * 2 + self.c)

    def along_dp(self, bit):
        return (self.dp_flip(bit), self.z * 2 + self.c)

    def barrier(self):
        sem = pltpu.get_barrier_semaphore()
        everyone = [self.near] + [self.along_z(s) for s in range(1, self.z_count)]
        everyone += [self.along_dp(bit) for bit in range(3)]
        for peer in everyone:
            pl.semaphore_signal(sem, inc=1, device_id=peer, device_id_type=MESH)
        pl.semaphore_wait(sem, len(everyone))


def remote(src, dst, sems, index, peer):
    send, recv = sems
    return pltpu.make_async_remote_copy(
        src_ref=src, dst_ref=dst, send_sem=send.at[index], recv_sem=recv.at[index],
        device_id=peer, device_id_type=MESH,
    )


def hop_count(dp_count, z_count):
    return (z_count - 1) + 7


def halves(ref):
    lanes = ref.shape[-1]
    if lanes % (2 * LANES):
        return ((0, slice(0, lanes)),)
    return ((0, slice(0, lanes // 2)), (1, slice(lanes // 2, lanes)))


class Gather:
    def __init__(self, place, shard, whole, sems):
        self.p, self.shard, self.whole, self.sems = place, shard, whole, sems
        self.base = place.z_count - 1

    def z_copy(self, shift, z):
        p = self.p
        return remote(self.shard, self.whole.at[p.dp, z, p.c], self.sems, shift - 1, p.along_z(shift))

    def own_copy(self, bit, owner):
        block = self.whole.at[owner, :, self.p.c]
        return remote(block, block, self.sems, self.base + bit, self.p.along_dp(bit))

    def far_copy(self, bit, lanes, owner):
        block = self.whole.at[owner, :, self.p.c, :, lanes]
        return remote(block, block, self.sems, self.base + 2 + bit, self.p.along_dp(1 - bit))

    def core_copy(self, core):
        half = self.whole.at[:, :, core]
        return remote(half, half, self.sems, self.base + 4, self.p.near)

    def start_z(self):
        p = self.p
        for shift in range(1, p.z_count):
            self.z_copy(shift, p.z).start()
        self.whole[p.dp, p.z, p.c] = self.shard[...]

    def start_dp(self):
        p = self.p
        for shift in range(1, p.z_count):
            self.z_copy(shift, p.z_at(-shift)).wait_recv()
        for bit in range(2):
            self.own_copy(bit, p.dp).start()

    def pass_on(self):
        p = self.p
        for bit in range(2):
            self.own_copy(bit, p.dp_flip(bit)).wait_recv()
        for bit, lanes in halves(self.whole):
            self.far_copy(bit, lanes, p.dp_flip(bit)).start()

    def start_core(self):
        p = self.p
        for bit, lanes in halves(self.whole):
            self.far_copy(bit, lanes, p.dp_flip(2)).wait_recv()
        self.core_copy(p.c).start()

    def finish(self):
        self.core_copy(1 - self.p.c).wait_recv()

    def drain(self):
        p = self.p
        for shift in range(1, p.z_count):
            self.z_copy(shift, p.z).wait_send()
        for bit in range(2):
            self.own_copy(bit, p.dp).wait_send()
        for bit, lanes in halves(self.whole):
            self.far_copy(bit, lanes, p.dp_flip(bit)).wait_send()
        self.core_copy(p.c).wait_send()


class Scatter:
    def __init__(self, place, total, result, bufs, sems):
        self.p, self.total, self.result, self.sems = place, total, result, sems
        self.out, self.from_core, self.from_dp, self.from_z = bufs
        self.base = place.z_count - 1

    def core_copy(self):
        return remote(self.out, self.from_core, self.sems, self.base + 6, self.p.near)

    def dp_copy(self, slot, bit, lanes):
        p = self.p
        block = p.dp_flip((2, bit, 1 - bit)[slot])
        return remote(
            self.out.at[block, :, :, lanes], self.from_dp.at[slot, :, :, lanes], self.sems,
            self.base + 2 * slot + bit, p.along_dp((bit, bit, 1 - bit)[slot]),
        )

    def z_copy(self, shift):
        p = self.p
        block = self.out.at[p.dp, p.z_at(shift)]
        return remote(block, self.from_z.at[shift - 1], self.sems, shift - 1, p.along_z(shift))

    def blocks(self, body):
        p = self.p

        def step(at, carry):
            body(at // p.z_count, lax.rem(at, p.z_count))
            return carry

        lax.fori_loop(0, p.dp_count * p.z_count, step, 0)

    def rows_at(self, d, z, core):
        size = self.result.shape[0]
        start = ((d * self.p.z_count + z) * 2 + core) * size
        return self.total.at[pl.ds(pl.multiple_of(start, size), size)]

    def mine(self, d, z):
        if len(self.total.shape) == 4:
            return self.total.at[d, z]
        return self.rows_at(d, z, self.p.c)

    def start_core(self):
        far = 1 - self.p.c

        def body(d, z):
            self.out[d, z] = self.rows_at(d, z, far)[...].astype(BF)

        if len(self.total.shape) == 2:
            self.blocks(body)
        self.core_copy().start()

    def start_dp(self):
        copy = self.core_copy()
        copy.wait_recv()
        copy.wait_send()

        def body(d, z):
            mine = self.mine(d, z)
            both = mine[...] + self.from_core[d, z].astype(F32)
            mine[...] = both
            self.out[d, z] = both.astype(BF)

        self.blocks(body)
        for slot in range(2):
            for bit, lanes in halves(self.out):
                self.dp_copy(slot, bit, lanes).start()

    def pass_on(self):
        p = self.p
        for bit, lanes in halves(self.out):
            self.dp_copy(0, bit, lanes).wait_recv()
            other = p.dp_flip(1 - bit)
            for z in range(p.z_count):
                added = self.mine(other, z)[:, lanes] + self.from_dp[0, z, :, lanes].astype(F32)
                self.out[other, z, :, lanes] = added.astype(BF)
            self.dp_copy(2, bit, lanes).start()

    def start_z(self):
        p = self.p
        for slot in (1, 2):
            for bit, lanes in halves(self.out):
                self.dp_copy(slot, bit, lanes).wait_recv()
        for z in range(p.z_count):
            mine = self.mine(p.dp, z)
            added = mine[...] + self.from_dp[1, z].astype(F32) + self.from_dp[2, z].astype(F32)
            mine[...] = added
            self.out[p.dp, z] = added.astype(BF)
        for shift in range(1, p.z_count):
            self.z_copy(shift).start()

    def finish(self):
        p = self.p
        added = self.mine(p.dp, p.z)[...]
        for shift in range(1, p.z_count):
            self.z_copy(shift).wait_recv()
            added = added + self.from_z[shift - 1].astype(F32)
        self.result[...] = added

    def drain(self):
        for slot in range(3):
            for bit, lanes in halves(self.out):
                self.dp_copy(slot, bit, lanes).wait_send()
        for shift in range(1, self.p.z_count):
            self.z_copy(shift).wait_send()


class SumAll:
    def __init__(self, place, total, result, bufs, sems):
        self.p, self.total, self.result, self.sems = place, total, result, sems
        self.send_dp, self.send_z, self.landing = bufs

    def copies(self, hop):
        p = self.p
        base = p.z_count - 1
        if hop == 0:
            return [(base + 3, remote(self.total, self.landing.at[base + 3], self.sems, base + 3, p.near))]
        if hop == 1:
            return [
                (base + b, remote(self.send_dp, self.landing.at[base + b], self.sems, base + b, p.along_dp(b)))
                for b in range(3)
            ]
        return [
            (s - 1, remote(self.send_z, self.landing.at[s - 1], self.sems, s - 1, p.along_z(s)))
            for s in range(1, p.z_count)
        ]

    def arrived(self, hop, own):
        added = own[...]
        for slot, copy in self.copies(hop):
            copy.wait_recv()
            added = added + self.landing[slot]
        return added

    def start(self, hop):
        for _, copy in self.copies(hop):
            copy.start()

    def start_core(self):
        self.start(0)

    def start_dp(self):
        self.send_dp[...] = self.arrived(0, self.total)
        self.start(1)

    def pass_on(self):
        pass

    def start_z(self):
        self.send_z[...] = self.arrived(1, self.send_dp)
        self.start(2)

    def finish(self):
        self.result[...] = self.arrived(2, self.send_z)

    def drain(self):
        for hop in range(3):
            for _, copy in self.copies(hop):
                copy.wait_send()


WEIGHTS = ("wk", "wq", "wv", "wm", "we", "ws")
GRADS = ("gws", "gwe", "gwm", "gqkv0", "gqkv1")
EARLY = ("post", "small", "wk", "wq", "wv")
LATE = ("wm", "we", "ws")


def work_scratch(count, seq, width, ff):
    vm = pltpu.VMEM
    return dict(
        ab=vm((4, count, seq, width), BF),
        mixed=vm((count, seq, width), BF),
        dfirst=vm((count, seq, width), F32),
        logt=vm((count, HEADS, seq), F32),
        delta=vm((count, 16, seq), F32),
        vt=vm((width, seq), BF),
        ot=vm((width, seq), BF),
        mask=vm((seq, seq), F32),
        xh1=vm((seq // FF_PARTS, width), F32),
        nl=vm((count, seq, width), BF),
        gff=vm((count, seq, width), BF),
        slope=vm((seq // FF_PARTS, ff), F32),
        gpos=vm((seq, width), F32),
        x=vm((count, seq, width), BF),
        go=vm((count, seq, width), BF),
        io_sem=pltpu.SemaphoreType.DMA((4, count)),
        part_sem=pltpu.SemaphoreType.DMA((2, 2, 4)),
        park_sem=pltpu.SemaphoreType.DMA((4, count)),
        load_sem=pltpu.SemaphoreType.DMA((4,)),
    )


def zero_sums(r):
    for name in ("gwm", "gpos", "gvec", "geb"):
        ref = getattr(r, name)
        ref[...] = jnp.zeros(ref.shape, ref.dtype)


def io_copies(r, count):
    def load(w):
        return (
            pltpu.make_async_copy(r.x_in.at[w], r.x.at[w], r.io_sem.at[0, w]),
            pltpu.make_async_copy(r.go_in.at[w], r.go.at[w], r.io_sem.at[1, w]),
        )

    def store_out(w):
        return pltpu.make_async_copy(r.go.at[w], r.out.at[w], r.io_sem.at[2, w])

    def store_gin(w):
        return pltpu.make_async_copy(r.x.at[w], r.gin.at[w], r.io_sem.at[3, w])

    return load, store_out, store_gin


def emit_whole(r, item, value):
    size = value.shape[0]
    if item < r.ws.shape[0]:
        r.gws[item * size : (item + 1) * size, :] = value
    else:
        c = item - r.ws.shape[0]
        r.gwe[:, c * size : (c + 1) * size] = value


def emit_halves(r, place, item, value):
    r.mask[...] = value
    chunks, size = r.ws.shape[0], value.shape[0]
    if item < chunks:
        blocks = [((item, z), z) for z in range(place.z_count)]
        kept, sent, rows = r.gws, r.gws_out, r.gws.shape[2]
        cols = slice(None)
    else:
        blocks = [((d, z), d * place.z_count + z) for d in range(place.dp_count) for z in range(place.z_count)]
        kept, sent, rows = r.gwe, r.gwe_out, r.gwe.shape[2]
        cols = slice((item - chunks) * size, (item - chunks + 1) * size)
    for at, block in blocks:
        start = pl.multiple_of((block * 2 + place.c) * rows, rows)
        kept[at + (slice(None), cols)] = r.mask[pl.ds(start, rows), :]
        start = pl.multiple_of((block * 2 + 1 - place.c) * rows, rows)
        sent[at + (slice(None), cols)] = r.mask[pl.ds(start, rows), :].astype(BF)


def alone_kernel(names, *refs):
    r = Refs(**dict(zip(names, refs)))
    count = r.x.shape[0]
    load, store_out, store_gin = io_copies(r, count)
    for w in range(count):
        for copy in load(w):
            copy.start()
    zero_sums(r)
    for w in range(count):
        for copy in load(w):
            copy.wait()

    def second(w):
        feed_forward(w, 0, r)
        store_out(w).start()

    def third(w):
        hidden_back(w, r)
        store_gin(w).start()

    windows(count, lambda w: hidden_and_keys(w, r))
    windows(count, lambda w: attention_forward(w, r))
    finish_parking(r)
    windows(count, second)
    weight_sums(r, lambda item, value: emit_whole(r, item, value), lambda item: None)
    for group in range(GROUPS):
        windows(count, lambda w: attention_backward(w, group, r))
        projection_sums(group, r)
    windows(count, third)
    r.gpos_out[...] = r.gpos[...]
    for w in range(count):
        store_out(w).wait()
        store_gin(w).wait()


def vectors_from(r, dp_count, z_count, rows):
    devices = dp_count * z_count * 2
    per_row = LANES // rows
    ff_rows = r.eb.shape[1] // devices
    per_row_ff = LANES // ff_rows

    def block(d):
        return r.small[d // (2 * z_count), (d // 2) % z_count, d % 2].astype(F32)

    for g in range(devices // per_row):
        added = block(g * per_row)[:8]
        for d in range(g * per_row + 1, (g + 1) * per_row):
            added = added + block(d)[:8]
        r.vec[:, g * LANES : (g + 1) * LANES] = added
    for g in range(devices // per_row_ff):
        added = block(g * per_row_ff)[8:9]
        for d in range(g * per_row_ff + 1, (g + 1) * per_row_ff):
            added = added + block(d)[8:9]
        r.eb[:, g * LANES : (g + 1) * LANES] = added


def place_small(r, place):
    rows, ff_rows = r.vec0.shape[1], r.ebs.shape[1]
    me = (place.dp * place.z_count + place.z) * 2 + place.c

    def spread(n):
        at = lax.rem(me, LANES // n) * n
        source = lax.broadcasted_iota(jnp.int32, (n, LANES), 0)
        target = lax.broadcasted_iota(jnp.int32, (n, LANES), 1)
        return jnp.where(target == source + at, 1.0, 0.0).astype(BF)

    for i in range(8):
        r.eight[i : i + 1, :] = getattr(r, "vec" + str(i))[...].astype(F32)
    r.small_low[0:8, :] = nn(r.eight[...].astype(BF), spread(rows)).astype(BF)
    one = jnp.broadcast_to(r.ebs[...].astype(F32), (8, ff_rows)).astype(BF)
    r.small_low[8:16, :] = nn(one, spread(ff_rows)).astype(BF)


def whole_kernel(counts, names, *refs):
    r = Refs(**dict(zip(names, refs)))
    count = r.x.shape[0]
    rows = r.wq_shard.shape[0]
    place = Place(*counts)
    load, store_out, store_gin = io_copies(r, count)
    for w in range(count):
        for copy in load(w):
            copy.start()
    place_small(r, place)
    gathers = {}
    for name in EARLY + LATE:
        shard = r.small_low if name == "small" else getattr(r, name + "_shard")
        sems = (getattr(r, name + "_send"), getattr(r, name + "_recv"))
        gathers[name] = Gather(place, shard, getattr(r, name), sems)
    early = [gathers[name] for name in EARLY]
    late = [gathers[name] for name in LATE]
    place.barrier()
    for job in early + late:
        job.start_z()
    zero_sums(r)
    for job in early:
        job.start_dp()
    for job in early:
        job.pass_on()
    for job in early:
        job.start_core()
    for job in late:
        job.start_dp()
    for job in early[:3]:
        job.finish()
    r.pos[...] = flat(r.post[...]).T
    vectors_from(r, counts[0], counts[1], rows)
    for w in range(count):
        for copy in load(w):
            copy.wait()
    windows(count, lambda w: hidden_and_keys(w, r))
    for job in early[3:]:
        job.finish()

    wm, we, ws = late
    first_plan = ((1, (wm.pass_on, we.pass_on)), (3, (ws.pass_on, wm.start_core)))

    def first_body(w):
        at_window(w, first_plan)
        attention_forward(w, r)

    windows(count, first_body)
    we.start_core()
    ws.start_core()
    finish_parking(r)
    for job in late:
        job.finish()

    def second_body(w):
        feed_forward(w, 0, r)
        store_out(w).start()

    windows(count, second_body)

    scatters = {}
    for job in early + late:
        job.drain()
    for name in GRADS + ("gpost",):
        total = r.mask if name == "gpost" else getattr(r, name)
        if name.startswith("gqkv"):
            group, size = int(name[-1]), getattr(r, name).shape[1]
            out = r.we.at[:, :, 1, :, pl.ds(group * size, size)]
        else:
            out = getattr(r, "post" if name == "gpost" else "w" + name[2:]).at[:, :, 0]
        setattr(r, name + "_out", out)
        bufs = [out] + [getattr(r, name + tail) for tail in ("_core", "_dp", "_z")]
        sems = (getattr(r, name + "_send"), getattr(r, name + "_recv"))
        scatters[name] = Scatter(place, total, getattr(r, name + "_result"), bufs, sems)
    sums = SumAll(
        place, r.gsmall, r.gsmall_result, (r.gsmall_dp, r.gsmall_z, r.gsmall_in), (r.gsmall_send, r.gsmall_recv)
    )
    gws, gwe, gwm = (scatters[name] for name in ("gws", "gwe", "gwm"))
    early_qkv, late_qkv, post = (scatters[name] for name in ("gqkv0", "gqkv1", "gpost"))
    gwm.start_core()

    def after(item):
        if item == 1:
            gwm.start_dp()
        if item == 3:
            gws.start_core()
            gwm.pass_on()
        if item == 5:
            gwm.start_z()
        if item == 6:
            gws.start_dp()
        if item == 7:
            gwe.start_core()

    weight_sums(r, lambda item, value: emit_halves(r, place, item, value), after)

    plans = (
        ((1, (gws.pass_on,)), (2, (gwe.start_dp,)), (3, (gws.start_z,))),
        ((1, (early_qkv.start_dp,)), (2, (gwe.start_z,)), (3, (early_qkv.pass_on,))),
        ((2, (late_qkv.start_dp,)),),
    )

    def heads_body(group):
        def body(w):
            at_window(w, plans[group])
            attention_backward(w, group, r)

        return body

    windows(count, heads_body(0))
    projection_sums(0, r)
    early_qkv.start_core()
    gwe.pass_on()
    windows(count, heads_body(1))
    projection_sums(1, r)
    late_qkv.start_core()
    early_qkv.start_z()

    def last_body(w):
        at_window(w, plans[2])
        hidden_back(w, r)
        store_gin(w).start()

    windows(count, last_body)
    r.mask[...] = r.gpos[...].T
    post.start_core()
    ff_rows = r.geb.shape[1] // r.gvec.shape[1]
    width = r.gvec.shape[1]
    r.gsmall[0:8, :] = r.gvec[...]
    r.gsmall[8:16, :] = jnp.zeros((8, width), F32)
    for i in range(ff_rows):
        r.gsmall[8 + i : 9 + i, :] = r.geb[:, i * width : (i + 1) * width]
    sums.start_core()
    late_qkv.pass_on()
    post.start_dp()
    sums.start_dp()
    post.pass_on()
    late_qkv.start_z()
    sums.start_z()
    post.start_z()
    everyone = [gws, gwe, gwm, early_qkv, late_qkv, sums, post]
    for job in everyone:
        job.finish()
    for job in everyone:
        job.drain()
    for w in range(count):
        store_out(w).wait()
        store_gin(w).wait()


def unpack_kernel(counts, names, *refs):
    r = Refs(**dict(zip(names, refs)))
    count = r.out.shape[0]
    loads, stores = [], []
    for w in range(count):
        for i, name in enumerate(("out", "gin")):
            source, target = getattr(r, name + "_in").at[w], getattr(r, name).at[w]
            loads.append(pltpu.make_async_copy(source, r.held.at[i, w], r.sem.at[0, i, w]))
            stores.append(pltpu.make_async_copy(r.held.at[i, w], target, r.sem.at[1, i, w]))
    for copy in loads:
        copy.start()
    for load, store in zip(loads, stores):
        load.wait()
        store.start()
    for name in GRADS[:3]:
        getattr(r, name)[...] = getattr(r, name + "_in")[...]
    size = r.gwq.shape[1] // GROUPS
    for group in range(GROUPS):
        source = getattr(r, "gqkv" + str(group) + "_in")
        for at, name in enumerate(("gwq", "gwk", "gwv")):
            getattr(r, name)[:, group * size : (group + 1) * size] = source[:, at * size : (at + 1) * size]
    r.gpos[...] = r.gpost_in[...].T
    place = Place(*counts)
    me = (place.dp * place.z_count + place.z) * 2 + place.c
    rows, ff_rows = r.gvec.shape[1], r.geb.shape[1]
    width = r.gsmall_in.shape[1]
    turned = pltpu.roll(r.gsmall_in[0:8, :], width - me * rows, axis=1)
    r.gvec[...] = turned[:, :rows]
    start = me * ff_rows
    lines = r.gsmall_in[8:16, :]
    line_at = lax.broadcasted_iota(jnp.int32, (8, width), 0)
    line = jnp.sum(jnp.where(line_at == start // width, lines, 0.0), axis=0, keepdims=True)
    line = jnp.broadcast_to(line, (8, width))
    r.geb[...] = pltpu.roll(line, width - lax.rem(start, width), axis=1)[0:1, :ff_rows]
    for copy in stores:
        copy.wait()


def call(kernel, name, ins, outs, scratch, **params):
    names = tuple(ins) + tuple(outs) + tuple(scratch)
    spec = lambda space: pl.BlockSpec(memory_space=space)
    results = pl.pallas_call(
        functools.partial(kernel, names),
        out_shape=tuple(shape for shape, _ in outs.values()),
        in_specs=[spec(space) for _, space in ins.values()],
        out_specs=tuple(spec(space) for _, space in outs.values()),
        scratch_shapes=list(scratch.values()),
        compiler_params=pltpu.CompilerParams(vmem_limit_bytes=63 * 2**20, **params),
        name=name,
    )(*[value for value, _ in ins.values()])
    return dict(zip(outs, results))


def local(dp_count, fsdp_count, inputs, lengths, grad_out, *params):
    micro, per_micro, seq, width = inputs.shape
    count = micro * per_micro
    wq, wk, wv, wm, we, ws, pos = params[:7]
    bq, bv, bm, eb, bs, g1, s1, g2, s2 = params[7:]
    ff = we.shape[1]
    rows, ff_rows = wq.shape[0], ws.shape[0]
    vectors = (bq, bv, bm, bs, g1, s1, g2, s2)
    vm, hbm = pltpu.VMEM, pl.ANY
    shape_of = jax.ShapeDtypeStruct
    merged = lambda a: a.reshape((count,) + a.shape[2:])
    act = shape_of((count, seq, width), BF)
    kept = shape_of((3, 4, count, seq, width), BF)
    data = dict(
        lens=(lengths, pltpu.SMEM), x_in=(merged(inputs), hbm), go_in=(merged(grad_out), hbm)
    )
    scratch = work_scratch(count, seq, width, ff)
    if dp_count == 4 and fsdp_count % 2 == 0 and rows % 16 == 0 and LANES % rows == 0 and LANES % ff_rows == 0:
        counts = (dp_count, fsdp_count // 2)
        lead = (dp_count, fsdp_count // 2, 2)
        shards = dict(wq=wq, wk=wk, wv=wv, wm=wm, we=we, ws=ws, post=pos.T)
        ins = dict(data)
        for name, shard in shards.items():
            ins[name + "_shard"] = (shard, vm)
        for i, vector in enumerate(vectors):
            ins["vec" + str(i)] = (vector[None], vm)
        ins["ebs"] = (eb[None], vm)
        outs = dict(out=(act, hbm), gin=(act, hbm), kept=(kept, hbm))
        part = shape_of((rows, 3 * width // GROUPS), F32)
        results = dict(gqkv0=part, gqkv1=part, gwm=wm, gwe=we, gws=ws, gpost=pos.T)
        for name, like in results.items():
            outs[name + "_result"] = (shape_of(like.shape, F32), vm)
        outs["gsmall_result"] = (shape_of((16, width), F32), vm)
        hops = hop_count(*counts)
        pair = lambda name: {name + tail: pltpu.SemaphoreType.DMA((hops,)) for tail in ("_send", "_recv")}
        for name, shard in shards.items():
            scratch[name] = vm(lead + shard.shape, BF)
            scratch.update(pair(name))
        scratch["small"] = vm(lead + (16, LANES), BF)
        scratch["eight"] = vm((8, rows), F32)
        scratch["small_low"] = vm((16, LANES), BF)
        scratch["pos"] = vm((seq, width), BF)
        scratch["vec"] = vm((8, width), F32)
        scratch["eb"] = vm((1, ff), F32)
        scratch["gvec"] = vm((8, width), F32)
        scratch["geb"] = vm((1, ff), F32)
        scratch.update(pair("small"))
        scratch.update(pair("gsmall"))
        for name, like in results.items():
            if name in ("gws", "gwe"):
                scratch[name] = vm(lead[:2] + like.shape, F32)
            elif name != "gpost":
                scratch[name] = vm((like.shape[0] * dp_count * fsdp_count, like.shape[1]), F32)
            scratch[name + "_core"] = vm(lead[:2] + like.shape, BF)
            scratch[name + "_dp"] = vm((3,) + lead[1:2] + like.shape, BF)
            scratch[name + "_z"] = vm((lead[1] - 1,) + like.shape, BF)
            scratch.update(pair(name))
        for tail in ("", "_dp", "_z"):
            scratch["gsmall" + tail] = vm((16, width), F32)
        scratch["gsmall_in"] = vm((hops, 16, width), F32)
        got = call(
            functools.partial(whole_kernel, counts), "layer", ins, outs, scratch,
            collective_id=0, has_side_effects=True,
        )
        ins = {}
        for name in ("out", "gin"):
            ins[name + "_in"] = (got[name], hbm)
        for name in GRADS + ("gpost", "gsmall"):
            ins[name + "_in"] = (got[name + "_result"], vm)
        outs = dict(out=(act, hbm), gin=(act, hbm))
        for name, like in dict(gwq=wq, gwk=wk, gwv=wv, gwm=wm, gwe=we, gws=ws).items():
            outs[name] = (shape_of(like.shape, F32), vm)
        outs["gpos"] = (shape_of(pos.shape, F32), vm)
        outs["gvec"] = (shape_of((8, rows), F32), vm)
        outs["geb"] = (shape_of((1, ff_rows), F32), vm)
        got = call(
            functools.partial(unpack_kernel, counts), "unpack", ins, outs,
            dict(held=vm((2,) + act.shape, BF), sem=pltpu.SemaphoreType.DMA((2, 2, count))),
        )
        gvec, geb, gpos = got["gvec"], got["geb"][0], got["gpos"]
        grads = got
    else:
        lead = (4, 4, 2)
        cut = lambda a: a.reshape(lead + (-1, a.shape[-1]))
        gather = lambda a, axis=0: lax.all_gather(a, AXES, axis=axis, tiled=True)
        share = lambda a, axis=0: lax.psum_scatter(a, AXES, scatter_dimension=axis, tiled=True)
        ins = dict(data)
        for name, shard in dict(wq=wq, wk=wk, wv=wv, wm=wm, we=we, ws=ws).items():
            ins[name] = (cut(gather(shard)), vm)
        ins["pos"] = (gather(pos, 1), vm)
        ins["vec"] = (jnp.stack([gather(a).astype(F32) for a in vectors]), vm)
        ins["eb"] = (gather(eb).astype(F32)[None], vm)
        outs = dict(out=(act, hbm), gin=(act, hbm), kept=(kept, hbm))
        for name, shape in dict(gws=(ff, width), gwe=(width, ff), gwm=(width, width)).items():
            outs[name] = (shape_of(shape, F32), vm)
        for group in range(GROUPS):
            outs["gqkv" + str(group)] = (shape_of((width, 3 * width // GROUPS), F32), vm)
        outs["gpos_out"] = (shape_of((seq, width), F32), vm)
        outs["gvec"] = (shape_of((8, width), F32), vm)
        outs["geb"] = (shape_of((1, ff), F32), vm)
        got = call(alone_kernel, "layer_alone", ins, outs, scratch)
        size = width // GROUPS
        for at, name in enumerate(("gwq", "gwk", "gwv")):
            parts = [got["gqkv" + str(g)][:, at * size : (at + 1) * size] for g in range(GROUPS)]
            got[name] = jnp.concatenate(parts, axis=1)
        grads = {name: share(got[name]) for name in ("gwq", "gwk", "gwv", "gwm", "gwe", "gws")}
        gpos = share(got["gpos_out"], 1)
        gvec = [share(got["gvec"][i]) for i in range(8)]
        geb = share(got["geb"][0])
    gbq, gbv, gbm, gbs, gg1, gs1, gg2, gs2 = (gvec[i] for i in range(8))
    return (
        got["out"].reshape(inputs.shape), got["gin"].reshape(inputs.shape),
        grads["gwq"], grads["gwk"], grads["gwv"], grads["gwm"], grads["gwe"], grads["gws"], gpos,
        gbq, gbv, gbm, geb, gbs, gg1, gs1, gg2, gs2,
    )


def solution(mesh):
    batch = P(None, AXES, None, None)
    matrix, vector, table = P(AXES, None), P(AXES), P(None, AXES)
    weights = (matrix,) * 6 + (table,) + (vector,) * 9
    return jax.shard_map(
        functools.partial(local, mesh.shape["dp"], mesh.shape["fsdp"]),
        mesh=mesh,
        in_specs=(batch, P(None, AXES), batch) + weights,
        out_specs=(batch, batch) + weights,
        check_vma=False,
    )
```

```python
import functools

import jax
import jax.numpy as jnp
from jax import lax
from jax.experimental import pallas as pl
from jax.experimental.pallas import tpu as pltpu
from jax.sharding import PartitionSpec as P

HEADS = 8
EPS = 1e-05
BF = jnp.bfloat16
F32 = jnp.float32
GELU_C = 0.7978845608028654
GELU_A = 0.044715
AXES = ("dp", "fsdp")
LANES = 128
MESH = pl.DeviceIdType.MESH
FF_PARTS = 1
GROUPS = 2

(BQ, BV, BM, BS, G1, S1, G2, S2) = range(8)
(Q, K, V, LOW) = range(4)


class Refs:
    def __init__(self, **kw):
        self.__dict__.update(kw)


def nn(a, b):
    return lax.dot_general(a, b, (((1,), (0,)), ((), ())), preferred_element_type=F32)


def nt(a, b):
    return lax.dot_general(a, b, (((1,), (1,)), ((), ())), preferred_element_type=F32)


def tn(a, b):
    return lax.dot_general(a, b, (((0,), (0,)), ((), ())), preferred_element_type=F32)


def flat(value):
    return value.reshape(-1, value.shape[-1])


def add_into(ref, value):
    ref[...] += value.reshape(ref.shape)


def add_row(ref, index, value):
    ref[index : index + 1, :] += jnp.sum(value, axis=0, keepdims=True)


def length_of(w, r):
    per_micro = r.lens.shape[1]
    return r.lens[w // per_micro, lax.rem(w, per_micro)]


def make_mask(w, r):
    seq = r.x.shape[1]
    key_at = lax.broadcasted_iota(jnp.int32, (seq, seq), 0)
    query_at = lax.broadcasted_iota(jnp.int32, (seq, seq), 1)
    ok = (key_at <= query_at) & (key_at < length_of(w, r))
    r.mask[...] = jnp.where(ok, 0.0, -1e30)


def make_causal(r):
    size = r.causal.shape[0]
    key_at = lax.broadcasted_iota(jnp.int32, (size, size), 0)
    query_at = lax.broadcasted_iota(jnp.int32, (size, size), 1)
    r.causal[...] = jnp.where(key_at <= query_at, 0.0, -1e30)


def hidden_and_keys(w, r):
    low = (r.x[w].astype(F32) + r.pos[...].astype(F32)).astype(BF)
    r.ab[LOW, w] = low
    r.ab[K, w] = nn(low, flat(r.wk[...])).astype(BF)


def attention_forward(w, r):
    seq, width = r.x.shape[1:]
    half = seq // 2
    head = width // HEADS
    low = r.ab[LOW, w]
    queries = (nn(low, flat(r.wq[...])) + r.vec[BQ : BQ + 1, :]).astype(BF)
    r.ab[Q, w] = (queries.astype(F32) * (head**-0.5)).astype(BF)
    values = (nn(low, flat(r.wv[...])) + r.vec[BV : BV + 1, :]).astype(BF)
    r.ab[V, w] = values
    r.vt[...] = values.T
    make_mask(w, r)
    lane = lax.broadcasted_iota(jnp.int32, (seq, 2 * head), 1)
    for h in range(HEADS):
        pair = slice((h // 2) * 2 * head, (h // 2 + 1) * 2 * head)
        mine = (lane < head) if h % 2 == 0 else (lane >= head)
        qh = jnp.where(mine, r.ab[Q, w, :, pair], jnp.zeros((), BF))
        kp = r.ab[K, w, :, pair]
        s0 = nt(kp[:half], qh) + r.mask[:half, :]
        s1 = nt(kp[half:], qh[half:]) + r.mask[half:, half:]
        m_left = jnp.max(s0[:, :half], axis=0, keepdims=True)
        m_right = jnp.maximum(
            jnp.max(s0[:, half:], axis=0, keepdims=True), jnp.max(s1, axis=0, keepdims=True)
        )
        top = jnp.concatenate([m_left, m_right], axis=1)
        e0 = jnp.exp(s0 - top)
        e1 = jnp.exp(s1 - m_right)
        n_all = jnp.sum(e0, axis=0, keepdims=True)
        n_right = n_all[:, half:] + jnp.sum(e1, axis=0, keepdims=True)
        total = jnp.concatenate([n_all[:, :half], n_right], axis=1)
        query_at = lax.broadcasted_iota(jnp.int32, (1, seq), 1)
        r.logt[w, h : h + 1, :] = jnp.where(query_at < length_of(w, r), top + jnp.log(total), 1e30)
        inv = 1.0 / total
        p0 = (e0 * inv).astype(BF)
        p1 = (e1 * inv[:, half:]).astype(BF)
        vt = r.vt[h * head : (h + 1) * head, :]
        o_left = nn(vt[:, :half], p0[:, :half])
        o_right = nn(vt, jnp.concatenate([p0[:, half:], p1], axis=0))
        r.ot[h * head : (h + 1) * head, :half] = o_left.astype(BF)
        r.ot[h * head : (h + 1) * head, half:] = o_right.astype(BF)
    r.mixed[w] = r.ot[...].T
    for i in range(4):
        park_copy(r, i, w).start()


def norm_parts(total):
    center = total - jnp.mean(total, -1, keepdims=True)
    spread = jnp.mean(center * center, -1, keepdims=True)
    inv = lax.rsqrt(spread + EPS)
    return center * inv, inv


def norm_back(e, xhat, inv):
    return inv * (
        e - jnp.mean(e, -1, keepdims=True) - xhat * jnp.mean(e * xhat, -1, keepdims=True)
    )


def slot_of(kind, w, c):
    return (kind + 2 * lax.rem(w, 2), c)


def part_copy(r, kind, w, part, c, rows):
    here = slice(part * rows, (part + 1) * rows)
    target = r.kept.at[1 + kind, c, w]
    return pltpu.make_async_copy(r.ab.at[slot_of(kind, w, c)], target, r.part_sem.at[kind, lax.rem(w, 2), c])


def park_copy(r, i, w):
    return pltpu.make_async_copy(r.ab.at[i, w], r.kept.at[0, i, w], r.park_sem.at[i, w])


def finish_parking(r):
    for i in range(4):
        for w in range(r.x.shape[0]):
            park_copy(r, i, w).wait()


def block_load(r, kind, c, buffer):
    return pltpu.make_async_copy(r.kept.at[kind, c], r.ab.at[buffer], r.load_sem.at[buffer])


BUFFERS = (2, 3, 0, 1, 2, 0, 1, 3)
FOLLOWS = {0: (2, 0), 1: (2, 3), 2: (2, 1), 3: (2, 2), 4: (0, 2), 5: (0, 0), 6: (0, 1), 7: (0, 3)}


def weight_sums(r, emit, after):
    count = r.x.shape[0]
    rows, chunks = r.slope.shape[0], r.ws.shape[0]
    for kind in range(2):
        for part in range(FF_PARTS):
            for c in range(chunks):
                part_copy(r, kind, count - 2, part, c, rows).wait()
                part_copy(r, kind, count - 1, part, c, rows).wait()
    for item in range(4):
        block_load(r, 1, item, BUFFERS[item]).start()
    for item in range(2 * chunks):
        buffer, c = BUFFERS[item], item % chunks
        block_load(r, 1 + item // chunks, c, buffer).wait()
        block = flat(r.ab[buffer])
        if item < chunks:
            emit(item, tn(block, flat(r.gff[...])))
        else:
            emit(item, tn(flat(r.nl[...]), block))
        block_load(r, *FOLLOWS[item], buffer).start()
        after(item)
    for buffer in range(4):
        block_load(r, 0, buffer, buffer).wait()


def feed_forward(w, part, r):
    rows, width = r.slope.shape[0], r.x.shape[-1]
    here = slice(part * rows, (part + 1) * rows)
    chunks = r.ws.shape[0]
    chunk = r.we.shape[-1] // chunks

    @pl.when(w > 1)
    def _():
        for kind in range(2):
            for c in range(chunks):
                part_copy(r, kind, w - 2, part, c, rows).wait()

    hid = r.x[w, here, :].astype(F32) + r.pos[here, :].astype(F32)
    first = hid + (nn(r.mixed[w, here, :], flat(r.wm[...])) + r.vec[BM : BM + 1, :])
    xhat1, inv1 = norm_parts(first)
    r.xh1[...] = xhat1
    normed = xhat1 * r.vec[G1 : G1 + 1, :] + r.vec[S1 : S1 + 1, :]
    r.nl[w, here, :] = normed.astype(BF)
    ff_out = None
    for c in range(chunks):
        cols = slice(c * chunk, (c + 1) * chunk)
        t = nn(r.nl[w, here, :], flat(r.we[..., cols])) + r.eb[:, cols]
        t2 = t * t
        th = jnp.tanh(t * (t2 * (GELU_A * GELU_C) + GELU_C))
        ht = 0.5 * t
        act = (ht * th + ht).astype(BF)
        slot = slot_of(0, w, c)
        r.ab[slot] = act
        slope = (0.5 * th + 0.5) + ht * (1.0 - th * th) * (t2 * (3 * GELU_A * GELU_C) + GELU_C)
        r.slope[:, cols] = slope
        part_out = nn(act, flat(r.ws[c]))
        ff_out = part_out if ff_out is None else ff_out + part_out
    second = normed + (ff_out + r.vec[BS : BS + 1, :])
    xhat2, inv2 = norm_parts(second)
    row_at = part * rows + lax.broadcasted_iota(jnp.int32, (rows, width), 0)
    cot = jnp.where(row_at < length_of(w, r), r.go[w, here, :].astype(F32), 0.0)
    r.go[w, here, :] = (xhat2 * r.vec[G2 : G2 + 1, :] + r.vec[S2 : S2 + 1, :]).astype(BF)
    add_row(r.gvec, G2, cot * xhat2)
    add_row(r.gvec, S2, cot)
    d_second = norm_back(cot * r.vec[G2 : G2 + 1, :], xhat2, inv2)
    gff = d_second.astype(BF)
    r.gff[w, here, :] = gff
    add_row(r.gvec, BS, gff.astype(F32))
    d_normed = d_second
    for c in range(chunks):
        cols = slice(c * chunk, (c + 1) * chunk)
        gpre = (nt(r.gff[w, here, :], flat(r.ws[c])) * r.slope[:, cols]).astype(BF)
        r.geb[:, cols] += jnp.sum(gpre.astype(F32), axis=0, keepdims=True)
        slot = slot_of(1, w, c)
        r.ab[slot] = gpre
        d_normed = d_normed + nt(gpre, flat(r.we[..., cols]))
    xhat1 = r.xh1[...]
    add_row(r.gvec, G1, d_normed * xhat1)
    add_row(r.gvec, S1, d_normed)
    d_first = norm_back(d_normed * r.vec[G1 : G1 + 1, :], xhat1, inv1)
    r.dfirst[w, here, :] = d_first
    gattn = d_first.astype(BF)
    add_row(r.gvec, BM, gattn.astype(F32))
    mixed = r.mixed[w, here, :]
    add_into(r.gwm, tn(mixed, gattn))
    gmix = nt(gattn, flat(r.wm[...])).astype(BF)
    head = width // HEADS
    prod = gmix.astype(F32) * mixed.astype(F32)
    hi = prod.astype(BF)
    lo = (prod - hi.astype(F32)).astype(BF)
    sel_row = lax.broadcasted_iota(jnp.int32, (16, width), 0)
    sel_col = lax.broadcasted_iota(jnp.int32, (16, width), 1)
    sel = jnp.where(sel_col // head == sel_row, 1.0, 0.0).astype(BF)
    r.delta[w, :, here] = nt(sel, hi) + nt(sel, lo)
    r.mixed[w, here, :] = gmix
    for kind in range(2):
        for c in range(chunks):
            part_copy(r, kind, w, part, c, rows).start()


def attention_backward(w, group, r):
    seq, width = r.x.shape[1:]
    half = seq // 2
    head = width // HEADS
    scale = head**-0.5
    cols = slice(group * (width // GROUPS), (group + 1) * (width // GROUPS))
    r.vt[cols, :] = r.ab[K, w, :, cols].T
    lane = lax.broadcasted_iota(jnp.int32, (seq, 2 * head), 1)
    pairs = HEADS // 2 // GROUPS
    for p in range(group * pairs, (group + 1) * pairs):
        pair = slice(p * 2 * head, (p + 1) * 2 * head)
        kp = r.ab[K, w, :, pair]
        vp = r.ab[V, w, :, pair]
        sums = None
        for odd in range(2):
            h = 2 * p + odd
            mine = (lane >= head) if odd else (lane < head)
            qh = jnp.where(mine, r.ab[Q, w, :, pair], jnp.zeros((), BF))
            gh = jnp.where(mine, r.mixed[w, :, pair], jnp.zeros((), BF))
            logt = r.logt[w, h : h + 1, :]
            delta = r.delta[w, h : h + 1, :]
            s0 = nt(kp[:half], qh)
            s0 = jnp.concatenate([s0[:, :half] + r.causal[...], s0[:, half:]], axis=1)
            p0 = jnp.exp(s0 - logt)
            p1 = jnp.exp(nt(kp[half:], qh[half:]) + r.causal[...] - logt[:, half:])
            d0 = (p0 * (nt(vp[:half], gh) - delta)).astype(BF)
            d1 = (p1 * (nt(vp[half:], gh[half:]) - delta[:, half:])).astype(BF)
            p0 = p0.astype(BF)
            p1 = p1.astype(BF)
            parts = (nn(d0, qh), nn(d1, qh[half:]), nn(p0, gh), nn(p1, gh[half:]))
            sums = parts if sums is None else tuple(a + b for a, b in zip(sums, parts))
            kt = r.vt[h * head : (h + 1) * head, :]
            q_left = nn(kt[:, :half], d0[:, :half])
            q_right = nn(kt, jnp.concatenate([d0[:, half:], d1], axis=0))
            r.ot[h * head : (h + 1) * head, :half] = (q_left * scale).astype(BF)
            r.ot[h * head : (h + 1) * head, half:] = (q_right * scale).astype(BF)
        grads = [part.astype(BF) for part in sums]
        r.ab[K, w, :half, pair] = grads[0]
        r.ab[K, w, half:, pair] = grads[1]
        r.ab[V, w, :half, pair] = grads[2]
        r.ab[V, w, half:, pair] = grads[3]
        gq = r.ot[pair, :].T
        r.ab[Q, w, :, pair] = gq
        r.gvec[BQ : BQ + 1, pair] += jnp.sum(gq.astype(F32), axis=0, keepdims=True)
        gv = grads[2].astype(F32) + grads[3].astype(F32)
        r.gvec[BV : BV + 1, pair] += jnp.sum(gv, axis=0, keepdims=True)


def projection_sums(group, r):
    width = r.x.shape[-1]
    size = width // GROUPS
    cols = slice(group * size, (group + 1) * size)
    total = getattr(r, "gqkv" + str(group))
    for at, kind in enumerate((Q, K, V)):
        total[:, at * size : (at + 1) * size] = tn(flat(r.ab[LOW]), flat(r.ab[kind, :, :, cols]))


def hidden_back(w, r):
    d_hidden = (
        r.dfirst[w]
        + nt(r.ab[Q, w], flat(r.wq[...]))
        + nt(r.ab[K, w], flat(r.wk[...]))
        + nt(r.ab[V, w], flat(r.wv[...]))
    )
    r.gpos[...] += d_hidden
    r.x[w] = d_hidden.astype(BF)


def windows(count, body):
    def step(w, carry):
        body(w)
        return carry

    lax.fori_loop(0, count, step, 0)


def at_window(w, plan):
    for index, steps in plan:

        @pl.when(w == index)
        def _():
            for step in steps:
                step()


class Place:
    def __init__(self, dp_count, z_count):
        self.dp_count, self.z_count = dp_count, z_count
        self.dp = lax.axis_index("dp")
        fsdp = lax.axis_index("fsdp")
        self.z, self.c = fsdp // 2, lax.rem(fsdp, 2)
        self.near = (self.dp, self.z * 2 + (1 - self.c))

    def z_at(self, shift):
        return lax.rem(self.z + shift + self.z_count, self.z_count)

    def dp_flip(self, bit):
        low, high = lax.rem(self.dp, 2), self.dp // 2
        if bit in (0, 2):
            low = 1 - low
        if bit in (1, 2):
            high = 1 - high
        return high * 2 + low

    def along_z(self, shift):
        return (self.dp, self.z_at(shift) * 2 + self.c)

    def along_dp(self, bit):
        return (self.dp_flip(bit), self.z * 2 + self.c)

    def barrier(self):
        sem = pltpu.get_barrier_semaphore()
        everyone = [self.near] + [self.along_z(s) for s in range(1, self.z_count)]
        everyone += [self.along_dp(bit) for bit in range(3)]
        for peer in everyone:
            pl.semaphore_signal(sem, inc=1, device_id=peer, device_id_type=MESH)
        pl.semaphore_wait(sem, len(everyone))


def remote(src, dst, sems, index, peer):
    send, recv = sems
    return pltpu.make_async_remote_copy(
        src_ref=src, dst_ref=dst, send_sem=send.at[index], recv_sem=recv.at[index],
        device_id=peer, device_id_type=MESH,
    )


def hop_count(dp_count, z_count):
    return (z_count - 1) + 10


def halves(ref):
    lanes = ref.shape[-1]
    if lanes % (2 * LANES):
        return ((0, slice(0, lanes)),)
    return ((0, slice(0, lanes // 2)), (1, slice(lanes // 2, lanes)))


class Gather:
    def __init__(self, place, shard, whole, sems):
        self.p, self.shard, self.whole, self.sems = place, shard, whole, sems
        self.base = place.z_count - 1

    def z_copy(self, shift, z):
        p = self.p
        return remote(self.shard, self.whole.at[p.dp, z, p.c], self.sems, shift - 1, p.along_z(shift))

    def own_copy(self, bit, owner):
        block = self.whole.at[owner, :, self.p.c]
        return remote(block, block, self.sems, self.base + bit, self.p.along_dp(bit))

    def far_copy(self, bit, lanes, owner):
        block = self.whole.at[owner, :, self.p.c, :, lanes]
        return remote(block, block, self.sems, self.base + 2 + bit, self.p.along_dp(1 - bit))

    def core_copy(self, core):
        half = self.whole.at[:, :, core]
        return remote(half, half, self.sems, self.base + 4, self.p.near)

    def start_z(self):
        p = self.p
        for shift in range(1, p.z_count):
            self.z_copy(shift, p.z).start()
        self.whole[p.dp, p.z, p.c] = self.shard[...]

    def start_dp(self):
        p = self.p
        for shift in range(1, p.z_count):
            self.z_copy(shift, p.z_at(-shift)).wait_recv()
        for bit in range(2):
            self.own_copy(bit, p.dp).start()

    def pass_on(self):
        p = self.p
        for bit in range(2):
            self.own_copy(bit, p.dp_flip(bit)).wait_recv()
        for bit, lanes in halves(self.whole):
            self.far_copy(bit, lanes, p.dp_flip(bit)).start()

    def start_core(self):
        p = self.p
        for bit, lanes in halves(self.whole):
            self.far_copy(bit, lanes, p.dp_flip(2)).wait_recv()
        self.core_copy(p.c).start()

    def finish(self):
        self.core_copy(1 - self.p.c).wait_recv()

    def drain(self):
        p = self.p
        for shift in range(1, p.z_count):
            self.z_copy(shift, p.z).wait_send()
        for bit in range(2):
            self.own_copy(bit, p.dp).wait_send()
        for bit, lanes in halves(self.whole):
            self.far_copy(bit, lanes, p.dp_flip(bit)).wait_send()
        self.core_copy(p.c).wait_send()


class Scatter:
    def __init__(self, place, total, result, bufs, sems):
        self.p, self.total, self.result, self.sems = place, total, result, sems
        self.out, self.from_core, self.from_dp, self.from_z = bufs
        self.base = place.z_count - 1

    pieces = ((slice(None), slice(None)),)

    def core_copy(self, piece):
        at = self.pieces[piece]
        return remote(self.out.at[at], self.from_core.at[at], self.sems, self.base + 6 + piece, self.p.near)

    def dp_copy(self, slot, bit, lanes):
        p = self.p
        block = p.dp_flip((2, bit, 1 - bit)[slot])
        return remote(
            self.out.at[block, :, :, lanes], self.from_dp.at[slot, :, :, lanes], self.sems,
            self.base + 2 * slot + bit, p.along_dp((bit, bit, 1 - bit)[slot]),
        )

    def z_copy(self, shift):
        p = self.p
        block = self.out.at[p.dp, p.z_at(shift)]
        return remote(block, self.from_z.at[shift - 1], self.sems, shift - 1, p.along_z(shift))

    def blocks(self, body):
        p = self.p

        def step(at, carry):
            body(at // p.z_count, lax.rem(at, p.z_count))
            return carry

        lax.fori_loop(0, p.dp_count * p.z_count, step, 0)

    def rows_at(self, d, z, core):
        size = self.result.shape[0]
        start = ((d * self.p.z_count + z) * 2 + core) * size
        return self.total.at[pl.ds(pl.multiple_of(start, size), size)]

    def mine(self, d, z):
        if len(self.total.shape) == 4:
            return self.total.at[d, z]
        return self.rows_at(d, z, self.p.c)

    def start_core(self):
        far = 1 - self.p.c

        def body(d, z):
            self.out[d, z] = self.rows_at(d, z, far)[...].astype(BF)

        self.blocks(body)
        self.core_copy(0).start()

    def start_dp(self):
        for piece in range(len(self.pieces)):
            self.core_copy(piece).wait_recv()
            self.core_copy(piece).wait_send()

        def body(d, z):
            mine = self.mine(d, z)
            both = mine[...] + self.from_core[d, z].astype(F32)
            mine[...] = both
            self.out[d, z] = both.astype(BF)

        self.blocks(body)
        for slot in range(2):
            for bit, lanes in halves(self.out):
                self.dp_copy(slot, bit, lanes).start()

    def pass_on(self):
        p = self.p
        for bit, lanes in halves(self.out):
            self.dp_copy(0, bit, lanes).wait_recv()
            other = p.dp_flip(1 - bit)
            for z in range(p.z_count):
                added = self.mine(other, z)[:, lanes] + self.from_dp[0, z, :, lanes].astype(F32)
                self.out[other, z, :, lanes] = added.astype(BF)
            self.dp_copy(2, bit, lanes).start()

    def start_z(self):
        p = self.p
        for slot in (1, 2):
            for bit, lanes in halves(self.out):
                self.dp_copy(slot, bit, lanes).wait_recv()
        for z in range(p.z_count):
            mine = self.mine(p.dp, z)
            added = mine[...] + self.from_dp[1, z].astype(F32) + self.from_dp[2, z].astype(F32)
            mine[...] = added
            self.out[p.dp, z] = added.astype(BF)
        for shift in range(1, p.z_count):
            self.z_copy(shift).start()

    def finish(self):
        p = self.p
        added = self.mine(p.dp, p.z)[...]
        for shift in range(1, p.z_count):
            self.z_copy(shift).wait_recv()
            added = added + self.from_z[shift - 1].astype(F32)
        self.result[...] = added

    def drain(self):
        for slot in range(3):
            for bit, lanes in halves(self.out):
                self.dp_copy(slot, bit, lanes).wait_send()
        for shift in range(1, self.p.z_count):
            self.z_copy(shift).wait_send()


class SumAll:
    def __init__(self, place, total, result, bufs, sems):
        self.p, self.total, self.result, self.sems = place, total, result, sems
        self.send_dp, self.send_z, self.landing = bufs

    def copies(self, hop):
        p = self.p
        base = p.z_count - 1
        if hop == 0:
            return [(base + 3, remote(self.total, self.landing.at[base + 3], self.sems, base + 3, p.near))]
        if hop == 1:
            return [
                (base + b, remote(self.send_dp, self.landing.at[base + b], self.sems, base + b, p.along_dp(b)))
                for b in range(3)
            ]
        return [
            (s - 1, remote(self.send_z, self.landing.at[s - 1], self.sems, s - 1, p.along_z(s)))
            for s in range(1, p.z_count)
        ]

    def arrived(self, hop, own):
        added = own[...]
        for slot, copy in self.copies(hop):
            copy.wait_recv()
            added = added + self.landing[slot]
        return added

    def start(self, hop):
        for _, copy in self.copies(hop):
            copy.start()

    def start_core(self):
        self.start(0)

    def start_dp(self):
        self.send_dp[...] = self.arrived(0, self.total)
        self.start(1)

    def pass_on(self):
        pass

    def start_z(self):
        self.send_z[...] = self.arrived(1, self.send_dp)
        self.start(2)

    def finish(self):
        self.result[...] = self.arrived(2, self.send_z)

    def drain(self):
        for hop in range(3):
            for _, copy in self.copies(hop):
                copy.wait_send()


WEIGHTS = ("wk", "wq", "wv", "wm", "we", "ws")
GRADS = ("gws", "gwe", "gwm", "gqkv0", "gqkv1")
EARLY = ("post", "small", "wk", "wq", "wv")
LATE = ("wm", "we", "ws")


def work_scratch(count, seq, width, ff):
    vm = pltpu.VMEM
    return dict(
        ab=vm((4, count, seq, width), BF),
        mixed=vm((count, seq, width), BF),
        dfirst=vm((count, seq, width), F32),
        logt=vm((count, HEADS, seq), F32),
        delta=vm((count, 16, seq), F32),
        vt=vm((width, seq), BF),
        ot=vm((width, seq), BF),
        mask=vm((seq, seq), F32),
        causal=vm((seq // 2, seq // 2), F32),
        xh1=vm((seq // FF_PARTS, width), F32),
        nl=vm((count, seq, width), BF),
        gff=vm((count, seq, width), BF),
        slope=vm((seq // FF_PARTS, ff), F32),
        gpos=vm((seq, width), F32),
        x=vm((count, seq, width), BF),
        go=vm((count, seq, width), BF),
        io_sem=pltpu.SemaphoreType.DMA((4, count)),
        part_sem=pltpu.SemaphoreType.DMA((2, 2, 4)),
        park_sem=pltpu.SemaphoreType.DMA((4, count)),
        load_sem=pltpu.SemaphoreType.DMA((4,)),
    )


def zero_sums(r):
    make_causal(r)
    for name in ("gwm", "gpos", "gvec", "geb"):
        ref = getattr(r, name)
        ref[...] = jnp.zeros(ref.shape, ref.dtype)


def io_copies(r, count):
    def load(w):
        return (
            pltpu.make_async_copy(r.x_in.at[w], r.x.at[w], r.io_sem.at[0, w]),
            pltpu.make_async_copy(r.go_in.at[w], r.go.at[w], r.io_sem.at[1, w]),
        )

    def store_out(w):
        return pltpu.make_async_copy(r.go.at[w], r.out.at[w], r.io_sem.at[2, w])

    def store_gin(w):
        return pltpu.make_async_copy(r.x.at[w], r.gin.at[w], r.io_sem.at[3, w])

    return load, store_out, store_gin


def emit_whole(r, item, value):
    size = value.shape[0]
    if item < r.ws.shape[0]:
        r.gws[item * size : (item + 1) * size, :] = value
    else:
        c = item - r.ws.shape[0]
        r.gwe[:, c * size : (c + 1) * size] = value


def emit_halves(r, place, item, value):
    r.mask[...] = value
    chunks, size = r.ws.shape[0], value.shape[0]
    if item < chunks:
        blocks = [((item, z), z) for z in range(place.z_count)]
        kept, sent, rows = r.gws, r.gws_out, r.gws.shape[2]
        cols = slice(None)
    else:
        blocks = [((d, z), d * place.z_count + z) for d in range(place.dp_count) for z in range(place.z_count)]
        kept, sent, rows = r.gwe, r.gwe_out, r.gwe.shape[2]
        cols = slice((item - chunks) * size, (item - chunks + 1) * size)
    for at, block in blocks:
        start = pl.multiple_of((block * 2 + place.c) * rows, rows)
        kept[at + (slice(None), cols)] = r.mask[pl.ds(start, rows), :]
        start = pl.multiple_of((block * 2 + 1 - place.c) * rows, rows)
        sent[at + (slice(None), cols)] = r.mask[pl.ds(start, rows), :].astype(BF)


def alone_kernel(names, *refs):
    r = Refs(**dict(zip(names, refs)))
    count = r.x.shape[0]
    load, store_out, store_gin = io_copies(r, count)
    for w in range(count):
        for copy in load(w):
            copy.start()
    zero_sums(r)
    for w in range(count):
        for copy in load(w):
            copy.wait()

    def second(w):
        feed_forward(w, 0, r)
        store_out(w).start()

    def third(w):
        hidden_back(w, r)
        store_gin(w).start()

    windows(count, lambda w: hidden_and_keys(w, r))
    windows(count, lambda w: attention_forward(w, r))
    finish_parking(r)
    windows(count, second)
    weight_sums(r, lambda item, value: emit_whole(r, item, value), lambda item: None)
    for group in range(GROUPS):
        windows(count, lambda w: attention_backward(w, group, r))
        projection_sums(group, r)
    windows(count, third)
    r.gpos_out[...] = r.gpos[...]
    for w in range(count):
        store_out(w).wait()
        store_gin(w).wait()


def vectors_from(r, dp_count, z_count, rows):
    devices = dp_count * z_count * 2
    per_row = LANES // rows
    ff_rows = r.eb.shape[1] // devices
    per_row_ff = LANES // ff_rows

    def block(d):
        return r.small[d // (2 * z_count), (d // 2) % z_count, d % 2].astype(F32)

    for g in range(devices // per_row):
        added = block(g * per_row)[:8]
        for d in range(g * per_row + 1, (g + 1) * per_row):
            added = added + block(d)[:8]
        r.vec[:, g * LANES : (g + 1) * LANES] = added
    for g in range(devices // per_row_ff):
        added = block(g * per_row_ff)[8:9]
        for d in range(g * per_row_ff + 1, (g + 1) * per_row_ff):
            added = added + block(d)[8:9]
        r.eb[:, g * LANES : (g + 1) * LANES] = added


def place_small(r, place):
    rows, ff_rows = r.vec0.shape[1], r.ebs.shape[1]
    me = (place.dp * place.z_count + place.z) * 2 + place.c

    def spread(n):
        at = lax.rem(me, LANES // n) * n
        source = lax.broadcasted_iota(jnp.int32, (n, LANES), 0)
        target = lax.broadcasted_iota(jnp.int32, (n, LANES), 1)
        return jnp.where(target == source + at, 1.0, 0.0).astype(BF)

    for i in range(8):
        r.eight[i : i + 1, :] = getattr(r, "vec" + str(i))[...].astype(F32)
    r.small_low[0:8, :] = nn(r.eight[...].astype(BF), spread(rows)).astype(BF)
    one = jnp.broadcast_to(r.ebs[...].astype(F32), (8, ff_rows)).astype(BF)
    r.small_low[8:16, :] = nn(one, spread(ff_rows)).astype(BF)


def whole_kernel(counts, names, *refs):
    r = Refs(**dict(zip(names, refs)))
    count = r.x.shape[0]
    rows = r.wq_shard.shape[0]
    place = Place(*counts)
    load, store_out, store_gin = io_copies(r, count)
    for w in range(count):
        for copy in load(w):
            copy.start()
    place_small(r, place)
    gathers = {}
    for name in EARLY + LATE:
        shard = r.small_low if name == "small" else getattr(r, name + "_shard")
        sems = (getattr(r, name + "_send"), getattr(r, name + "_recv"))
        gathers[name] = Gather(place, shard, getattr(r, name), sems)
    early = [gathers[name] for name in EARLY]
    late = [gathers[name] for name in LATE]
    place.barrier()
    for job in early + late:
        job.start_z()
    zero_sums(r)
    for job in early:
        job.start_dp()
    for job in early:
        job.pass_on()
    for job in early:
        job.start_core()
    for job in late:
        job.start_dp()
    for job in early[:3]:
        job.finish()
    r.pos[...] = flat(r.post[...]).T
    vectors_from(r, counts[0], counts[1], rows)
    for w in range(count):
        for copy in load(w):
            copy.wait()
    windows(count, lambda w: hidden_and_keys(w, r))
    for job in early[3:]:
        job.finish()

    wm, we, ws = late
    first_plan = ((1, (wm.pass_on, we.pass_on)), (3, (ws.pass_on, wm.start_core)))

    def first_body(w):
        at_window(w, first_plan)
        attention_forward(w, r)

    windows(count, first_body)
    we.start_core()
    ws.start_core()
    finish_parking(r)
    for job in late:
        job.finish()

    def second_body(w):
        feed_forward(w, 0, r)
        store_out(w).start()

    windows(count, second_body)

    scatters = {}
    for job in early + late:
        job.drain()
    for name in GRADS + ("gpost",):
        total = r.mask if name == "gpost" else getattr(r, name)
        if name.startswith("gqkv"):
            group, size = int(name[-1]), getattr(r, name).shape[1]
            out = r.we.at[:, :, 1, :, pl.ds(group * size, size)]
        else:
            out = getattr(r, "post" if name == "gpost" else "w" + name[2:]).at[:, :, 0]
        setattr(r, name + "_out", out)
        bufs = [out] + [getattr(r, name + tail) for tail in ("_core", "_dp", "_z")]
        sems = (getattr(r, name + "_send"), getattr(r, name + "_recv"))
        scatters[name] = Scatter(place, total, getattr(r, name + "_result"), bufs, sems)
    sums = SumAll(
        place, r.gsmall, r.gsmall_result, (r.gsmall_dp, r.gsmall_z, r.gsmall_in), (r.gsmall_send, r.gsmall_recv)
    )
    gws, gwe, gwm = (scatters[name] for name in ("gws", "gwe", "gwm"))
    early_qkv, late_qkv, post = (scatters[name] for name in ("gqkv0", "gqkv1", "gpost"))
    gwm.start_core()
    chunks = counts[0]
    gws.pieces = tuple((c, slice(None)) for c in range(chunks))
    size = r.we.shape[-1] // chunks
    gwe.pieces = tuple(
        (slice(None), slice(None), slice(None), slice(c * size, (c + 1) * size)) for c in range(chunks)
    )

    def after(item):
        job = gws if item < chunks else gwe
        job.core_copy(item % chunks).start()
        if item == 1:
            gwm.start_dp()
        if item == 3:
            gwm.pass_on()
        if item == 5:
            gwm.start_z()
        if item == 6:
            gws.start_dp()

    weight_sums(r, lambda item, value: emit_halves(r, place, item, value), after)

    plans = (
        ((1, (gws.pass_on,)), (2, (gwe.start_dp,)), (3, (gws.start_z,))),
        ((1, (early_qkv.start_dp,)), (2, (gwe.start_z,)), (3, (early_qkv.pass_on,))),
        ((2, (late_qkv.start_dp,)),),
    )

    def heads_body(group):
        def body(w):
            at_window(w, plans[group])
            attention_backward(w, group, r)

        return body

    windows(count, heads_body(0))
    projection_sums(0, r)
    early_qkv.start_core()
    gwe.pass_on()
    windows(count, heads_body(1))
    projection_sums(1, r)
    late_qkv.start_core()
    early_qkv.start_z()

    def last_body(w):
        at_window(w, plans[2])
        hidden_back(w, r)
        store_gin(w).start()

    windows(count, last_body)
    r.mask[...] = r.gpos[...].T
    post.start_core()
    ff_rows = r.geb.shape[1] // r.gvec.shape[1]
    width = r.gvec.shape[1]
    r.gsmall[0:8, :] = r.gvec[...]
    r.gsmall[8:16, :] = jnp.zeros((8, width), F32)
    for i in range(ff_rows):
        r.gsmall[8 + i : 9 + i, :] = r.geb[:, i * width : (i + 1) * width]
    sums.start_core()
    late_qkv.pass_on()
    post.start_dp()
    sums.start_dp()
    post.pass_on()
    late_qkv.start_z()
    sums.start_z()
    post.start_z()
    everyone = [gws, gwe, gwm, early_qkv, late_qkv, sums, post]
    for job in everyone:
        job.finish()
    for job in everyone:
        job.drain()
    for w in range(count):
        store_out(w).wait()
        store_gin(w).wait()


def unpack_kernel(counts, names, *refs):
    r = Refs(**dict(zip(names, refs)))
    count = r.out.shape[0]
    loads, stores = [], []
    for w in range(count):
        for i, name in enumerate(("out", "gin")):
            source, target = getattr(r, name + "_in").at[w], getattr(r, name).at[w]
            loads.append(pltpu.make_async_copy(source, r.held.at[i, w], r.sem.at[0, i, w]))
            stores.append(pltpu.make_async_copy(r.held.at[i, w], target, r.sem.at[1, i, w]))
    for copy in loads:
        copy.start()
    for load, store in zip(loads, stores):
        load.wait()
        store.start()
    for name in GRADS[:3]:
        getattr(r, name)[...] = getattr(r, name + "_in")[...]
    size = r.gwq.shape[1] // GROUPS
    for group in range(GROUPS):
        source = getattr(r, "gqkv" + str(group) + "_in")
        for at, name in enumerate(("gwq", "gwk", "gwv")):
            getattr(r, name)[:, group * size : (group + 1) * size] = source[:, at * size : (at + 1) * size]
    r.gpost[...] = r.gpost_in[...]
    place = Place(*counts)
    me = (place.dp * place.z_count + place.z) * 2 + place.c
    rows, ff_rows = r.gvec0.shape[1], r.geb.shape[1]
    width = r.gsmall_in.shape[1]
    turned = pltpu.roll(r.gsmall_in[0:8, :], width - me * rows, axis=1)
    for i in range(8):
        getattr(r, "gvec" + str(i))[...] = turned[i : i + 1, :rows]
    start = me * ff_rows
    lines = r.gsmall_in[8:16, :]
    line_at = lax.broadcasted_iota(jnp.int32, (8, width), 0)
    line = jnp.sum(jnp.where(line_at == start // width, lines, 0.0), axis=0, keepdims=True)
    line = jnp.broadcast_to(line, (8, width))
    r.geb[...] = pltpu.roll(line, width - lax.rem(start, width), axis=1)[0:1, :ff_rows]
    for copy in stores:
        copy.wait()


def call(kernel, name, ins, outs, scratch, **params):
    names = tuple(ins) + tuple(outs) + tuple(scratch)
    spec = lambda space: pl.BlockSpec(memory_space=space)
    results = pl.pallas_call(
        functools.partial(kernel, names),
        out_shape=tuple(shape for shape, _ in outs.values()),
        in_specs=[spec(space) for _, space in ins.values()],
        out_specs=tuple(spec(space) for _, space in outs.values()),
        scratch_shapes=list(scratch.values()),
        compiler_params=pltpu.CompilerParams(vmem_limit_bytes=63 * 2**20, **params),
        name=name,
    )(*[value for value, _ in ins.values()])
    return dict(zip(outs, results))


def local(dp_count, fsdp_count, inputs, lengths, grad_out, *params):
    micro, per_micro, seq, width = inputs.shape
    count = micro * per_micro
    wq, wk, wv, wm, we, ws, pos = params[:7]
    bq, bv, bm, eb, bs, g1, s1, g2, s2 = params[7:]
    ff = we.shape[1]
    rows, ff_rows = wq.shape[0], ws.shape[0]
    vectors = (bq, bv, bm, bs, g1, s1, g2, s2)
    vm, hbm = pltpu.VMEM, pl.ANY
    shape_of = jax.ShapeDtypeStruct
    merged = lambda a: a.reshape((count,) + a.shape[2:])
    act = shape_of((count, seq, width), BF)
    kept = shape_of((3, 4, count, seq, width), BF)
    data = dict(
        lens=(lengths, pltpu.SMEM), x_in=(merged(inputs), hbm), go_in=(merged(grad_out), hbm)
    )
    scratch = work_scratch(count, seq, width, ff)
    if dp_count == 4 and fsdp_count % 2 == 0 and rows % 16 == 0 and LANES % rows == 0 and LANES % ff_rows == 0:
        counts = (dp_count, fsdp_count // 2)
        lead = (dp_count, fsdp_count // 2, 2)
        shards = dict(wq=wq, wk=wk, wv=wv, wm=wm, we=we, ws=ws, post=pos.T)
        ins = dict(data)
        for name, shard in shards.items():
            ins[name + "_shard"] = (shard, vm)
        for i, vector in enumerate(vectors):
            ins["vec" + str(i)] = (vector[None], vm)
        ins["ebs"] = (eb[None], vm)
        outs = dict(out=(act, hbm), gin=(act, hbm), kept=(kept, hbm))
        part = shape_of((rows, 3 * width // GROUPS), F32)
        results = dict(gqkv0=part, gqkv1=part, gwm=wm, gwe=we, gws=ws, gpost=pos.T)
        for name, like in results.items():
            outs[name + "_result"] = (shape_of(like.shape, F32), vm)
        outs["gsmall_result"] = (shape_of((16, width), F32), vm)
        hops = hop_count(*counts)
        pair = lambda name: {name + tail: pltpu.SemaphoreType.DMA((hops,)) for tail in ("_send", "_recv")}
        for name, shard in shards.items():
            scratch[name] = vm(lead + shard.shape, BF)
            scratch.update(pair(name))
        scratch["small"] = vm(lead + (16, LANES), BF)
        scratch["eight"] = vm((8, rows), F32)
        scratch["small_low"] = vm((16, LANES), BF)
        scratch["pos"] = vm((seq, width), BF)
        scratch["vec"] = vm((8, width), F32)
        scratch["eb"] = vm((1, ff), F32)
        scratch["gvec"] = vm((8, width), F32)
        scratch["geb"] = vm((1, ff), F32)
        scratch.update(pair("small"))
        scratch.update(pair("gsmall"))
        for name, like in results.items():
            if name in ("gws", "gwe"):
                scratch[name] = vm(lead[:2] + like.shape, F32)
            elif name != "gpost":
                scratch[name] = vm((like.shape[0] * dp_count * fsdp_count, like.shape[1]), F32)
            scratch[name + "_core"] = vm(lead[:2] + like.shape, BF)
            scratch[name + "_dp"] = vm((3,) + lead[1:2] + like.shape, BF)
            scratch[name + "_z"] = vm((lead[1] - 1,) + like.shape, BF)
            scratch.update(pair(name))
        for tail in ("", "_dp", "_z"):
            scratch["gsmall" + tail] = vm((16, width), F32)
        scratch["gsmall_in"] = vm((hops, 16, width), F32)
        got = call(
            functools.partial(whole_kernel, counts), "layer", ins, outs, scratch,
            collective_id=0, has_side_effects=True,
        )
        ins = {}
        for name in ("out", "gin"):
            ins[name + "_in"] = (got[name], hbm)
        for name in GRADS + ("gpost", "gsmall"):
            ins[name + "_in"] = (got[name + "_result"], vm)
        outs = dict(out=(act, hbm), gin=(act, hbm))
        for name, like in dict(gwq=wq, gwk=wk, gwv=wv, gwm=wm, gwe=we, gws=ws).items():
            outs[name] = (shape_of(like.shape, F32), vm)
        outs["gpost"] = (shape_of((rows, seq), F32), vm)
        for i in range(8):
            outs["gvec" + str(i)] = (shape_of((1, rows), F32), vm)
        outs["geb"] = (shape_of((1, ff_rows), F32), vm)
        got = call(
            functools.partial(unpack_kernel, counts), "unpack", ins, outs,
            dict(held=vm((2,) + act.shape, BF), sem=pltpu.SemaphoreType.DMA((2, 2, count))),
        )
        gvec = [got["gvec" + str(i)].reshape(rows) for i in range(8)]
        geb, gpos = got["geb"].reshape(ff_rows), got["gpost"].T
        grads = got
    else:
        lead = (4, 4, 2)
        cut = lambda a: a.reshape(lead + (-1, a.shape[-1]))
        gather = lambda a, axis=0: lax.all_gather(a, AXES, axis=axis, tiled=True)
        share = lambda a, axis=0: lax.psum_scatter(a, AXES, scatter_dimension=axis, tiled=True)
        ins = dict(data)
        for name, shard in dict(wq=wq, wk=wk, wv=wv, wm=wm, we=we, ws=ws).items():
            ins[name] = (cut(gather(shard)), vm)
        ins["pos"] = (gather(pos, 1), vm)
        ins["vec"] = (jnp.stack([gather(a).astype(F32) for a in vectors]), vm)
        ins["eb"] = (gather(eb).astype(F32)[None], vm)
        outs = dict(out=(act, hbm), gin=(act, hbm), kept=(kept, hbm))
        for name, shape in dict(gws=(ff, width), gwe=(width, ff), gwm=(width, width)).items():
            outs[name] = (shape_of(shape, F32), vm)
        for group in range(GROUPS):
            outs["gqkv" + str(group)] = (shape_of((width, 3 * width // GROUPS), F32), vm)
        outs["gpos_out"] = (shape_of((seq, width), F32), vm)
        outs["gvec"] = (shape_of((8, width), F32), vm)
        outs["geb"] = (shape_of((1, ff), F32), vm)
        got = call(alone_kernel, "layer_alone", ins, outs, scratch)
        size = width // GROUPS
        for at, name in enumerate(("gwq", "gwk", "gwv")):
            parts = [got["gqkv" + str(g)][:, at * size : (at + 1) * size] for g in range(GROUPS)]
            got[name] = jnp.concatenate(parts, axis=1)
        grads = {name: share(got[name]) for name in ("gwq", "gwk", "gwv", "gwm", "gwe", "gws")}
        gpos = share(got["gpos_out"], 1)
        gvec = [share(got["gvec"][i]) for i in range(8)]
        geb = share(got["geb"][0])
    gbq, gbv, gbm, gbs, gg1, gs1, gg2, gs2 = (gvec[i] for i in range(8))
    return (
        got["out"].reshape(inputs.shape), got["gin"].reshape(inputs.shape),
        grads["gwq"], grads["gwk"], grads["gwv"], grads["gwm"], grads["gwe"], grads["gws"], gpos,
        gbq, gbv, gbm, geb, gbs, gg1, gs1, gg2, gs2,
    )


def solution(mesh):
    batch = P(None, AXES, None, None)
    matrix, vector, table = P(AXES, None), P(AXES), P(None, AXES)
    weights = (matrix,) * 6 + (table,) + (vector,) * 9
    return jax.shard_map(
        functools.partial(local, mesh.shape["dp"], mesh.shape["fsdp"]),
        mesh=mesh,
        in_specs=(batch, P(None, AXES), batch) + weights,
        out_specs=(batch, batch) + weights,
        check_vma=False,
    )
```

```python
import functools

import jax
import jax.numpy as jnp
from jax import lax
from jax.experimental import pallas as pl
from jax.experimental.pallas import tpu as pltpu
from jax.sharding import PartitionSpec as P

HEADS = 8
EPS = 1e-05
BF = jnp.bfloat16
F32 = jnp.float32
GELU_C = 0.7978845608028654
GELU_A = 0.044715
AXES = ("dp", "fsdp")
LANES = 128
MESH = pl.DeviceIdType.MESH
FF_PARTS = 1
GROUPS = 2

(BQ, BV, BM, BS, G1, S1, G2, S2) = range(8)
(Q, K, V, LOW) = range(4)


class Refs:
    def __init__(self, **kw):
        self.__dict__.update(kw)


def nn(a, b):
    return lax.dot_general(a, b, (((1,), (0,)), ((), ())), preferred_element_type=F32)


def nt(a, b):
    return lax.dot_general(a, b, (((1,), (1,)), ((), ())), preferred_element_type=F32)


def tn(a, b):
    return lax.dot_general(a, b, (((0,), (0,)), ((), ())), preferred_element_type=F32)


def flat(value):
    return value.reshape(-1, value.shape[-1])


def add_into(ref, value):
    ref[...] += value.reshape(ref.shape)


def add_row(ref, index, value):
    ref[index : index + 1, :] += jnp.sum(value, axis=0, keepdims=True)


def length_of(w, r):
    per_micro = r.lens.shape[1]
    return r.lens[w // per_micro, lax.rem(w, per_micro)]


def make_mask(w, r):
    seq = r.x.shape[1]
    key_at = lax.broadcasted_iota(jnp.int32, (seq, seq), 0)
    query_at = lax.broadcasted_iota(jnp.int32, (seq, seq), 1)
    ok = (key_at <= query_at) & (key_at < length_of(w, r))
    r.mask[...] = jnp.where(ok, 0.0, -1e30)


def make_causal(r):
    size = r.causal.shape[0]
    key_at = lax.broadcasted_iota(jnp.int32, (size, size), 0)
    query_at = lax.broadcasted_iota(jnp.int32, (size, size), 1)
    r.causal[...] = jnp.where(key_at <= query_at, 0.0, -1e30)


def hidden_and_keys(w, r):
    low = (r.x[w].astype(F32) + r.pos[...].astype(F32)).astype(BF)
    r.ab[LOW, w] = low
    r.ab[K, w] = nn(low, flat(r.wk[...])).astype(BF)


def attention_forward(w, r):
    seq, width = r.x.shape[1:]
    half = seq // 2
    head = width // HEADS
    low = r.ab[LOW, w]
    queries = (nn(low, flat(r.wq[...])) + r.vec[BQ : BQ + 1, :]).astype(BF)
    r.ab[Q, w] = (queries.astype(F32) * (head**-0.5)).astype(BF)
    values = (nn(low, flat(r.wv[...])) + r.vec[BV : BV + 1, :]).astype(BF)
    r.ab[V, w] = values
    r.vt[...] = values.T
    make_mask(w, r)
    lane = lax.broadcasted_iota(jnp.int32, (seq, 2 * head), 1)
    for h in range(HEADS):
        pair = slice((h // 2) * 2 * head, (h // 2 + 1) * 2 * head)
        mine = (lane < head) if h % 2 == 0 else (lane >= head)
        qh = jnp.where(mine, r.ab[Q, w, :, pair], jnp.zeros((), BF))
        kp = r.ab[K, w, :, pair]
        s0 = nt(kp[:half], qh) + r.mask[:half, :]
        s1 = nt(kp[half:], qh[half:]) + r.mask[half:, half:]
        m_left = jnp.max(s0[:, :half], axis=0, keepdims=True)
        m_right = jnp.maximum(
            jnp.max(s0[:, half:], axis=0, keepdims=True), jnp.max(s1, axis=0, keepdims=True)
        )
        top = jnp.concatenate([m_left, m_right], axis=1)
        e0 = jnp.exp(s0 - top)
        e1 = jnp.exp(s1 - m_right)
        n_all = jnp.sum(e0, axis=0, keepdims=True)
        n_right = n_all[:, half:] + jnp.sum(e1, axis=0, keepdims=True)
        total = jnp.concatenate([n_all[:, :half], n_right], axis=1)
        query_at = lax.broadcasted_iota(jnp.int32, (1, seq), 1)
        r.logt[w, h : h + 1, :] = jnp.where(query_at < length_of(w, r), top + jnp.log(total), 1e30)
        inv = 1.0 / total
        p0 = (e0 * inv).astype(BF)
        p1 = (e1 * inv[:, half:]).astype(BF)
        vt = r.vt[h * head : (h + 1) * head, :]
        o_left = nn(vt[:, :half], p0[:, :half])
        o_right = nn(vt, jnp.concatenate([p0[:, half:], p1], axis=0))
        r.ot[h * head : (h + 1) * head, :half] = o_left.astype(BF)
        r.ot[h * head : (h + 1) * head, half:] = o_right.astype(BF)
    r.mixed[w] = r.ot[...].T
    for i in range(4):
        park_copy(r, i, w).start()


def norm_parts(total):
    center = total - jnp.mean(total, -1, keepdims=True)
    spread = jnp.mean(center * center, -1, keepdims=True)
    inv = lax.rsqrt(spread + EPS)
    return center * inv, inv


def norm_back(e, xhat, inv):
    return inv * (
        e - jnp.mean(e, -1, keepdims=True) - xhat * jnp.mean(e * xhat, -1, keepdims=True)
    )


def slot_of(kind, w, c):
    return (kind + 2 * lax.rem(w, 2), c)


def part_copy(r, kind, w, part, c, rows):
    here = slice(part * rows, (part + 1) * rows)
    target = r.kept.at[1 + kind, c, w]
    return pltpu.make_async_copy(r.ab.at[slot_of(kind, w, c)], target, r.part_sem.at[kind, lax.rem(w, 2), c])


def park_copy(r, i, w):
    return pltpu.make_async_copy(r.ab.at[i, w], r.kept.at[0, i, w], r.park_sem.at[i, w])


def finish_parking(r):
    for i in range(4):
        for w in range(r.x.shape[0]):
            park_copy(r, i, w).wait()


def block_load(r, kind, c, buffer):
    return pltpu.make_async_copy(r.kept.at[kind, c], r.ab.at[buffer], r.load_sem.at[buffer])


BUFFERS = (2, 3, 0, 1, 2, 0, 1, 3)
FOLLOWS = {0: (2, 0), 1: (2, 3), 2: (2, 1), 3: (2, 2), 4: (0, 2), 5: (0, 0), 6: (0, 1), 7: (0, 3)}


def weight_sums(r, emit, after):
    count = r.x.shape[0]
    rows, chunks = r.slope.shape[0], r.ws.shape[0]
    for kind in range(2):
        for part in range(FF_PARTS):
            for c in range(chunks):
                part_copy(r, kind, count - 2, part, c, rows).wait()
                part_copy(r, kind, count - 1, part, c, rows).wait()
    for item in range(4):
        block_load(r, 1, item, BUFFERS[item]).start()
    for item in range(2 * chunks):
        buffer, c = BUFFERS[item], item % chunks
        block_load(r, 1 + item // chunks, c, buffer).wait()
        block = flat(r.ab[buffer])
        if item < chunks:
            emit(item, tn(block, flat(r.gff[...])))
        else:
            emit(item, tn(flat(r.nl[...]), block))
        block_load(r, *FOLLOWS[item], buffer).start()
        after(item)
    for buffer in range(4):
        block_load(r, 0, buffer, buffer).wait()


def feed_forward(w, part, r):
    rows, width = r.slope.shape[0], r.x.shape[-1]
    here = slice(part * rows, (part + 1) * rows)
    chunks = r.ws.shape[0]
    chunk = r.we.shape[-1] // chunks

    @pl.when(w > 1)
    def _():
        for kind in range(2):
            for c in range(chunks):
                part_copy(r, kind, w - 2, part, c, rows).wait()

    hid = r.x[w, here, :].astype(F32) + r.pos[here, :].astype(F32)
    first = hid + (nn(r.mixed[w, here, :], flat(r.wm[...])) + r.vec[BM : BM + 1, :])
    xhat1, inv1 = norm_parts(first)
    r.xh1[...] = xhat1
    normed = xhat1 * r.vec[G1 : G1 + 1, :] + r.vec[S1 : S1 + 1, :]
    r.nl[w, here, :] = normed.astype(BF)
    ff_out = None
    for c in range(chunks):
        cols = slice(c * chunk, (c + 1) * chunk)
        t = nn(r.nl[w, here, :], flat(r.we[..., cols])) + r.eb[:, cols]
        t2 = t * t
        th = jnp.tanh(t * (t2 * (GELU_A * GELU_C) + GELU_C))
        ht = 0.5 * t
        act = (ht * th + ht).astype(BF)
        slot = slot_of(0, w, c)
        r.ab[slot] = act
        slope = (0.5 * th + 0.5) + ht * (1.0 - th * th) * (t2 * (3 * GELU_A * GELU_C) + GELU_C)
        r.slope[:, cols] = slope
        part_out = nn(act, flat(r.ws[c]))
        ff_out = part_out if ff_out is None else ff_out + part_out
    second = normed + (ff_out + r.vec[BS : BS + 1, :])
    xhat2, inv2 = norm_parts(second)
    row_at = part * rows + lax.broadcasted_iota(jnp.int32, (rows, width), 0)
    cot = jnp.where(row_at < length_of(w, r), r.go[w, here, :].astype(F32), 0.0)
    r.go[w, here, :] = (xhat2 * r.vec[G2 : G2 + 1, :] + r.vec[S2 : S2 + 1, :]).astype(BF)
    add_row(r.gvec, G2, cot * xhat2)
    add_row(r.gvec, S2, cot)
    d_second = norm_back(cot * r.vec[G2 : G2 + 1, :], xhat2, inv2)
    gff = d_second.astype(BF)
    r.gff[w, here, :] = gff
    add_row(r.gvec, BS, gff.astype(F32))
    d_normed = d_second
    for c in range(chunks):
        cols = slice(c * chunk, (c + 1) * chunk)
        gpre = (nt(r.gff[w, here, :], flat(r.ws[c])) * r.slope[:, cols]).astype(BF)
        r.geb[:, cols] += jnp.sum(gpre.astype(F32), axis=0, keepdims=True)
        slot = slot_of(1, w, c)
        r.ab[slot] = gpre
        d_normed = d_normed + nt(gpre, flat(r.we[..., cols]))
    xhat1 = r.xh1[...]
    add_row(r.gvec, G1, d_normed * xhat1)
    add_row(r.gvec, S1, d_normed)
    d_first = norm_back(d_normed * r.vec[G1 : G1 + 1, :], xhat1, inv1)
    r.dfirst[w, here, :] = d_first
    gattn = d_first.astype(BF)
    add_row(r.gvec, BM, gattn.astype(F32))
    mixed = r.mixed[w, here, :]
    add_into(r.gwm, tn(mixed, gattn))
    gmix = nt(gattn, flat(r.wm[...])).astype(BF)
    head = width // HEADS
    prod = gmix.astype(F32) * mixed.astype(F32)
    hi = prod.astype(BF)
    lo = (prod - hi.astype(F32)).astype(BF)
    sel_row = lax.broadcasted_iota(jnp.int32, (16, width), 0)
    sel_col = lax.broadcasted_iota(jnp.int32, (16, width), 1)
    sel = jnp.where(sel_col // head == sel_row, 1.0, 0.0).astype(BF)
    r.delta[w, :, here] = nt(sel, hi) + nt(sel, lo)
    r.mixed[w, here, :] = gmix
    for kind in range(2):
        for c in range(chunks):
            part_copy(r, kind, w, part, c, rows).start()


def attention_backward(w, group, r):
    seq, width = r.x.shape[1:]
    half = seq // 2
    head = width // HEADS
    scale = head**-0.5
    cols = slice(group * (width // GROUPS), (group + 1) * (width // GROUPS))
    r.vt[cols, :] = r.ab[K, w, :, cols].T
    lane = lax.broadcasted_iota(jnp.int32, (seq, 2 * head), 1)
    pairs = HEADS // 2 // GROUPS
    for p in range(group * pairs, (group + 1) * pairs):
        pair = slice(p * 2 * head, (p + 1) * 2 * head)
        kp = r.ab[K, w, :, pair]
        vp = r.ab[V, w, :, pair]
        sums = None
        for odd in range(2):
            h = 2 * p + odd
            mine = (lane >= head) if odd else (lane < head)
            qh = jnp.where(mine, r.ab[Q, w, :, pair], jnp.zeros((), BF))
            gh = jnp.where(mine, r.mixed[w, :, pair], jnp.zeros((), BF))
            logt = r.logt[w, h : h + 1, :]
            delta = r.delta[w, h : h + 1, :]
            s0 = nt(kp[:half], qh)
            s0 = jnp.concatenate([s0[:, :half] + r.causal[...], s0[:, half:]], axis=1)
            p0 = jnp.exp(s0 - logt)
            p1 = jnp.exp(nt(kp[half:], qh[half:]) + r.causal[...] - logt[:, half:])
            d0 = (p0 * (nt(vp[:half], gh) - delta)).astype(BF)
            d1 = (p1 * (nt(vp[half:], gh[half:]) - delta[:, half:])).astype(BF)
            p0 = p0.astype(BF)
            p1 = p1.astype(BF)
            parts = (nn(d0, qh), nn(d1, qh[half:]), nn(p0, gh), nn(p1, gh[half:]))
            sums = parts if sums is None else tuple(a + b for a, b in zip(sums, parts))
            kt = r.vt[h * head : (h + 1) * head, :]
            q_left = nn(kt[:, :half], d0[:, :half])
            q_right = nn(kt, jnp.concatenate([d0[:, half:], d1], axis=0))
            r.ot[h * head : (h + 1) * head, :half] = (q_left * scale).astype(BF)
            r.ot[h * head : (h + 1) * head, half:] = (q_right * scale).astype(BF)
        grads = [part.astype(BF) for part in sums]
        r.ab[K, w, :half, pair] = grads[0]
        r.ab[K, w, half:, pair] = grads[1]
        r.ab[V, w, :half, pair] = grads[2]
        r.ab[V, w, half:, pair] = grads[3]
        gq = r.ot[pair, :].T
        r.ab[Q, w, :, pair] = gq
        r.gvec[BQ : BQ + 1, pair] += jnp.sum(gq.astype(F32), axis=0, keepdims=True)
        gv = grads[2].astype(F32) + grads[3].astype(F32)
        r.gvec[BV : BV + 1, pair] += jnp.sum(gv, axis=0, keepdims=True)


def projection_sums(group, r):
    width = r.x.shape[-1]
    size = width // GROUPS
    cols = slice(group * size, (group + 1) * size)
    total = getattr(r, "gqkv" + str(group))
    for at, kind in enumerate((Q, K, V)):
        total[:, at * size : (at + 1) * size] = tn(flat(r.ab[LOW]), flat(r.ab[kind, :, :, cols]))


def hidden_back(w, r):
    d_hidden = (
        r.dfirst[w]
        + nt(r.ab[Q, w], flat(r.wq[...]))
        + nt(r.ab[K, w], flat(r.wk[...]))
        + nt(r.ab[V, w], flat(r.wv[...]))
    )
    r.gpos[...] += d_hidden
    r.x[w] = d_hidden.astype(BF)


def windows(count, body):
    def step(w, carry):
        body(w)
        return carry

    lax.fori_loop(0, count, step, 0)


def at_window(w, plan):
    for index, steps in plan:

        @pl.when(w == index)
        def _():
            for step in steps:
                step()


class Place:
    def __init__(self, dp_count, z_count):
        self.dp_count, self.z_count = dp_count, z_count
        self.dp = lax.axis_index("dp")
        fsdp = lax.axis_index("fsdp")
        self.z, self.c = fsdp // 2, lax.rem(fsdp, 2)
        self.near = (self.dp, self.z * 2 + (1 - self.c))

    def z_at(self, shift):
        return lax.rem(self.z + shift + self.z_count, self.z_count)

    def dp_flip(self, bit):
        low, high = lax.rem(self.dp, 2), self.dp // 2
        if bit in (0, 2):
            low = 1 - low
        if bit in (1, 2):
            high = 1 - high
        return high * 2 + low

    def along_z(self, shift):
        return (self.dp, self.z_at(shift) * 2 + self.c)

    def along_dp(self, bit):
        return (self.dp_flip(bit), self.z * 2 + self.c)

    def barrier(self):
        sem = pltpu.get_barrier_semaphore()
        everyone = [self.near] + [self.along_z(s) for s in range(1, self.z_count)]
        everyone += [self.along_dp(bit) for bit in range(3)]
        for peer in everyone:
            pl.semaphore_signal(sem, inc=1, device_id=peer, device_id_type=MESH)
        pl.semaphore_wait(sem, len(everyone))


def remote(src, dst, sems, index, peer):
    send, recv = sems
    return pltpu.make_async_remote_copy(
        src_ref=src, dst_ref=dst, send_sem=send.at[index], recv_sem=recv.at[index],
        device_id=peer, device_id_type=MESH,
    )


def hop_count(dp_count, z_count):
    return (z_count - 1) + 10


def halves(ref):
    lanes = ref.shape[-1]
    if lanes % (2 * LANES):
        return ((0, slice(0, lanes)),)
    return ((0, slice(0, lanes // 2)), (1, slice(lanes // 2, lanes)))


class Gather:
    def __init__(self, place, shard, whole, sems):
        self.p, self.shard, self.whole, self.sems = place, shard, whole, sems
        self.base = place.z_count - 1

    def z_copy(self, shift, z):
        p = self.p
        return remote(self.shard, self.whole.at[p.dp, z, p.c], self.sems, shift - 1, p.along_z(shift))

    def own_copy(self, bit, owner):
        block = self.whole.at[owner, :, self.p.c]
        return remote(block, block, self.sems, self.base + bit, self.p.along_dp(bit))

    def far_copy(self, bit, lanes, owner):
        block = self.whole.at[owner, :, self.p.c, :, lanes]
        return remote(block, block, self.sems, self.base + 2 + bit, self.p.along_dp(1 - bit))

    def core_copy(self, core):
        half = self.whole.at[:, :, core]
        return remote(half, half, self.sems, self.base + 4, self.p.near)

    def start_z(self):
        p = self.p
        for shift in range(1, p.z_count):
            self.z_copy(shift, p.z).start()
        self.whole[p.dp, p.z, p.c] = self.shard[...]

    def start_dp(self):
        p = self.p
        for shift in range(1, p.z_count):
            self.z_copy(shift, p.z_at(-shift)).wait_recv()
        for bit in range(2):
            self.own_copy(bit, p.dp).start()

    def pass_on(self):
        p = self.p
        for bit in range(2):
            self.own_copy(bit, p.dp_flip(bit)).wait_recv()
        for bit, lanes in halves(self.whole):
            self.far_copy(bit, lanes, p.dp_flip(bit)).start()

    def start_core(self):
        p = self.p
        for bit, lanes in halves(self.whole):
            self.far_copy(bit, lanes, p.dp_flip(2)).wait_recv()
        self.core_copy(p.c).start()

    def finish(self):
        self.core_copy(1 - self.p.c).wait_recv()

    def drain(self):
        p = self.p
        for shift in range(1, p.z_count):
            self.z_copy(shift, p.z).wait_send()
        for bit in range(2):
            self.own_copy(bit, p.dp).wait_send()
        for bit, lanes in halves(self.whole):
            self.far_copy(bit, lanes, p.dp_flip(bit)).wait_send()
        self.core_copy(p.c).wait_send()


class Scatter:
    def __init__(self, place, total, result, bufs, sems):
        self.p, self.total, self.result, self.sems = place, total, result, sems
        self.out, self.from_core, self.from_dp, self.from_z = bufs
        self.base = place.z_count - 1

    pieces = ((slice(None), slice(None)),)

    def core_copy(self, piece):
        at = self.pieces[piece]
        return remote(self.out.at[at], self.from_core.at[at], self.sems, self.base + 6 + piece, self.p.near)

    def dp_copy(self, slot, bit, lanes):
        p = self.p
        block = p.dp_flip((2, bit, 1 - bit)[slot])
        return remote(
            self.out.at[block, :, :, lanes], self.from_dp.at[slot, :, :, lanes], self.sems,
            self.base + 2 * slot + bit, p.along_dp((bit, bit, 1 - bit)[slot]),
        )

    def z_copy(self, shift):
        p = self.p
        block = self.out.at[p.dp, p.z_at(shift)]
        return remote(block, self.from_z.at[shift - 1], self.sems, shift - 1, p.along_z(shift))

    def blocks(self, body):
        p = self.p

        def step(at, carry):
            body(at // p.z_count, lax.rem(at, p.z_count))
            return carry

        lax.fori_loop(0, p.dp_count * p.z_count, step, 0)

    def rows_at(self, d, z, core):
        size = self.result.shape[0]
        start = ((d * self.p.z_count + z) * 2 + core) * size
        return self.total.at[pl.ds(pl.multiple_of(start, size), size)]

    def mine(self, d, z):
        if len(self.total.shape) == 4:
            return self.total.at[d, z]
        return self.rows_at(d, z, self.p.c)

    def start_core(self):
        far = 1 - self.p.c

        def body(d, z):
            self.out[d, z] = self.rows_at(d, z, far)[...].astype(BF)

        self.blocks(body)
        self.core_copy(0).start()

    def summed(self, d, z, lanes):
        return self.mine(d, z)[:, lanes] + self.from_core[d, z, :, lanes].astype(F32)

    def start_dp(self):
        p = self.p
        for piece in range(len(self.pieces)):
            self.core_copy(piece).wait_recv()
            self.core_copy(piece).wait_send()
        for slot in range(2):
            for bit, lanes in halves(self.out):
                block = p.dp_flip((2, bit)[slot])
                for z in range(p.z_count):
                    self.out[block, z, :, lanes] = self.summed(block, z, lanes).astype(BF)
                self.dp_copy(slot, bit, lanes).start()

    def pass_on(self):
        p = self.p
        for bit, lanes in halves(self.out):
            self.dp_copy(0, bit, lanes).wait_recv()
            other = p.dp_flip(1 - bit)
            for z in range(p.z_count):
                added = self.summed(other, z, lanes) + self.from_dp[0, z, :, lanes].astype(F32)
                self.out[other, z, :, lanes] = added.astype(BF)
            self.dp_copy(2, bit, lanes).start()

    def along(self, z):
        added = self.summed(self.p.dp, z, slice(None))
        return added + self.from_dp[1, z].astype(F32) + self.from_dp[2, z].astype(F32)

    def start_z(self):
        p = self.p
        for slot in (1, 2):
            for bit, lanes in halves(self.out):
                self.dp_copy(slot, bit, lanes).wait_recv()
        for shift in range(1, p.z_count):
            z = p.z_at(shift)
            self.out[p.dp, z] = self.along(z).astype(BF)
            self.z_copy(shift).start()

    def finish(self):
        p = self.p
        added = self.along(p.z)
        for shift in range(1, p.z_count):
            self.z_copy(shift).wait_recv()
            added = added + self.from_z[shift - 1].astype(F32)
        self.result[...] = added

    def drain(self):
        for slot in range(3):
            for bit, lanes in halves(self.out):
                self.dp_copy(slot, bit, lanes).wait_send()
        for shift in range(1, self.p.z_count):
            self.z_copy(shift).wait_send()


class SumAll:
    def __init__(self, place, total, result, bufs, sems):
        self.p, self.total, self.result, self.sems = place, total, result, sems
        self.send_dp, self.send_z, self.landing = bufs

    def copies(self, hop):
        p = self.p
        base = p.z_count - 1
        if hop == 0:
            return [(base + 3, remote(self.total, self.landing.at[base + 3], self.sems, base + 3, p.near))]
        if hop == 1:
            return [
                (base + b, remote(self.send_dp, self.landing.at[base + b], self.sems, base + b, p.along_dp(b)))
                for b in range(3)
            ]
        return [
            (s - 1, remote(self.send_z, self.landing.at[s - 1], self.sems, s - 1, p.along_z(s)))
            for s in range(1, p.z_count)
        ]

    def arrived(self, hop, own):
        added = own[...]
        for slot, copy in self.copies(hop):
            copy.wait_recv()
            added = added + self.landing[slot]
        return added

    def start(self, hop):
        for _, copy in self.copies(hop):
            copy.start()

    def start_core(self):
        self.start(0)

    def start_dp(self):
        self.send_dp[...] = self.arrived(0, self.total)
        self.start(1)

    def pass_on(self):
        pass

    def start_z(self):
        self.send_z[...] = self.arrived(1, self.send_dp)
        self.start(2)

    def finish(self):
        self.result[...] = self.arrived(2, self.send_z)

    def drain(self):
        for hop in range(3):
            for _, copy in self.copies(hop):
                copy.wait_send()


WEIGHTS = ("wk", "wq", "wv", "wm", "we", "ws")
GRADS = ("gws", "gwe", "gwm", "gqkv0", "gqkv1")
EARLY = ("post", "small", "wk", "wq", "wv")
LATE = ("wm", "we", "ws")


def work_scratch(count, seq, width, ff):
    vm = pltpu.VMEM
    return dict(
        ab=vm((4, count, seq, width), BF),
        mixed=vm((count, seq, width), BF),
        dfirst=vm((count, seq, width), F32),
        logt=vm((count, HEADS, seq), F32),
        delta=vm((count, 16, seq), F32),
        vt=vm((width, seq), BF),
        ot=vm((width, seq), BF),
        mask=vm((seq, seq), F32),
        causal=vm((seq // 2, seq // 2), F32),
        xh1=vm((seq // FF_PARTS, width), F32),
        nl=vm((count, seq, width), BF),
        gff=vm((count, seq, width), BF),
        slope=vm((seq // FF_PARTS, ff), F32),
        gpos=vm((seq, width), F32),
        x=vm((count, seq, width), BF),
        go=vm((count, seq, width), BF),
        io_sem=pltpu.SemaphoreType.DMA((4, count)),
        part_sem=pltpu.SemaphoreType.DMA((2, 2, 4)),
        park_sem=pltpu.SemaphoreType.DMA((4, count)),
        load_sem=pltpu.SemaphoreType.DMA((4,)),
    )


def zero_sums(r):
    make_causal(r)
    for name in ("gwm", "gpos", "gvec", "geb"):
        ref = getattr(r, name)
        ref[...] = jnp.zeros(ref.shape, ref.dtype)


def io_copies(r, count):
    def load(w):
        return (
            pltpu.make_async_copy(r.x_in.at[w], r.x.at[w], r.io_sem.at[0, w]),
            pltpu.make_async_copy(r.go_in.at[w], r.go.at[w], r.io_sem.at[1, w]),
        )

    def store_out(w):
        return pltpu.make_async_copy(r.go.at[w], r.out.at[w], r.io_sem.at[2, w])

    def store_gin(w):
        return pltpu.make_async_copy(r.x.at[w], r.gin.at[w], r.io_sem.at[3, w])

    return load, store_out, store_gin


def emit_whole(r, item, value):
    size = value.shape[0]
    if item < r.ws.shape[0]:
        r.gws[item * size : (item + 1) * size, :] = value
    else:
        c = item - r.ws.shape[0]
        r.gwe[:, c * size : (c + 1) * size] = value


def emit_halves(r, place, item, value):
    r.mask[...] = value
    chunks, size = r.ws.shape[0], value.shape[0]
    if item < chunks:
        blocks = [((item, z), z) for z in range(place.z_count)]
        kept, sent, rows = r.gws, r.gws_out, r.gws.shape[2]
        cols = slice(None)
    else:
        blocks = [((d, z), d * place.z_count + z) for d in range(place.dp_count) for z in range(place.z_count)]
        kept, sent, rows = r.gwe, r.gwe_out, r.gwe.shape[2]
        cols = slice((item - chunks) * size, (item - chunks + 1) * size)
    for at, block in blocks:
        start = pl.multiple_of((block * 2 + place.c) * rows, rows)
        kept[at + (slice(None), cols)] = r.mask[pl.ds(start, rows), :]
        start = pl.multiple_of((block * 2 + 1 - place.c) * rows, rows)
        sent[at + (slice(None), cols)] = r.mask[pl.ds(start, rows), :].astype(BF)


def alone_kernel(names, *refs):
    r = Refs(**dict(zip(names, refs)))
    count = r.x.shape[0]
    load, store_out, store_gin = io_copies(r, count)
    for w in range(count):
        for copy in load(w):
            copy.start()
    zero_sums(r)
    for w in range(count):
        for copy in load(w):
            copy.wait()

    def second(w):
        feed_forward(w, 0, r)
        store_out(w).start()

    def third(w):
        hidden_back(w, r)
        store_gin(w).start()

    windows(count, lambda w: hidden_and_keys(w, r))
    windows(count, lambda w: attention_forward(w, r))
    finish_parking(r)
    windows(count, second)
    weight_sums(r, lambda item, value: emit_whole(r, item, value), lambda item: None)
    for group in range(GROUPS):
        windows(count, lambda w: attention_backward(w, group, r))
        projection_sums(group, r)
    windows(count, third)
    r.gpos_out[...] = r.gpos[...]
    for w in range(count):
        store_out(w).wait()
        store_gin(w).wait()


def vectors_from(r, dp_count, z_count, rows):
    devices = dp_count * z_count * 2
    per_row = LANES // rows
    ff_rows = r.eb.shape[1] // devices
    per_row_ff = LANES // ff_rows

    def block(d):
        return r.small[d // (2 * z_count), (d // 2) % z_count, d % 2].astype(F32)

    for g in range(devices // per_row):
        added = block(g * per_row)[:8]
        for d in range(g * per_row + 1, (g + 1) * per_row):
            added = added + block(d)[:8]
        r.vec[:, g * LANES : (g + 1) * LANES] = added
    for g in range(devices // per_row_ff):
        added = block(g * per_row_ff)[8:9]
        for d in range(g * per_row_ff + 1, (g + 1) * per_row_ff):
            added = added + block(d)[8:9]
        r.eb[:, g * LANES : (g + 1) * LANES] = added


def place_small(r, place):
    rows, ff_rows = r.vec0.shape[1], r.ebs.shape[1]
    me = (place.dp * place.z_count + place.z) * 2 + place.c

    def spread(n):
        at = lax.rem(me, LANES // n) * n
        source = lax.broadcasted_iota(jnp.int32, (n, LANES), 0)
        target = lax.broadcasted_iota(jnp.int32, (n, LANES), 1)
        return jnp.where(target == source + at, 1.0, 0.0).astype(BF)

    for i in range(8):
        r.eight[i : i + 1, :] = getattr(r, "vec" + str(i))[...].astype(F32)
    r.small_low[0:8, :] = nn(r.eight[...].astype(BF), spread(rows)).astype(BF)
    one = jnp.broadcast_to(r.ebs[...].astype(F32), (8, ff_rows)).astype(BF)
    r.small_low[8:16, :] = nn(one, spread(ff_rows)).astype(BF)


def whole_kernel(counts, names, *refs):
    r = Refs(**dict(zip(names, refs)))
    count = r.x.shape[0]
    rows = r.wq_shard.shape[0]
    place = Place(*counts)
    load, store_out, store_gin = io_copies(r, count)
    for w in range(count):
        for copy in load(w):
            copy.start()
    place_small(r, place)
    gathers = {}
    for name in EARLY + LATE:
        shard = r.small_low if name == "small" else getattr(r, name + "_shard")
        sems = (getattr(r, name + "_send"), getattr(r, name + "_recv"))
        gathers[name] = Gather(place, shard, getattr(r, name), sems)
    early = [gathers[name] for name in EARLY]
    late = [gathers[name] for name in LATE]
    place.barrier()
    for job in early + late:
        job.start_z()
    zero_sums(r)
    for job in early:
        job.start_dp()
    for job in early:
        job.pass_on()
    for job in early:
        job.start_core()
    for job in late:
        job.start_dp()
    for job in early[:3]:
        job.finish()
    r.pos[...] = flat(r.post[...]).T
    vectors_from(r, counts[0], counts[1], rows)
    for w in range(count):
        for copy in load(w):
            copy.wait()
    windows(count, lambda w: hidden_and_keys(w, r))
    for job in early[3:]:
        job.finish()

    wm, we, ws = late
    first_plan = ((1, (wm.pass_on,)), (2, (we.pass_on, wm.start_core)), (3, (ws.pass_on, we.start_core)))

    def first_body(w):
        at_window(w, first_plan)
        attention_forward(w, r)

    windows(count, first_body)
    ws.start_core()
    finish_parking(r)
    for job in late:
        job.finish()

    def second_body(w):
        feed_forward(w, 0, r)
        store_out(w).start()

    windows(count, second_body)

    scatters = {}
    for job in early + late:
        job.drain()
    for name in GRADS + ("gpost",):
        total = r.mask if name == "gpost" else getattr(r, name)
        if name.startswith("gqkv"):
            group, size = int(name[-1]), getattr(r, name).shape[1]
            out = r.we.at[:, :, 1, :, pl.ds(group * size, size)]
        else:
            out = getattr(r, "post" if name == "gpost" else "w" + name[2:]).at[:, :, 0]
        setattr(r, name + "_out", out)
        bufs = [out] + [getattr(r, name + tail) for tail in ("_core", "_dp", "_z")]
        sems = (getattr(r, name + "_send"), getattr(r, name + "_recv"))
        scatters[name] = Scatter(place, total, getattr(r, name + "_result"), bufs, sems)
    sums = SumAll(
        place, r.gsmall, r.gsmall_result, (r.gsmall_dp, r.gsmall_z, r.gsmall_in), (r.gsmall_send, r.gsmall_recv)
    )
    gws, gwe, gwm = (scatters[name] for name in ("gws", "gwe", "gwm"))
    early_qkv, late_qkv, post = (scatters[name] for name in ("gqkv0", "gqkv1", "gpost"))
    gwm.start_core()
    chunks = counts[0]
    gws.pieces = tuple((c, slice(None)) for c in range(chunks))
    size = r.we.shape[-1] // chunks
    gwe.pieces = tuple(
        (slice(None), slice(None), slice(None), slice(c * size, (c + 1) * size)) for c in range(chunks)
    )

    def after(item):
        job = gws if item < chunks else gwe
        job.core_copy(item % chunks).start()
        if item == 1:
            gwm.start_dp()
        if item == 3:
            gwm.pass_on()
        if item == 5:
            gwm.start_z()
        if item == 6:
            gws.start_dp()

    weight_sums(r, lambda item, value: emit_halves(r, place, item, value), after)

    plans = (
        ((1, (gws.pass_on,)), (2, (gwe.start_dp,)), (3, (gws.start_z,))),
        ((1, (early_qkv.start_dp,)), (2, (gwe.start_z,)), (3, (early_qkv.pass_on,))),
        ((2, (late_qkv.start_dp,)),),
    )

    def heads_body(group):
        def body(w):
            at_window(w, plans[group])
            attention_backward(w, group, r)

        return body

    windows(count, heads_body(0))
    projection_sums(0, r)
    early_qkv.start_core()
    gwe.pass_on()
    windows(count, heads_body(1))
    projection_sums(1, r)
    late_qkv.start_core()
    early_qkv.start_z()

    def last_body(w):
        at_window(w, plans[2])
        hidden_back(w, r)
        store_gin(w).start()

    windows(count, last_body)
    r.mask[...] = r.gpos[...].T
    post.start_core()
    ff_rows = r.geb.shape[1] // r.gvec.shape[1]
    width = r.gvec.shape[1]
    r.gsmall[0:8, :] = r.gvec[...]
    r.gsmall[8:16, :] = jnp.zeros((8, width), F32)
    for i in range(ff_rows):
        r.gsmall[8 + i : 9 + i, :] = r.geb[:, i * width : (i + 1) * width]
    sums.start_core()
    late_qkv.pass_on()
    post.start_dp()
    sums.start_dp()
    post.pass_on()
    late_qkv.start_z()
    sums.start_z()
    post.start_z()
    everyone = [gws, gwe, gwm, early_qkv, late_qkv, sums, post]
    for job in everyone:
        job.finish()
    for job in everyone:
        job.drain()
    for w in range(count):
        store_out(w).wait()
        store_gin(w).wait()


def unpack_kernel(counts, names, *refs):
    r = Refs(**dict(zip(names, refs)))
    count = r.out.shape[0]
    loads, stores = [], []
    for w in range(count):
        for i, name in enumerate(("out", "gin")):
            source, target = getattr(r, name + "_in").at[w], getattr(r, name).at[w]
            loads.append(pltpu.make_async_copy(source, r.held.at[i, w], r.sem.at[0, i, w]))
            stores.append(pltpu.make_async_copy(r.held.at[i, w], target, r.sem.at[1, i, w]))
    for copy in loads:
        copy.start()
    for load, store in zip(loads, stores):
        load.wait()
        store.start()
    for name in GRADS[:3]:
        getattr(r, name)[...] = getattr(r, name + "_in")[...]
    size = r.gwq.shape[1] // GROUPS
    for group in range(GROUPS):
        source = getattr(r, "gqkv" + str(group) + "_in")
        for at, name in enumerate(("gwq", "gwk", "gwv")):
            getattr(r, name)[:, group * size : (group + 1) * size] = source[:, at * size : (at + 1) * size]
    r.gpost[...] = r.gpost_in[...]
    place = Place(*counts)
    me = (place.dp * place.z_count + place.z) * 2 + place.c
    rows, ff_rows = r.gvec0.shape[1], r.geb.shape[1]
    width = r.gsmall_in.shape[1]
    turned = pltpu.roll(r.gsmall_in[0:8, :], width - me * rows, axis=1)
    for i in range(8):
        getattr(r, "gvec" + str(i))[...] = turned[i : i + 1, :rows]
    start = me * ff_rows
    lines = r.gsmall_in[8:16, :]
    line_at = lax.broadcasted_iota(jnp.int32, (8, width), 0)
    line = jnp.sum(jnp.where(line_at == start // width, lines, 0.0), axis=0, keepdims=True)
    line = jnp.broadcast_to(line, (8, width))
    r.geb[...] = pltpu.roll(line, width - lax.rem(start, width), axis=1)[0:1, :ff_rows]
    for copy in stores:
        copy.wait()


def call(kernel, name, ins, outs, scratch, **params):
    names = tuple(ins) + tuple(outs) + tuple(scratch)
    spec = lambda space: pl.BlockSpec(memory_space=space)
    results = pl.pallas_call(
        functools.partial(kernel, names),
        out_shape=tuple(shape for shape, _ in outs.values()),
        in_specs=[spec(space) for _, space in ins.values()],
        out_specs=tuple(spec(space) for _, space in outs.values()),
        scratch_shapes=list(scratch.values()),
        compiler_params=pltpu.CompilerParams(vmem_limit_bytes=63 * 2**20, **params),
        name=name,
    )(*[value for value, _ in ins.values()])
    return dict(zip(outs, results))


def local(dp_count, fsdp_count, inputs, lengths, grad_out, *params):
    micro, per_micro, seq, width = inputs.shape
    count = micro * per_micro
    wq, wk, wv, wm, we, ws, pos = params[:7]
    bq, bv, bm, eb, bs, g1, s1, g2, s2 = params[7:]
    ff = we.shape[1]
    rows, ff_rows = wq.shape[0], ws.shape[0]
    vectors = (bq, bv, bm, bs, g1, s1, g2, s2)
    vm, hbm = pltpu.VMEM, pl.ANY
    shape_of = jax.ShapeDtypeStruct
    merged = lambda a: a.reshape((count,) + a.shape[2:])
    act = shape_of((count, seq, width), BF)
    kept = shape_of((3, 4, count, seq, width), BF)
    data = dict(
        lens=(lengths, pltpu.SMEM), x_in=(merged(inputs), hbm), go_in=(merged(grad_out), hbm)
    )
    scratch = work_scratch(count, seq, width, ff)
    if dp_count == 4 and fsdp_count % 2 == 0 and rows % 16 == 0 and LANES % rows == 0 and LANES % ff_rows == 0:
        counts = (dp_count, fsdp_count // 2)
        lead = (dp_count, fsdp_count // 2, 2)
        shards = dict(wq=wq, wk=wk, wv=wv, wm=wm, we=we, ws=ws, post=pos.T)
        ins = dict(data)
        for name, shard in shards.items():
            ins[name + "_shard"] = (shard, vm)
        for i, vector in enumerate(vectors):
            ins["vec" + str(i)] = (vector[None], vm)
        ins["ebs"] = (eb[None], vm)
        outs = dict(out=(act, hbm), gin=(act, hbm), kept=(kept, hbm))
        part = shape_of((rows, 3 * width // GROUPS), F32)
        results = dict(gqkv0=part, gqkv1=part, gwm=wm, gwe=we, gws=ws, gpost=pos.T)
        for name, like in results.items():
            outs[name + "_result"] = (shape_of(like.shape, F32), vm)
        outs["gsmall_result"] = (shape_of((16, width), F32), vm)
        hops = hop_count(*counts)
        pair = lambda name: {name + tail: pltpu.SemaphoreType.DMA((hops,)) for tail in ("_send", "_recv")}
        for name, shard in shards.items():
            scratch[name] = vm(lead + shard.shape, BF)
            scratch.update(pair(name))
        scratch["small"] = vm(lead + (16, LANES), BF)
        scratch["eight"] = vm((8, rows), F32)
        scratch["small_low"] = vm((16, LANES), BF)
        scratch["pos"] = vm((seq, width), BF)
        scratch["vec"] = vm((8, width), F32)
        scratch["eb"] = vm((1, ff), F32)
        scratch["gvec"] = vm((8, width), F32)
        scratch["geb"] = vm((1, ff), F32)
        scratch.update(pair("small"))
        scratch.update(pair("gsmall"))
        for name, like in results.items():
            if name in ("gws", "gwe"):
                scratch[name] = vm(lead[:2] + like.shape, F32)
            elif name != "gpost":
                scratch[name] = vm((like.shape[0] * dp_count * fsdp_count, like.shape[1]), F32)
            scratch[name + "_core"] = vm(lead[:2] + like.shape, BF)
            scratch[name + "_dp"] = vm((3,) + lead[1:2] + like.shape, BF)
            scratch[name + "_z"] = vm((lead[1] - 1,) + like.shape, BF)
            scratch.update(pair(name))
        for tail in ("", "_dp", "_z"):
            scratch["gsmall" + tail] = vm((16, width), F32)
        scratch["gsmall_in"] = vm((hops, 16, width), F32)
        got = call(
            functools.partial(whole_kernel, counts), "layer", ins, outs, scratch,
            collective_id=0, has_side_effects=True,
        )
        ins = {}
        for name in ("out", "gin"):
            ins[name + "_in"] = (got[name], hbm)
        for name in GRADS + ("gpost", "gsmall"):
            ins[name + "_in"] = (got[name + "_result"], vm)
        outs = dict(out=(act, hbm), gin=(act, hbm))
        for name, like in dict(gwq=wq, gwk=wk, gwv=wv, gwm=wm, gwe=we, gws=ws).items():
            outs[name] = (shape_of(like.shape, F32), vm)
        outs["gpost"] = (shape_of((rows, seq), F32), vm)
        for i in range(8):
            outs["gvec" + str(i)] = (shape_of((1, rows), F32), vm)
        outs["geb"] = (shape_of((1, ff_rows), F32), vm)
        got = call(
            functools.partial(unpack_kernel, counts), "unpack", ins, outs,
            dict(held=vm((2,) + act.shape, BF), sem=pltpu.SemaphoreType.DMA((2, 2, count))),
        )
        gvec = [got["gvec" + str(i)].reshape(rows) for i in range(8)]
        geb, gpos = got["geb"].reshape(ff_rows), got["gpost"].T
        grads = got
    else:
        lead = (4, 4, 2)
        cut = lambda a: a.reshape(lead + (-1, a.shape[-1]))
        gather = lambda a, axis=0: lax.all_gather(a, AXES, axis=axis, tiled=True)
        share = lambda a, axis=0: lax.psum_scatter(a, AXES, scatter_dimension=axis, tiled=True)
        ins = dict(data)
        for name, shard in dict(wq=wq, wk=wk, wv=wv, wm=wm, we=we, ws=ws).items():
            ins[name] = (cut(gather(shard)), vm)
        ins["pos"] = (gather(pos, 1), vm)
        ins["vec"] = (jnp.stack([gather(a).astype(F32) for a in vectors]), vm)
        ins["eb"] = (gather(eb).astype(F32)[None], vm)
        outs = dict(out=(act, hbm), gin=(act, hbm), kept=(kept, hbm))
        for name, shape in dict(gws=(ff, width), gwe=(width, ff), gwm=(width, width)).items():
            outs[name] = (shape_of(shape, F32), vm)
        for group in range(GROUPS):
            outs["gqkv" + str(group)] = (shape_of((width, 3 * width // GROUPS), F32), vm)
        outs["gpos_out"] = (shape_of((seq, width), F32), vm)
        outs["gvec"] = (shape_of((8, width), F32), vm)
        outs["geb"] = (shape_of((1, ff), F32), vm)
        got = call(alone_kernel, "layer_alone", ins, outs, scratch)
        size = width // GROUPS
        for at, name in enumerate(("gwq", "gwk", "gwv")):
            parts = [got["gqkv" + str(g)][:, at * size : (at + 1) * size] for g in range(GROUPS)]
            got[name] = jnp.concatenate(parts, axis=1)
        grads = {name: share(got[name]) for name in ("gwq", "gwk", "gwv", "gwm", "gwe", "gws")}
        gpos = share(got["gpos_out"], 1)
        gvec = [share(got["gvec"][i]) for i in range(8)]
        geb = share(got["geb"][0])
    gbq, gbv, gbm, gbs, gg1, gs1, gg2, gs2 = (gvec[i] for i in range(8))
    return (
        got["out"].reshape(inputs.shape), got["gin"].reshape(inputs.shape),
        grads["gwq"], grads["gwk"], grads["gwv"], grads["gwm"], grads["gwe"], grads["gws"], gpos,
        gbq, gbv, gbm, geb, gbs, gg1, gs1, gg2, gs2,
    )


def solution(mesh):
    batch = P(None, AXES, None, None)
    matrix, vector, table = P(AXES, None), P(AXES), P(None, AXES)
    weights = (matrix,) * 6 + (table,) + (vector,) * 9
    return jax.shard_map(
        functools.partial(local, mesh.shape["dp"], mesh.shape["fsdp"]),
        mesh=mesh,
        in_specs=(batch, P(None, AXES), batch) + weights,
        out_specs=(batch, batch) + weights,
        check_vma=False,
    )
```
